32 devices in a mesh: section: 2 (over x), dp: 8 (over z, y), mp: 2 (over core).
Axes of the slice: x: 2, y: 2, z: 4, core: 2. Of those that a mesh axis runs over, the one named last changes fastest.
Arguments:
- inputs: bfloat16 [2, 2048, 1024], P(None, ('dp', 'mp')), may hold values from -6 to 6
- target_inputs: bfloat16 [2, 2048, 1024], P(None, ('dp', 'mp')), may hold values from -6 to 6
- cotangent: bfloat16 [2, 2048, 1024], P(None, ('dp', 'mp')), may hold values from -6 to 6
- slot_counts: int32 [2, 2], replicated, may hold values from 2 to 4
- w_qkv: bfloat16 [2, 3, 1024, 1024], P('section', None, None, 'mp'), may hold values from -0.1875 to 0.1875
- w_out: bfloat16 [2, 1024, 1024], P('section', None, 'mp'), may hold values from -0.75 to 0.75
- norm1_gain: float32 [2, 1024], P('section'), may hold values from 0.5 to 1.5
- norm1_bias: float32 [2, 1024], P('section'), may hold values from -1.2 to 1.2
- w_up: bfloat16 [2, 1024, 4096], P('section', None, 'mp'), may hold values from -0.1875 to 0.1875
- w_down: bfloat16 [2, 1024, 4096], P('section', None, 'mp'), may hold values from -0.125 to 0.125
- norm2_gain: float32 [2, 1024], P('section'), may hold values from 0.5 to 1.5
- norm2_bias: float32 [2, 1024], P('section'), may hold values from -1.2 to 1.2
- cross_qkv: bfloat16 [3, 1024, 1024], P(None, None, 'mp'), may hold values from -0.1875 to 0.1875
- cross_out: bfloat16 [1024, 1024], P(None, 'mp'), may hold values from -0.75 to 0.75
- norm3_gain: float32 [1024], replicated, may hold values from 0.5 to 1.5
- norm3_bias: float32 [1024], replicated, may hold values from -1.2 to 1.2
Outputs:
- segment_outputs: bfloat16 [2, 2, 2048, 1024], P('section', None, ('dp', 'mp'))
- input_grads: bfloat16 [2, 2, 2048, 1024], P('section', None, ('dp', 'mp'))
- grad_qkv: float32 [2, 3, 1024, 1024], P('section', None, 'dp', 'mp')
- grad_out: float32 [2, 1024, 1024], P('section', 'dp', 'mp')
- grad_norm1_gain: float32 [2, 1024], P('section', 'dp')
- grad_norm1_bias: float32 [2, 1024], P('section', 'dp')
- grad_up: float32 [2, 1024, 4096], P('section', 'dp', 'mp')
- grad_down: float32 [2, 1024, 4096], P('section', 'dp', 'mp')
- grad_norm2_gain: float32 [2, 1024], P('section', 'dp')
- grad_norm2_bias: float32 [2, 1024], P('section', 'dp')
- grad_cross_qkv: float32 [3, 1024, 1024], P(None, ('section', 'dp'), 'mp')
- grad_cross_out: float32 [1024, 1024], P(('section', 'dp'), 'mp')
- grad_norm3_gain: float32 [1024], P(('section', 'dp'))
- grad_norm3_bias: float32 [1024], P(('section', 'dp'))
The draws below stay inside these ranges and needn't reach their ends.
All inputs are finite; a program needn't handle non-finite values.
Results may differ from the reference program's by a relative error of at most 0.029.
Values may be sent and summed in bfloat16 or wider, within the bound.
A program may use at most 256 MiB of HBM per device.

```python
from functools import partial
import jax
import jax.numpy as jnp
from jax import lax

D = 1024
HEADS = 16
HEAD = 64
FF = 4096
SLOT = 256
QSLOTS = 4
MICRO = 2
TOKENS = 2048
QUESTIONS = 2
SECTIONS = 2


def set_ends(array, rng, least, top_value):
    longest = array.shape.index(max(array.shape))
    spots = []
    for shift in (0, 1):
        where = [jax.random.randint(jax.random.fold_in(rng, axis), (), 0, length) for axis, length in enumerate(array.shape)]
        where[longest] = (where[longest] + shift) % array.shape[longest]
        spots.append(tuple(where))
    return array.at[spots[0]].set(least).at[spots[1]].set(top_value)


def raised(entries, stream_key, source, target, parts, factor):
    owner, partner = [(jnp.arange(entries.shape[axis_at]) // (entries.shape[axis_at] // parts)).reshape([-1 if axis == axis_at else 1 for axis in range(entries.ndim)]) for axis_at in (source, target)]
    chosen = jax.random.permutation(stream_key, parts)[partner]
    strong = (owner == chosen) | (owner == (partner + parts // 2) % parts)
    return jnp.where(strong, factor * entries, entries)


def block_scale(own_key, extent, shards, low, top_value):
    def one(dim, parts):
        heights = jax.random.uniform(jax.random.fold_in(jax.random.fold_in(own_key, 6), dim), (parts,), jnp.float32, low / len(shards), top_value / len(shards))
        return jnp.repeat(jnp.exp(heights), extent[dim] // parts).reshape((-1,) + (1,) * (len(extent) - dim - 1))

    level = one(*shards[0])
    for cut in shards[1:]:
        level = level * one(*cut)
    return level


def bell_draw(key, dims, scale, limit, pieces=(), kind=jnp.bfloat16):
    factor_of = block_scale(key, dims, pieces, -0.22, 0.18) if pieces else 1.0
    entries = jax.random.normal(key, dims, jnp.float32) * scale * factor_of
    return jnp.minimum(jnp.maximum(entries, -limit), limit).astype(kind)


def noise_with(own_key, shape, scale, reach, shards, heavy, held_as=jnp.bfloat16):
    array = scale * jax.random.normal(own_key, shape, jnp.float32)
    if shards:
        array = array * block_scale(own_key, shape, shards, -0.22, 0.18)
    return jnp.clip(raised(array, jax.random.fold_in(own_key, 3), *heavy), -reach, reach).astype(held_as)


def setup_inputs(seed: int = 0) -> dict:
    key_of = jax.random.split(jax.random.key(seed), 17)
    return {
        "inputs": bell_draw(key_of[0], (MICRO, TOKENS, D), 1.0, 6.0, ((1, 16),)),
        "target_inputs": bell_draw(key_of[1], (MICRO, TOKENS, D), 1.0, 6.0, ((1, 16),)),
        "cotangent": noise_with(key_of[2], (MICRO, TOKENS, D), 1.0, 6.0, ((1, 16),), (1, 2, 16, 2.0)),
        "slot_counts": set_ends(jax.random.randint(key_of[3], (MICRO, QUESTIONS), 2, QSLOTS + 1), jax.random.fold_in(key_of[3], 1), 2, QSLOTS).astype(jnp.int32),
        "w_qkv": bell_draw(key_of[4], (SECTIONS, 3, D, D), D ** -0.5, 0.1875, ((0, 2), (3, 2))),
        "w_out": bell_draw(key_of[5], (SECTIONS, D, D), (D // 16) ** -0.5, 0.75, ((0, 2), (2, 2))),
        "norm1_gain": jnp.clip(1.0 + 0.1 * jax.random.normal(key_of[6], (SECTIONS, D), jnp.float32), 0.5, 1.5),
        "norm1_bias": bell_draw(key_of[7], (SECTIONS, D), 0.2, 1.2, ((0, 2),), jnp.float32),
        "w_up": bell_draw(key_of[8], (SECTIONS, D, FF), D ** -0.5, 0.1875, ((0, 2), (2, 2))),
        "w_down": bell_draw(key_of[9], (SECTIONS, D, FF), (FF // 2) ** -0.5, 0.125, ((0, 2), (2, 2))),
        "norm2_gain": jnp.clip(1.0 + 0.1 * jax.random.normal(key_of[10], (SECTIONS, D), jnp.float32), 0.5, 1.5),
        "norm2_bias": bell_draw(key_of[11], (SECTIONS, D), 0.2, 1.2, ((0, 2),), jnp.float32),
        "cross_qkv": bell_draw(key_of[12], (3, D, D), D ** -0.5, 0.1875, ((2, 2),)),
        "cross_out": bell_draw(key_of[13], (D, D), (D // 16) ** -0.5, 0.75, ((1, 2),)),
        "norm3_gain": jnp.clip(1.0 + 0.1 * jax.random.normal(key_of[14], (D,), jnp.float32), 0.5, 1.5),
        "norm3_bias": bell_draw(key_of[15], (D,), 0.2, 1.2, (), jnp.float32),
    }


@jax.custom_vjp
def low(v):
    return lax.optimization_barrier(v.astype(jnp.bfloat16)).astype(jnp.float32)

@jax.custom_vjp
def low_back(v):
    return v

def low_keep(v):
    return (low(v), None)

def low_pass(kept, grad):
    return (grad,)

def back_keep(v):
    return (v, None)

def back_low(kept, grad):
    return (low(grad),)
low.defvjp(low_keep, low_pass)
low_back.defvjp(back_keep, back_low)
HIGH = lax.Precision.HIGHEST

def layer_norm(values, gain, bias_term):
    center = values - lax.optimization_barrier(jnp.mean(values, -1, keepdims=True))
    spread = lax.optimization_barrier(jnp.mean(center * center, -1, keepdims=True))
    return center * lax.rsqrt(spread + 1e-05) * gain + bias_term

def attend(queries, keys, values, causal):
    count = queries.shape[0] // SLOT
    shaped_q = queries.reshape(count, SLOT, HEADS, HEAD)
    shaped_k = keys.reshape(count, SLOT, HEADS, HEAD)
    shaped_v = values.reshape(count, SLOT, HEADS, HEAD)
    scores = low_back(jnp.einsum('bqhd,bkhd->bhqk', shaped_q, shaped_k, precision=HIGH) * HEAD ** (-0.5))
    if causal:
        places = jnp.arange(SLOT, dtype=jnp.int32)
        allowed = places[:, None] >= places[None, :]
        scores = jnp.where(allowed, scores, -1000000000.0)
    peak = lax.optimization_barrier(jnp.max(scores, -1, keepdims=True))
    expo = jnp.exp(scores - peak)
    weights = low(expo / lax.optimization_barrier(jnp.sum(expo, -1, keepdims=True)))
    mixed = jnp.einsum('bhqk,bkhd->bqhd', weights, shaped_v, precision=HIGH)
    return low(low_back(mixed.reshape(queries.shape[0], D)))

def sublayers(layer_in, memory, own, cross):
    wqkv, wout, gain_one, bias_one, wup, wdown, gain_two, bias_two = own
    cross_weights, cross_proj, gain_three, bias_three = cross
    projected = low(low_back(jnp.einsum('nd,tdc->tnc', layer_in, wqkv, precision=HIGH)))
    causal = memory is not None
    mixed = jax.checkpoint(partial(attend, causal=causal))(projected[0], projected[1], projected[2])
    branch = low_back(jnp.dot(mixed, wout.T, precision=HIGH))
    normed = layer_norm(layer_in + branch, gain_one, bias_one)
    crossed = normed
    if memory is not None:
        query = low(low_back(jnp.dot(low(normed), cross_weights[0], precision=HIGH)))
        keyval = low(low_back(jnp.einsum('nd,tdc->tnc', memory, cross_weights[1:], precision=HIGH)))
        cross_mixed = jax.checkpoint(partial(attend, causal=False))(query, keyval[0], keyval[1])
        cross_branch = low_back(jnp.dot(cross_mixed, cross_proj.T, precision=HIGH))
        crossed = layer_norm(normed + cross_branch, gain_three, bias_three)
    hidden_pre = low_back(jnp.dot(low(crossed), wup, precision=HIGH))
    activated = low(jax.nn.gelu(hidden_pre, approximate=False))
    second = low_back(jnp.dot(activated, wdown.T, precision=HIGH))
    return layer_norm(crossed + second, gain_two, bias_two)

def reference(inputs, target_inputs, cotangent, slot_counts, w_qkv, w_out, norm1_gain, norm1_bias, w_up, w_down, norm2_gain, norm2_bias, cross_qkv, cross_out, norm3_gain, norm3_bias):
    weights = (w_qkv.astype(jnp.float32), w_out.astype(jnp.float32), norm1_gain, norm1_bias, w_up.astype(jnp.float32), w_down.astype(jnp.float32), norm2_gain, norm2_bias)
    cross = (cross_qkv.astype(jnp.float32), cross_out.astype(jnp.float32), norm3_gain, norm3_bias)
    rows = jnp.arange(TOKENS, dtype=jnp.int32)
    slot_ids = rows // SLOT
    question = slot_ids // QSLOTS
    place = slot_ids % QSLOTS
    valid = (place[None, :] < slot_counts[:, question]).astype(jnp.float32)

    def model(source, target, params, cross_params):
        memories = []
        finals = []
        for micro_index in range(MICRO):
            own_enc = [p[0] for p in params]
            own_dec = [p[1] for p in params]
            enc_in = low(low_back(source[micro_index]))
            memory = sublayers(enc_in, None, own_enc, cross_params)
            dec_in = low(low_back(target[micro_index]))
            final = sublayers(dec_in, low(low_back(memory)), own_dec, cross_params)
            memories.append(memory)
            finals.append(final)
        stacked = jnp.stack(finals)
        return (stacked, jnp.stack([jnp.stack(memories), stacked]))
    source = inputs.astype(jnp.float32)
    target = target_inputs.astype(jnp.float32)
    finals, back_fn, outputs = jax.vjp(model, source, target, weights, cross, has_aux=True)
    masked_grad = cotangent.astype(jnp.float32) * valid[:, :, None]
    grad_source, grad_target, grad_weights, grad_cross = back_fn(masked_grad)
    input_grads = jnp.stack([grad_source, grad_target]).astype(jnp.bfloat16)
    return (outputs.astype(jnp.bfloat16), input_grads, grad_weights[0], grad_weights[1], grad_weights[2], grad_weights[3], grad_weights[4], grad_weights[5], grad_weights[6], grad_weights[7], grad_cross[0], grad_cross[1], grad_cross[2], grad_cross[3])
```

```python
import functools

import jax
import jax.numpy as jnp
from jax import lax
from jax.experimental import pallas as pl
from jax.experimental.pallas import tpu as pltpu
from jax.sharding import PartitionSpec as P

HEAD = 64
SLOT = 256
QSLOTS = 4
CHUNK = 512
PAIR = 2 * HEAD
STRIP = 64
EPS = 1e-5
NEG = -1000000000.0
MESH = pl.DeviceIdType.MESH
BF = jnp.bfloat16
F32 = jnp.float32
VM = pltpu.VMEM


def dot_nn(a, b):
    return lax.dot_general(a, b, (((1,), (0,)), ((), ())), preferred_element_type=F32)


def dot_nt(a, b):
    return lax.dot_general(a, b, (((1,), (1,)), ((), ())), preferred_element_type=F32)


def dot_tn(a, b):
    return lax.dot_general(a, b, (((0,), (0,)), ((), ())), preferred_element_type=F32)


def loop(count, body):
    def step(i, carry):
        body(i)
        return carry

    lax.fori_loop(0, count, step, 0)


def head_masks():
    lane = lax.broadcasted_iota(jnp.int32, (1, PAIR), 1)
    first = jnp.where(lane < HEAD, 1.0, 0.0).astype(BF)
    second = jnp.where(lane < HEAD, 0.0, 1.0).astype(BF)
    return first, second


def probs_of(query, keys, mask, limit):
    scores = dot_nt(query * (mask * (HEAD**-0.5)).astype(BF), keys)
    if limit is not None:
        row = lax.broadcasted_iota(jnp.int32, scores.shape, 0)
        col = lax.broadcasted_iota(jnp.int32, scores.shape, 1)
        scores = jnp.where(row + limit >= col, scores, NEG)
    expo = jnp.exp(scores - jnp.max(scores, -1, keepdims=True))
    return expo / jnp.sum(expo, -1, keepdims=True)


def attend_forward(proj, mixed, rows, lanes, limit):
    query, keys, values = proj[0, rows, lanes], proj[1, rows, lanes], proj[2, rows, lanes]
    masks = head_masks()
    low = [probs_of(query, keys, mask, limit).astype(BF) for mask in masks]
    mixed[rows, lanes] = dot_nn(
        jnp.concatenate(low, 1), jnp.concatenate([values * mask for mask in masks], 0)
    ).astype(BF)


def attend_backward(proj, d_mixed, d_proj, rows, lanes, limit):
    query, keys, values = proj[0, rows, lanes], proj[1, rows, lanes], proj[2, rows, lanes]
    grad = d_mixed[rows, lanes]
    masks = head_masks()
    low, d_scores = [], []
    for mask in masks:
        weights = probs_of(query, keys, mask, limit)
        d_weights = dot_nt(grad * mask, values)
        inner = jnp.sum(weights * d_weights, -1, keepdims=True)
        d_scores.append((weights * (d_weights - inner)).astype(BF))
        low.append(weights.astype(BF))
    scale = HEAD**-0.5
    d_proj[2, rows, lanes] = dot_tn(
        jnp.concatenate(low, 0), jnp.concatenate([grad * mask for mask in masks], 0)
    ).astype(BF)
    d_proj[0, rows, lanes] = (
        dot_nn(jnp.concatenate(d_scores, 1), jnp.concatenate([keys * mask for mask in masks], 0))
        * scale
    ).astype(BF)
    d_proj[1, rows, lanes] = (
        dot_tn(jnp.concatenate(d_scores, 0), jnp.concatenate([query * mask for mask in masks], 0))
        * scale
    ).astype(BF)


def norm_forward(value, gain, bias):
    center = value - jnp.mean(value, -1, keepdims=True)
    scale = lax.rsqrt(jnp.mean(center * center, -1, keepdims=True) + EPS)
    unit = center * scale
    return unit, scale, unit * gain + bias


def norm_backward(grad, unit, scale, gain, sums, which):
    fold = lambda v: jnp.sum(v.reshape(v.shape[0] // 8, 8, v.shape[1]), 0)
    sums[which] += fold(grad * unit)
    sums[which + 1] += fold(grad)
    d_unit = grad * gain
    first = jnp.mean(d_unit, -1, keepdims=True)
    second = jnp.mean(d_unit * unit, -1, keepdims=True)
    return scale * (d_unit - first - unit * second)


def layer_kernel(
    sections,
    inputs,
    targets,
    cotangent,
    counts,
    qkv_hbm,
    out_hbm,
    gain1,
    bias1,
    up_hbm,
    down_hbm,
    gain2,
    bias2,
    cross_hbm,
    cross_out_hbm,
    gain3,
    bias3,
    seg_out,
    in_grad,
    norm_out,
    a_out,
    b_out,
    w_qkv,
    w_out,
    w_up,
    w_down,
    w_cross,
    w_cross_out,
    a_fac,
    b_fac,
    proj,
    cross_proj,
    unit1,
    unit2,
    unit3,
    scale1,
    scale2,
    scale3,
    resid,
    slope,
    d_out,
    d_mix,
    sent,
    got,
    half_send,
    half_own,
    half_got,
    sums,
    load_sem,
    x_sem,
    ex_send,
    ex_recv,
    hop_send,
    hop_recv,
    out_sem,
):
    section = lax.axis_index("section")
    dp = lax.axis_index("dp")
    core = lax.axis_index("mp")
    decoder = section == sections - 1
    encoder = section != sections - 1
    mate = (section, dp, 1 - core)
    across = (1 - section, dp, core)
    half = seg_out.shape[2]
    slot = 2 * half
    limit = jnp.where(decoder, 0, slot)
    width = w_up.shape[1]
    parts = width // CHUNK
    own = core * half
    other = (1 - core) * half

    d_branch, crossed, d_attn, layer_in, normed_low, memory, d_cross = (a_fac.at[i] for i in range(7))
    act = b_fac.at[0:parts]
    d_hidden = b_fac.at[parts : 2 * parts]
    mixed = b_fac.at[2 * parts]
    d_proj = b_fac.at[2 * parts + 1 : 2 * parts + 4]
    d_cross_proj = b_fac.at[2 * parts + 4 : 2 * parts + 7]
    cross_mixed = b_fac.at[2 * parts + 7]

    def rows_of(m):
        return pl.ds(pl.multiple_of(m * slot, slot), slot)

    def half_of(m, offset):
        return pl.ds(pl.multiple_of(m * slot + offset, half), half)

    def strip_of(m, k):
        return pl.ds(pl.multiple_of(m * slot + k * STRIP, STRIP), STRIP)

    def lanes_of(j):
        return pl.ds(pl.multiple_of(j * PAIR, PAIR), PAIR)

    barrier = pltpu.get_barrier_semaphore()
    for device in (mate, across):
        pl.semaphore_signal(barrier, inc=1, device_id=device, device_id_type=MESH)

    loads = [
        pltpu.make_async_copy(src, dst, load_sem.at[i])
        for i, (src, dst) in enumerate(
            (
                (qkv_hbm.at[0], w_qkv),
                (out_hbm.at[0], w_out),
                (up_hbm.at[0], w_up),
                (down_hbm.at[0], w_down),
                (cross_hbm, w_cross),
                (cross_out_hbm, w_cross_out),
            )
        )
    ]

    def local_rows(src, dst, m, sem):
        return pltpu.make_async_copy(src.at[m], dst.at[half_of(m, own)], sem)

    def mate_rows(src, dst, m, send, recv):
        return pltpu.make_async_remote_copy(
            src_ref=src.at[m],
            dst_ref=dst.at[half_of(m, own)],
            send_sem=send,
            recv_sem=recv,
            device_id=mate,
            device_id_type=MESH,
        )

    def start_rows(src, dst, base):
        for m in range(2):
            local_rows(src, dst, m, x_sem.at[base + m]).start()
        for m in range(2):
            mate_rows(src, dst, m, x_sem.at[base + 2 + m], x_sem.at[base + 4 + m]).start()

    def wait_rows(src, dst, base, m):
        local_rows(src, dst, m, x_sem.at[base + m]).wait()
        mate_rows(src, dst, m, x_sem.at[base + 2 + m], x_sem.at[base + 4 + m]).wait()

    @pl.when(encoder)
    def _():
        for m in range(2):
            local_rows(inputs, layer_in, m, x_sem.at[m]).start()

    @pl.when(decoder)
    def _():
        for m in range(2):
            local_rows(targets, layer_in, m, x_sem.at[m]).start()

    loads[0].start()
    loads[1].start()
    pl.semaphore_wait(barrier, 2)

    def mate_start(src, dst, base):
        for m in range(2):
            mate_rows(src, dst, m, x_sem.at[base + 2 + m], x_sem.at[base + 4 + m]).start()

    @pl.when(encoder)
    def _():
        mate_start(inputs, layer_in, 0)

    @pl.when(decoder)
    def _():
        mate_start(targets, layer_in, 0)

    for copy in loads[2:]:
        copy.start()

    @pl.when(decoder)
    def _():
        start_rows(cotangent, d_out, 6)

    sums[...] = jnp.zeros_like(sums)

    def exchange(which, buffer, m):
        return pltpu.make_async_remote_copy(
            src_ref=sent.at[rows_of(m)],
            dst_ref=got.at[buffer, rows_of(m)],
            send_sem=ex_send.at[which, m],
            recv_sem=ex_recv.at[which, m],
            device_id=mate,
            device_id_type=MESH,
        )

    def half_exchange(which, m):
        return pltpu.make_async_remote_copy(
            src_ref=half_send.at[which, m],
            dst_ref=half_got.at[which, m],
            send_sem=hop_send.at[4 + which, m],
            recv_sem=hop_recv.at[4 + which, m],
            device_id=mate,
            device_id_type=MESH,
        )

    def across_copy(src, dst, which, m):
        return pltpu.make_async_remote_copy(
            src_ref=src,
            dst_ref=dst.at[half_of(m, own)],
            send_sem=hop_send.at[which, m],
            recv_sem=hop_recv.at[which, m],
            device_id=across,
            device_id_type=MESH,
        )

    def forward_copy(ref, which, m):
        return pltpu.make_async_remote_copy(
            src_ref=ref.at[half_of(m, own)],
            dst_ref=ref.at[half_of(m, own)],
            send_sem=hop_send.at[which, m],
            recv_sem=hop_recv.at[which, m],
            device_id=mate,
            device_id_type=MESH,
        )

    def project_out(value, weight, m):
        for n in range(sent.shape[1] // CHUNK):
            cols = slice(n * CHUNK, (n + 1) * CHUNK)
            sent[rows_of(m), cols] = dot_nt(value, weight[cols, :]).astype(BF)

    def summed(buffer, strip):
        return sent[strip].astype(F32) + got[buffer, strip].astype(F32)

    loads[0].wait()

    def attention_in(m):
        @pl.when(encoder)
        def _():
            wait_rows(inputs, layer_in, 0, m)

        @pl.when(decoder)
        def _():
            wait_rows(targets, layer_in, 0, m)

        rows = rows_of(m)
        for t in range(3):
            proj[t, rows] = dot_nn(layer_in[rows], w_qkv[t]).astype(BF)
        loop(CHUNK // PAIR, lambda j: attend_forward(proj, mixed, rows, lanes_of(j), limit))
        project_out(mixed[rows], w_out, m)
        exchange(0, 0, m).start()

    loads[1].wait()
    loop(2, attention_in)
    for copy in loads[2:]:
        copy.wait()

    def after_attention(m):
        exchange(0, 0, m).wait()

        def norm(k):
            strip = strip_of(m, k)
            unit, scale, value = norm_forward(
                layer_in[strip].astype(F32) + summed(0, strip), gain1[...], bias1[...]
            )
            unit1[strip] = unit.astype(BF)
            scale1[strip] = scale
            resid[strip] = value
            normed_low[strip] = value.astype(BF)
            crossed[strip] = value.astype(BF)

        loop(slot // STRIP, norm)

        @pl.when(decoder)
        def _():
            rows = rows_of(m)
            cross_proj[0, rows] = dot_nn(normed_low[rows], w_cross[0]).astype(BF)
            across_copy(seg_out.at[0, m], memory, 0, m).wait_recv()
            forward_copy(memory, 1, m).start()
            forward_copy(memory, 1, m).wait()
            for t in range(1, 3):
                cross_proj[t, rows] = dot_nn(memory[rows], w_cross[t]).astype(BF)
            loop(
                CHUNK // PAIR,
                lambda j: attend_forward(cross_proj, cross_mixed, rows, lanes_of(j), None),
            )
            project_out(cross_mixed[rows], w_cross_out, m)
            exchange(1, 1, m).start()

    loop(2, after_attention)

    def feed_forward(m):
        rows = rows_of(m)

        @pl.when(decoder)
        def _():
            exchange(1, 1, m).wait()

            def norm(k):
                strip = strip_of(m, k)
                unit, scale, value = norm_forward(
                    resid[strip] + summed(1, strip), gain3[...], bias3[...]
                )
                unit3[strip] = unit.astype(BF)
                scale3[strip] = scale
                resid[strip] = value
                crossed[strip] = value.astype(BF)

            loop(slot // STRIP, norm)

        for n in range(parts):
            pre = dot_nn(crossed[rows], w_up[:, n * CHUNK : (n + 1) * CHUNK])
            rise = 0.5 + 0.5 * lax.erf(pre * (0.5**0.5))
            act[n, rows] = (pre * rise).astype(BF)
            slope[n, rows] = (rise + pre * jnp.exp(-0.5 * pre * pre) * 0.3989422804014327).astype(BF)
        project_out(jnp.concatenate([act[n, rows] for n in range(parts)], 1), w_down, m)
        exchange(2, 2, m).start()

    loop(2, feed_forward)

    def finish_forward(m):
        exchange(2, 2, m).wait()

        def norm(k):
            strip = strip_of(m, k)
            unit, scale, value = norm_forward(
                resid[strip] + summed(2, strip), gain2[...], bias2[...]
            )
            unit2[strip] = unit.astype(BF)
            scale2[strip] = scale
            place = k * STRIP - own

            @pl.when((place >= 0) & (place < half))
            def _():
                seg_out[0, m, pl.ds(pl.multiple_of(lax.rem(k * STRIP, half), STRIP), STRIP)] = (
                    value.astype(BF)
                )

        loop(slot // STRIP, norm)

        @pl.when(encoder)
        def _():
            across_copy(seg_out.at[0, m], memory, 0, m).start()

    loop(2, finish_forward)

    question = dp // QSLOTS
    spot = dp - question * QSLOTS

    def feed_backward(m):
        rows = rows_of(m)

        @pl.when(encoder)
        def _():
            across_copy(half_send.at[0, m], d_out, 2, m).wait_recv()
            forward_copy(d_out, 3, m).start()
            forward_copy(d_out, 3, m).wait()

        @pl.when(decoder)
        def _():
            wait_rows(cotangent, d_out, 6, m)

        keep = jnp.where(spot < counts[m, question], 1.0, 0.0)
        keep = jnp.where(decoder, keep, 1.0)

        def norm(k):
            strip = strip_of(m, k)
            grad = norm_backward(
                d_out[strip].astype(F32) * keep,
                unit2[strip].astype(F32),
                scale2[strip],
                gain2[...],
                sums,
                2,
            )
            resid[strip] = grad
            d_branch[strip] = grad.astype(BF)

        loop(slot // STRIP, norm)
        for n in range(parts):
            grad = dot_nn(d_branch[rows], w_down[:, n * CHUNK : (n + 1) * CHUNK])
            d_hidden[n, rows] = (grad * slope[n, rows].astype(F32)).astype(BF)
        project_out(jnp.concatenate([d_hidden[n, rows] for n in range(parts)], 1), w_up, m)
        exchange(3, 0, m).start()

    loop(2, feed_backward)

    def cross_backward(m):
        rows = rows_of(m)

        def norm(k):
            strip = strip_of(m, k)
            grad = norm_backward(
                resid[strip] + summed(0, strip),
                unit3[strip].astype(F32),
                scale3[strip],
                gain3[...],
                sums,
                4,
            )
            resid[strip] = grad
            d_cross[strip] = grad.astype(BF)

        loop(slot // STRIP, norm)
        d_mix[rows] = dot_nn(d_cross[rows], w_cross_out[...]).astype(BF)
        loop(
            CHUNK // PAIR,
            lambda j: attend_backward(cross_proj, d_mix, d_cross_proj, rows, lanes_of(j), None),
        )

        def memory_part(offset):
            piece = half_of(m, offset)
            return jnp.concatenate([d_cross_proj[1, piece], d_cross_proj[2, piece]], 1)

        def memory_weight(n):
            cols = slice(n * CHUNK, (n + 1) * CHUNK)
            return jnp.concatenate([w_cross[1, cols], w_cross[2, cols]], 1)

        for n in range(sent.shape[1] // CHUNK):
            cols = slice(n * CHUNK, (n + 1) * CHUNK)
            half_send[0, m, :, cols] = dot_nt(memory_part(other), memory_weight(n)).astype(BF)
        half_exchange(0, m).start()
        for n in range(sent.shape[1] // CHUNK):
            cols = slice(n * CHUNK, (n + 1) * CHUNK)
            half_own[m, :, cols] = dot_nt(memory_part(own), memory_weight(n))
        project_out(d_cross_proj[0, rows], w_cross[0], m)
        exchange(4, 1, m).start()
        half_exchange(0, m).wait()
        half_send[0, m] = (half_own[m] + half_got[0, m].astype(F32)).astype(BF)
        across_copy(half_send.at[0, m], d_out, 2, m).start()

    def attention_back(m):
        rows = rows_of(m)

        def norm_rows(buffer):
            def norm(k):
                strip = strip_of(m, k)
                grad = norm_backward(
                    resid[strip] + summed(buffer, strip),
                    unit1[strip].astype(F32),
                    scale1[strip],
                    gain1[...],
                    sums,
                    0,
                )
                resid[strip] = grad
                d_attn[strip] = grad.astype(BF)

            loop(slot // STRIP, norm)

        @pl.when(decoder)
        def _():
            exchange(4, 1, m).wait()

        @pl.when(encoder)
        def _():
            exchange(3, 0, m).wait()

        norm_rows(jnp.where(decoder, 1, 0))
        d_mix[rows] = dot_nn(d_attn[rows], w_out[...]).astype(BF)
        loop(
            CHUNK // PAIR, lambda j: attend_backward(proj, d_mix, d_proj, rows, lanes_of(j), limit)
        )

        def input_part(offset):
            piece = half_of(m, offset)
            return jnp.concatenate([d_proj[t, piece] for t in range(3)], 1)

        def input_weight(n):
            cols = slice(n * CHUNK, (n + 1) * CHUNK)
            return jnp.concatenate([w_qkv[t, cols] for t in range(3)], 1)

        for n in range(sent.shape[1] // CHUNK):
            cols = slice(n * CHUNK, (n + 1) * CHUNK)
            half_send[1, m, :, cols] = dot_nt(input_part(other), input_weight(n)).astype(BF)
        half_exchange(1, m).start()
        for n in range(sent.shape[1] // CHUNK):
            cols = slice(n * CHUNK, (n + 1) * CHUNK)
            half_own[m, :, cols] = dot_nt(input_part(own), input_weight(n))

    @pl.when(decoder)
    def _():
        def both(m):
            exchange(3, 0, m).wait()
            cross_backward(m)

        loop(2, both)

    loop(2, attention_back)

    def finish_backward(m):
        half_exchange(1, m).wait()
        in_grad[0, m] = (
            resid[half_of(m, own)] + half_own[m] + half_got[1, m].astype(F32)
        ).astype(BF)

    loop(2, finish_backward)

    @pl.when(encoder)
    def _():
        for m in range(2):
            across_copy(seg_out.at[0, m], memory, 0, m).wait_send()

    @pl.when(decoder)
    def _():
        for m in range(2):
            across_copy(half_send.at[0, m], d_out, 2, m).wait_send()

    for i in range(6):
        norm_out[i : i + 1] = jnp.sum(sums[i], 0, keepdims=True)
    norm_out[6:8] = jnp.zeros_like(norm_out[6:8])
    copies = [
        pltpu.make_async_copy(a_fac, a_out, out_sem.at[0]),
        pltpu.make_async_copy(b_fac, b_out, out_sem.at[1]),
    ]
    for copy in copies:
        copy.start()
    for copy in copies:
        copy.wait()


def body(
    sections,
    inputs,
    target_inputs,
    cotangent,
    slot_counts,
    w_qkv,
    w_out,
    norm1_gain,
    norm1_bias,
    w_up,
    w_down,
    norm2_gain,
    norm2_bias,
    cross_qkv,
    cross_out,
    norm3_gain,
    norm3_bias,
):
    micro, half, depth = inputs.shape
    rows = micro * 2 * half
    heads = w_out.shape[2]
    width = w_up.shape[2]
    parts = width // CHUNK
    chunks = 2 * parts + 8
    hbm = pl.BlockSpec(memory_space=pl.ANY)
    vmem = pl.BlockSpec(memory_space=VM)
    smem = pl.BlockSpec(memory_space=pltpu.SMEM)
    shape = jax.ShapeDtypeStruct
    seg_out, in_grad, norms, a_fac, b_fac = pl.pallas_call(
        functools.partial(layer_kernel, sections),
        out_shape=(
            shape((1, micro, half, depth), BF),
            shape((1, micro, half, depth), BF),
            shape((8, depth), F32),
            shape((7, rows, depth), BF),
            shape((chunks, rows, CHUNK), BF),
        ),
        in_specs=[hbm, hbm, hbm, smem, hbm, hbm, vmem, vmem, hbm, hbm, vmem, vmem, hbm, hbm, vmem, vmem],
        out_specs=(vmem, vmem, vmem, hbm, hbm),
        scratch_shapes=[
            VM((3, depth, heads), BF),
            VM((depth, heads), BF),
            VM((depth, width), BF),
            VM((depth, width), BF),
            VM((3, depth, heads), BF),
            VM((depth, heads), BF),
            VM((7, rows, depth), BF),
            VM((chunks, rows, CHUNK), BF),
            VM((3, rows, heads), BF),
            VM((3, rows, heads), BF),
            VM((rows, depth), BF),
            VM((rows, depth), BF),
            VM((rows, depth), BF),
            VM((rows, 1), F32),
            VM((rows, 1), F32),
            VM((rows, 1), F32),
            VM((rows, depth), F32),
            VM((parts, rows, CHUNK), BF),
            VM((rows, depth), BF),
            VM((rows, heads), BF),
            VM((rows, depth), BF),
            VM((3, rows, depth), BF),
            VM((2, micro, half, depth), BF),
            VM((micro, half, depth), F32),
            VM((2, micro, half, depth), BF),
            VM((6, 8, depth), F32),
            pltpu.SemaphoreType.DMA((6,)),
            pltpu.SemaphoreType.DMA((12,)),
            pltpu.SemaphoreType.DMA((5, micro)),
            pltpu.SemaphoreType.DMA((5, micro)),
            pltpu.SemaphoreType.DMA((6, micro)),
            pltpu.SemaphoreType.DMA((6, micro)),
            pltpu.SemaphoreType.DMA((2,)),
        ],
        compiler_params=pltpu.CompilerParams(
            collective_id=0, has_side_effects=True, vmem_limit_bytes=60 * 2**20
        ),
        name="layers",
    )(
        inputs,
        target_inputs,
        cotangent,
        slot_counts,
        w_qkv,
        w_out,
        norm1_gain,
        norm1_bias,
        w_up,
        w_down,
        norm2_gain,
        norm2_bias,
        cross_qkv,
        cross_out,
        norm3_gain[None],
        norm3_bias[None],
    )
    decoder = lax.axis_index("section") == sections - 1

    def weight_grad(left, first, count):
        return jnp.einsum(
            "nd,tnc->tdc", a_fac[left], b_fac[first : first + count], preferred_element_type=F32
        ).astype(BF)

    def shared(grad, axes, dim):
        return lax.psum_scatter(grad, axes, scatter_dimension=dim, tiled=True)

    def wide(grad):
        return jnp.swapaxes(grad, 0, 1).reshape(depth, -1)

    grad_down = shared(wide(weight_grad(0, 0, parts)), "dp", 0)
    grad_up = shared(wide(weight_grad(1, parts, parts)), "dp", 0)
    grad_out = shared(weight_grad(2, 2 * parts, 1)[0], "dp", 0)
    grad_qkv = shared(weight_grad(3, 2 * parts + 1, 3), "dp", 1)
    cross = jnp.concatenate(
        [
            weight_grad(4, 2 * parts + 4, 1),
            weight_grad(5, 2 * parts + 5, 2),
            weight_grad(6, 2 * parts + 7, 1),
        ],
        0,
    )
    cross = shared(jnp.where(decoder, cross, jnp.zeros_like(cross)), ("section", "dp"), 1)
    small = shared(norms[:4], "dp", 1)
    norm3 = jnp.where(decoder, norms[4:6], jnp.zeros_like(norms[4:6]))
    norm3 = shared(norm3, ("section", "dp"), 1)
    return (
        seg_out,
        in_grad,
        grad_qkv[None].astype(F32),
        grad_out[None].astype(F32),
        small[0:1],
        small[1:2],
        grad_up[None].astype(F32),
        grad_down[None].astype(F32),
        small[2:3],
        small[3:4],
        cross[:3].astype(F32),
        cross[3].astype(F32),
        norm3[0],
        norm3[1],
    )


def solution(mesh):
    return jax.shard_map(
        functools.partial(body, mesh.shape["section"]),
        mesh=mesh,
        in_specs=(
            P(None, ("dp", "mp"), None),
            P(None, ("dp", "mp"), None),
            P(None, ("dp", "mp"), None),
            P(),
            P("section", None, None, "mp"),
            P("section", None, "mp"),
            P("section", None),
            P("section", None),
            P("section", None, "mp"),
            P("section", None, "mp"),
            P("section", None),
            P("section", None),
            P(None, None, "mp"),
            P(None, "mp"),
            P(),
            P(),
        ),
        out_specs=(
            P("section", None, ("dp", "mp"), None),
            P("section", None, ("dp", "mp"), None),
            P("section", None, "dp", "mp"),
            P("section", "dp", "mp"),
            P("section", "dp"),
            P("section", "dp"),
            P("section", "dp", "mp"),
            P("section", "dp", "mp"),
            P("section", "dp"),
            P("section", "dp"),
            P(None, ("section", "dp"), "mp"),
            P(("section", "dp"), "mp"),
            P(("section", "dp")),
            P(("section", "dp")),
        ),
        check_vma=False,
    )
```

```python
import functools

import jax
import jax.numpy as jnp
from jax import lax
from jax.experimental import pallas as pl
from jax.experimental.pallas import tpu as pltpu
from jax.sharding import PartitionSpec as P

HEAD = 64
SLOT = 256
QSLOTS = 4
CHUNK = 512
PAIR = 2 * HEAD
STRIP = 64
EPS = 1e-5
NEG = -1000000000.0
MESH = pl.DeviceIdType.MESH
BF = jnp.bfloat16
F32 = jnp.float32
VM = pltpu.VMEM


def dot_nn(a, b):
    return lax.dot_general(a, b, (((1,), (0,)), ((), ())), preferred_element_type=F32)


def dot_nt(a, b):
    return lax.dot_general(a, b, (((1,), (1,)), ((), ())), preferred_element_type=F32)


def dot_tn(a, b):
    return lax.dot_general(a, b, (((0,), (0,)), ((), ())), preferred_element_type=F32)


def loop(count, body):
    def step(i, carry):
        body(i)
        return carry

    lax.fori_loop(0, count, step, 0)


def head_masks():
    lane = lax.broadcasted_iota(jnp.int32, (1, PAIR), 1)
    first = jnp.where(lane < HEAD, 1.0, 0.0).astype(BF)
    second = jnp.where(lane < HEAD, 0.0, 1.0).astype(BF)
    return first, second


def probs_of(query, keys, mask, limit):
    scores = dot_nt(query * (mask * (HEAD**-0.5)).astype(BF), keys)
    if limit is not None:
        row = lax.broadcasted_iota(jnp.int32, scores.shape, 0)
        col = lax.broadcasted_iota(jnp.int32, scores.shape, 1)
        scores = jnp.where(row + limit >= col, scores, NEG)
    expo = jnp.exp(scores - jnp.max(scores, -1, keepdims=True))
    return expo / jnp.sum(expo, -1, keepdims=True)


def attend_forward(proj, mixed, rows, lanes, limit):
    query, keys, values = proj[0, rows, lanes], proj[1, rows, lanes], proj[2, rows, lanes]
    masks = head_masks()
    low = [probs_of(query, keys, mask, limit).astype(BF) for mask in masks]
    mixed[rows, lanes] = dot_nn(
        jnp.concatenate(low, 1), jnp.concatenate([values * mask for mask in masks], 0)
    ).astype(BF)


def attend_backward(proj, d_mixed, d_proj, rows, lanes, limit):
    query, keys, values = proj[0, rows, lanes], proj[1, rows, lanes], proj[2, rows, lanes]
    grad = d_mixed[rows, lanes]
    masks = head_masks()
    low, d_scores = [], []
    for mask in masks:
        weights = probs_of(query, keys, mask, limit)
        d_weights = dot_nt(grad * mask, values)
        inner = jnp.sum(weights * d_weights, -1, keepdims=True)
        d_scores.append((weights * (d_weights - inner)).astype(BF))
        low.append(weights.astype(BF))
    scale = HEAD**-0.5
    d_proj[2, rows, lanes] = dot_tn(
        jnp.concatenate(low, 0), jnp.concatenate([grad * mask for mask in masks], 0)
    ).astype(BF)
    d_proj[0, rows, lanes] = (
        dot_nn(jnp.concatenate(d_scores, 1), jnp.concatenate([keys * mask for mask in masks], 0))
        * scale
    ).astype(BF)
    d_proj[1, rows, lanes] = (
        dot_tn(jnp.concatenate(d_scores, 0), jnp.concatenate([query * mask for mask in masks], 0))
        * scale
    ).astype(BF)


def norm_forward(value, gain, bias):
    center = value - jnp.mean(value, -1, keepdims=True)
    scale = lax.rsqrt(jnp.mean(center * center, -1, keepdims=True) + EPS)
    unit = center * scale
    return unit, scale, unit * gain + bias


def norm_backward(grad, unit, scale, gain, sums, which):
    fold = lambda v: jnp.sum(v.reshape(v.shape[0] // 8, 8, v.shape[1]), 0)
    sums[which] += fold(grad * unit)
    sums[which + 1] += fold(grad)
    d_unit = grad * gain
    first = jnp.mean(d_unit, -1, keepdims=True)
    second = jnp.mean(d_unit * unit, -1, keepdims=True)
    return scale * (d_unit - first - unit * second)


class GradientShare:
    AHEAD = 8
    WINDOW = 4
    DEPTH = 6
    FINAL = 8

    def __init__(self, size, section, dp, core, decoder, a_fac, b_fac, tiles, w_up, w_down, w_cross, slope, resid, *share):
        (self.pair_got, self.acc, self.nb, self.pair_send, self.pair_recv, self.line_send, self.line_recv,
         self.cross_send, self.cross_recv, self.norm_send, self.norm_recv, self.final_sem,
         self.pair_credit, self.left_credit, self.right_credit, self.cross_credit) = share
        self.line = size // 2
        self.section, self.dp, self.core = section, dp, core
        self.decoder, self.encoder = decoder, jnp.logical_not(decoder)
        self.z, self.y = dp // 2, lax.rem(dp, 2)
        self.a_fac, self.b_fac, self.tiles = a_fac, b_fac, tiles
        self.w_up, self.w_down, self.w_cross, self.slope, self.resid = w_up, w_down, w_cross, slope, resid
        self.rows = a_fac.shape[2] // size
        self.own_chunks = b_fac.shape[0] - 4
        self.chunks = self.own_chunks + 2
        self.partner = (section, dp + 1 - 2 * self.y, core)
        self.right = (section, dp + 2, core)
        self.left = (section, dp - 2, core)
        self.across = (1 - section, dp, core)
        self.has_left, self.has_right = self.z > 0, self.z < self.line - 1

    def greet(self, barrier):
        pl.semaphore_signal(barrier, inc=1, device_id=self.partner, device_id_type=MESH)

        @pl.when(self.has_left)
        def _():
            pl.semaphore_signal(barrier, inc=1, device_id=self.left, device_id_type=MESH)

        @pl.when(self.has_right)
        def _():
            pl.semaphore_signal(barrier, inc=1, device_id=self.right, device_id_type=MESH)

        return 1 + jnp.where(self.has_left, 1, 0) + jnp.where(self.has_right, 1, 0)

    def tile_rows(self, k):
        return pl.ds(pl.multiple_of(k * self.rows, self.rows), self.rows)

    def cols(self, k):
        return pl.ds(pl.multiple_of(k * CHUNK, CHUNK), CHUNK)

    def pair_slot(self, i, k):
        return self.w_down.at[self.tile_rows(lax.rem(i, self.AHEAD)), self.cols(k)]

    def pair_copy(self, i, k):
        slot = lax.rem(i, self.AHEAD) * self.line + k
        return pltpu.make_async_remote_copy(
            src_ref=self.pair_slot(i, k),
            dst_ref=self.pair_got.at[slot],
            send_sem=self.pair_send.at[slot],
            recv_sem=self.pair_recv.at[slot],
            device_id=self.partner,
            device_id_type=MESH,
        )

    def line_slot(self, i, k):
        slot = lax.rem(i, self.DEPTH) * self.line + k
        return self.w_cross.at[slot // 8, self.tile_rows(lax.rem(slot, 8))]

    def line_got(self, side, i, k):
        return self.w_up.at[self.tile_rows(lax.rem(i, self.WINDOW) * 2 + side), self.cols(k)]

    def line_copy(self, side, i, k):
        return pltpu.make_async_remote_copy(
            src_ref=self.line_slot(i, k),
            dst_ref=self.line_got(side, i, k),
            send_sem=self.line_send.at[lax.rem(i, self.DEPTH) * self.line + k],
            recv_sem=self.line_recv.at[side, lax.rem(i, self.WINDOW) * self.line + k],
            device_id=self.left if side else self.right,
            device_id_type=MESH,
        )

    def cross_copy(self, q):
        return pltpu.make_async_remote_copy(
            src_ref=self.slope.at[q],
            dst_ref=self.slope.at[q],
            send_sem=self.cross_send.at[q],
            recv_sem=self.cross_recv.at[q],
            device_id=self.across,
            device_id_type=MESH,
        )

    def own_tile(self, i, k, y):
        main = i < self.own_chunks

        @pl.when(main)
        def _():
            left = jnp.minimum(i // 4, 2) + jnp.where(i > 8, 1, 0)
            shard = k * 2 + y
            self.acc[...] = dot_tn(self.a_fac[left, :, self.tile_rows(shard)], self.b_fac[i])

        first = (i - self.own_chunks) * 2
        small = self.rows // 2

        @pl.when(jnp.logical_not(main) & self.decoder)
        def _():
            base = self.a_fac.shape[2] // 2
            for e in range(2):
                q = first + e
                block = dot_tn(
                    self.a_fac[4 + (q + 1) // 2, :, pl.ds(pl.multiple_of(base + k * self.rows, self.rows), self.rows)],
                    self.b_fac[self.own_chunks + q],
                )
                self.acc[e * small : (e + 1) * small] = jnp.where(y == 0, block[:small], block[small:])

        @pl.when(jnp.logical_not(main) & self.encoder)
        def _():
            for e in range(2):
                place = pl.ds(pl.multiple_of(k * self.rows + y * small, small), small)
                self.acc[e * small : (e + 1) * small] = self.slope[first + e, place].astype(F32)

    def pair_step(self, i):
        @pl.when(i >= self.AHEAD)
        def _():
            pl.semaphore_wait(self.pair_credit, 1)

        @pl.when((i >= self.own_chunks) & self.encoder)
        def _():
            for e in range(2):
                self.cross_copy((i - self.own_chunks) * 2 + e).wait_recv()

        def one(k):
            @pl.when(i >= self.AHEAD)
            def _():
                self.pair_copy(i, k).wait_send()

            self.own_tile(i, k, 1 - self.y)
            slot = self.pair_slot(i, k)
            slot[...] = self.acc[...].astype(BF)
            self.pair_copy(i, k).start()

        loop(self.line, one)

    def begin(self):
        @pl.when(self.has_left)
        def _():
            pl.semaphore_signal(self.right_credit, inc=self.WINDOW, device_id=self.left, device_id_type=MESH)

        @pl.when(self.has_right)
        def _():
            pl.semaphore_signal(self.left_credit, inc=self.WINDOW, device_id=self.right, device_id_type=MESH)

        @pl.when(self.encoder)
        def _():
            pl.semaphore_signal(self.cross_credit, inc=1, device_id=self.across, device_id_type=MESH)

        loop(self.AHEAD, self.pair_step)

    def line_step(self, i):
        @pl.when(self.has_right)
        def _():
            pl.semaphore_wait(self.right_credit, 1)

        @pl.when(self.has_left)
        def _():
            pl.semaphore_wait(self.left_credit, 1)

        def partial(k):
            self.own_tile(i, k, self.y)
            self.pair_copy(i, k).wait_recv()
            slot = lax.rem(i, self.AHEAD) * self.line + k
            self.acc[...] += self.pair_got[slot].astype(F32)

        def arrived(side, k):
            self.line_copy(side, i, k).wait_recv()
            self.acc[...] += self.line_got(side, i, k)[...].astype(F32)

        def send(side, k, inner):
            @pl.when(i >= self.DEPTH)
            def _():
                self.line_copy(side, i, k).wait_send()

            partial(k)

            @pl.when(inner)
            def _():
                arrived(side, k)

            slot = self.line_slot(i, k)
            slot[...] = self.acc[...].astype(BF)
            self.line_copy(side, i, k).start()

        def to_right(j):
            k = self.line - 1 - j

            @pl.when(k > self.z)
            def _():
                send(0, k, self.has_left)

        def to_left(k):
            @pl.when(k < self.z)
            def _():
                send(1, k, self.has_right)

        loop(self.line - 1, to_right)
        loop(self.line - 1, to_left)
        partial(self.z)

        @pl.when(self.has_left)
        def _():
            arrived(0, self.z)

        @pl.when(self.has_right)
        def _():
            arrived(1, self.z)

        @pl.when(i >= self.FINAL)
        def _():
            self.final_copy(i).wait()

        slot = self.final_slot(i)
        slot[...] = self.acc[...]
        self.final_copy(i).start()

        @pl.when(i + self.WINDOW < self.chunks)
        def _():
            @pl.when(self.has_left)
            def _():
                pl.semaphore_signal(self.right_credit, inc=1, device_id=self.left, device_id_type=MESH)

            @pl.when(self.has_right)
            def _():
                pl.semaphore_signal(self.left_credit, inc=1, device_id=self.right, device_id_type=MESH)

        @pl.when(i + self.AHEAD < self.chunks)
        def _():
            pl.semaphore_signal(self.pair_credit, inc=1, device_id=self.partner, device_id_type=MESH)
            self.pair_step(i + self.AHEAD)

    def final_slot(self, i):
        slot = lax.rem(i, self.FINAL)
        return self.resid.at[self.tile_rows(slot // 2), self.cols(lax.rem(slot, 2))]

    def final_copy(self, i):
        return pltpu.make_async_copy(
            self.final_slot(i), self.tiles.at[i], self.final_sem.at[lax.rem(i, self.FINAL)]
        )

    def cross_part(self):
        @pl.when(self.decoder)
        def _():
            pl.semaphore_wait(self.cross_credit, 1)

            def one(q):
                def tile(k):
                    self.slope[q, self.tile_rows(k)] = dot_tn(
                        self.a_fac[4 + (q + 1) // 2, :, self.tile_rows(k)],
                        self.b_fac[self.own_chunks + q],
                    ).astype(BF)

                loop(4, tile)
                self.cross_copy(q).start()

            loop(4, one)

    def norm_copy(self, src, dst, device):
        return pltpu.make_async_remote_copy(
            src_ref=self.nb.at[src],
            dst_ref=self.nb.at[dst],
            send_sem=self.norm_send.at[dst],
            recv_sem=self.norm_recv.at[dst],
            device_id=device,
            device_id_type=MESH,
        )

    def norms(self, sums, norm_out, norm3_out):
        nb, has_left, has_right = self.nb, self.has_left, self.has_right
        for i in range(6):
            nb[0, i : i + 1] = jnp.sum(sums[i], 0, keepdims=True)
        nb[0, 6:8] = jnp.zeros_like(nb[0, 6:8])
        to_right = self.norm_copy(3, 1, self.right)
        to_left = self.norm_copy(4, 2, self.left)
        nb[3] = nb[0]
        nb[4] = nb[0]
        nb[5] = nb[0]

        @pl.when(jnp.logical_not(has_left))
        def _():
            to_right.start()

        @pl.when(jnp.logical_not(has_right))
        def _():
            to_left.start()

        @pl.when(has_left)
        def _():
            to_right.wait_recv()
            nb[5] += nb[1]

            @pl.when(has_right)
            def _():
                nb[3] += nb[1]
                to_right.start()

        @pl.when(has_right)
        def _():
            to_left.wait_recv()
            nb[5] += nb[2]

            @pl.when(has_left)
            def _():
                nb[4] += nb[2]
                to_left.start()

        self.norm_copy(5, 6, self.partner).start()
        self.norm_out, self.norm3_out = norm_out, norm3_out

    def finish_norms(self):
        nb = self.nb
        self.norm_copy(5, 6, self.partner).wait()

        @pl.when(self.has_right)
        def _():
            self.norm_copy(3, 1, self.right).wait_send()

        @pl.when(self.has_left)
        def _():
            self.norm_copy(4, 2, self.left).wait_send()

        nb[7] = nb[5] + nb[6]
        hand = self.norm_copy(7, 8, self.across)

        @pl.when(self.decoder)
        def _():
            hand.start()
            nb[8] = nb[7]

        self.norm_out[...] = nb[7, :, pl.ds(pl.multiple_of(self.dp * 128, 128), 128)]

        @pl.when(self.encoder)
        def _():
            hand.wait_recv()

        place = self.section * self.line * 2 + self.dp
        block = nb[8, :, pl.ds(pl.multiple_of(place // 2 * 128, 128), 128)]
        self.norm3_out[...] = jnp.where(self.y == 0, block, pltpu.roll(block, 64, 1))

        @pl.when(self.decoder)
        def _():
            hand.wait_send()

    def run(self):
        loop(self.chunks - 2, self.line_step)
        self.finish_norms()
        loop(2, lambda p: self.line_step(self.chunks - 2 + p))

    def drain(self):
        for slot in range(self.AHEAD):
            for k in range(self.line):
                self.pair_copy(slot, k).wait_send()

        for slot in range(self.DEPTH):
            for k in range(self.line):

                @pl.when(self.z != k)
                def _():
                    self.line_copy(0, slot, k).wait_send()

        for slot in range(self.FINAL):
            self.final_copy(slot).wait()

        @pl.when(self.decoder)
        def _():
            for q in range(4):
                self.cross_copy(q).wait_send()


def layer_kernel(
    sections,
    ring,
    inputs,
    targets,
    cotangent,
    counts,
    qkv_hbm,
    out_hbm,
    gain1,
    bias1,
    up_hbm,
    down_hbm,
    gain2,
    bias2,
    cross_hbm,
    cross_out_hbm,
    gain3,
    bias3,
    seg_out,
    in_grad,
    norm_out,
    first_out,
    second_out,
    w_qkv,
    w_out,
    w_up,
    w_down,
    w_cross,
    w_cross_out,
    a_fac,
    b_fac,
    proj,
    cross_proj,
    unit1,
    unit2,
    unit3,
    scale1,
    scale2,
    scale3,
    resid,
    slope,
    d_out,
    d_mix,
    sent,
    got,
    half_send,
    half_own,
    half_got,
    sums,
    load_sem,
    x_sem,
    ex_send,
    ex_recv,
    hop_send,
    hop_recv,
    out_sem,
    *share,
):
    section = lax.axis_index("section")
    dp = lax.axis_index("dp")
    core = lax.axis_index("mp")
    decoder = section == sections - 1
    encoder = section != sections - 1
    mate = (section, dp, 1 - core)
    across = (1 - section, dp, core)
    half = seg_out.shape[2]
    slot = 2 * half
    limit = jnp.where(decoder, 0, slot)
    width = w_up.shape[1]
    parts = width // CHUNK
    own = core * half
    other = (1 - core) * half

    d_branch, crossed, d_attn, layer_in, normed_low, memory, d_cross = (a_fac.at[i] for i in range(7))
    act = b_fac.at[0:parts]
    d_hidden = b_fac.at[parts : 2 * parts]
    mixed = b_fac.at[2 * parts]
    d_proj = b_fac.at[2 * parts + 1 : 2 * parts + 4]
    d_cross_proj = b_fac.at[2 * parts + 4 : 2 * parts + 7]
    cross_mixed = b_fac.at[2 * parts + 7]

    def rows_of(m):
        return pl.ds(pl.multiple_of(m * slot, slot), slot)

    def half_of(m, offset):
        return pl.ds(pl.multiple_of(m * slot + offset, half), half)

    def strip_of(m, k):
        return pl.ds(pl.multiple_of(m * slot + k * STRIP, STRIP), STRIP)

    def lanes_of(j):
        return pl.ds(pl.multiple_of(j * PAIR, PAIR), PAIR)

    barrier = pltpu.get_barrier_semaphore()
    for device in (mate, across):
        pl.semaphore_signal(barrier, inc=1, device_id=device, device_id_type=MESH)
    if ring:
        total = GradientShare(ring, section, dp, core, decoder, a_fac, b_fac, first_out, w_up, w_down, w_cross, slope, resid, *share)
        greeted = 2 + total.greet(barrier)
    else:
        greeted = 2

    loads = [
        pltpu.make_async_copy(src, dst, load_sem.at[i])
        for i, (src, dst) in enumerate(
            (
                (qkv_hbm.at[0], w_qkv),
                (out_hbm.at[0], w_out),
                (up_hbm.at[0], w_up),
                (down_hbm.at[0], w_down),
                (cross_hbm, w_cross),
                (cross_out_hbm, w_cross_out),
            )
        )
    ]

    def local_rows(src, dst, m, sem):
        return pltpu.make_async_copy(src.at[m], dst.at[half_of(m, own)], sem)

    def mate_rows(src, dst, m, send, recv):
        return pltpu.make_async_remote_copy(
            src_ref=src.at[m],
            dst_ref=dst.at[half_of(m, own)],
            send_sem=send,
            recv_sem=recv,
            device_id=mate,
            device_id_type=MESH,
        )

    def start_rows(src, dst, base):
        for m in range(2):
            local_rows(src, dst, m, x_sem.at[base + m]).start()
        for m in range(2):
            mate_rows(src, dst, m, x_sem.at[base + 2 + m], x_sem.at[base + 4 + m]).start()

    def wait_rows(src, dst, base, m):
        local_rows(src, dst, m, x_sem.at[base + m]).wait()
        mate_rows(src, dst, m, x_sem.at[base + 2 + m], x_sem.at[base + 4 + m]).wait()

    @pl.when(encoder)
    def _():
        for m in range(2):
            local_rows(inputs, layer_in, m, x_sem.at[m]).start()

    @pl.when(decoder)
    def _():
        for m in range(2):
            local_rows(targets, layer_in, m, x_sem.at[m]).start()

    loads[0].start()
    loads[1].start()
    pl.semaphore_wait(barrier, greeted)

    def mate_start(src, dst, base):
        for m in range(2):
            mate_rows(src, dst, m, x_sem.at[base + 2 + m], x_sem.at[base + 4 + m]).start()

    @pl.when(encoder)
    def _():
        mate_start(inputs, layer_in, 0)

    @pl.when(decoder)
    def _():
        mate_start(targets, layer_in, 0)

    for copy in loads[2:]:
        copy.start()

    @pl.when(decoder)
    def _():
        start_rows(cotangent, d_out, 6)

    sums[...] = jnp.zeros_like(sums)

    def exchange(which, buffer, m):
        return pltpu.make_async_remote_copy(
            src_ref=sent.at[rows_of(m)],
            dst_ref=got.at[buffer, rows_of(m)],
            send_sem=ex_send.at[which, m],
            recv_sem=ex_recv.at[which, m],
            device_id=mate,
            device_id_type=MESH,
        )

    def half_exchange(which, m):
        return pltpu.make_async_remote_copy(
            src_ref=half_send.at[which, m],
            dst_ref=half_got.at[which, m],
            send_sem=hop_send.at[4 + which, m],
            recv_sem=hop_recv.at[4 + which, m],
            device_id=mate,
            device_id_type=MESH,
        )

    def across_copy(src, dst, which, m):
        return pltpu.make_async_remote_copy(
            src_ref=src,
            dst_ref=dst.at[half_of(m, own)],
            send_sem=hop_send.at[which, m],
            recv_sem=hop_recv.at[which, m],
            device_id=across,
            device_id_type=MESH,
        )

    def forward_copy(ref, which, m):
        return pltpu.make_async_remote_copy(
            src_ref=ref.at[half_of(m, own)],
            dst_ref=ref.at[half_of(m, own)],
            send_sem=hop_send.at[which, m],
            recv_sem=hop_recv.at[which, m],
            device_id=mate,
            device_id_type=MESH,
        )

    def project_out(value, weight, m):
        for n in range(sent.shape[1] // CHUNK):
            cols = slice(n * CHUNK, (n + 1) * CHUNK)
            sent[rows_of(m), cols] = dot_nt(value, weight[cols, :]).astype(BF)

    def summed(buffer, strip):
        return sent[strip].astype(F32) + got[buffer, strip].astype(F32)

    loads[0].wait()

    def attention_in(m):
        @pl.when(encoder)
        def _():
            wait_rows(inputs, layer_in, 0, m)

        @pl.when(decoder)
        def _():
            wait_rows(targets, layer_in, 0, m)

        rows = rows_of(m)
        for t in range(3):
            proj[t, rows] = dot_nn(layer_in[rows], w_qkv[t]).astype(BF)
        loop(CHUNK // PAIR, lambda j: attend_forward(proj, mixed, rows, lanes_of(j), limit))
        project_out(mixed[rows], w_out, m)
        exchange(0, 0, m).start()

    loads[1].wait()
    loop(2, attention_in)
    for copy in loads[2:]:
        copy.wait()

    def after_attention(m):
        exchange(0, 0, m).wait()

        def norm(k):
            strip = strip_of(m, k)
            unit, scale, value = norm_forward(
                layer_in[strip].astype(F32) + summed(0, strip), gain1[...], bias1[...]
            )
            unit1[strip] = unit.astype(BF)
            scale1[strip] = scale
            resid[strip] = value
            normed_low[strip] = value.astype(BF)
            crossed[strip] = value.astype(BF)

        loop(slot // STRIP, norm)

        @pl.when(decoder)
        def _():
            rows = rows_of(m)
            cross_proj[0, rows] = dot_nn(normed_low[rows], w_cross[0]).astype(BF)
            across_copy(seg_out.at[0, m], memory, 0, m).wait_recv()
            forward_copy(memory, 1, m).start()
            forward_copy(memory, 1, m).wait()
            for t in range(1, 3):
                cross_proj[t, rows] = dot_nn(memory[rows], w_cross[t]).astype(BF)
            loop(
                CHUNK // PAIR,
                lambda j: attend_forward(cross_proj, cross_mixed, rows, lanes_of(j), None),
            )
            project_out(cross_mixed[rows], w_cross_out, m)
            exchange(1, 1, m).start()

    loop(2, after_attention)

    def feed_forward(m):
        rows = rows_of(m)

        @pl.when(decoder)
        def _():
            exchange(1, 1, m).wait()

            def norm(k):
                strip = strip_of(m, k)
                unit, scale, value = norm_forward(
                    resid[strip] + summed(1, strip), gain3[...], bias3[...]
                )
                unit3[strip] = unit.astype(BF)
                scale3[strip] = scale
                resid[strip] = value
                crossed[strip] = value.astype(BF)

            loop(slot // STRIP, norm)

        for n in range(parts):
            pre = dot_nn(crossed[rows], w_up[:, n * CHUNK : (n + 1) * CHUNK])
            rise = 0.5 + 0.5 * lax.erf(pre * (0.5**0.5))
            act[n, rows] = (pre * rise).astype(BF)
            slope[n, rows] = (rise + pre * jnp.exp(-0.5 * pre * pre) * 0.3989422804014327).astype(BF)
        project_out(jnp.concatenate([act[n, rows] for n in range(parts)], 1), w_down, m)
        exchange(2, 2, m).start()

    loop(2, feed_forward)

    def finish_forward(m):
        exchange(2, 2, m).wait()

        def norm(k):
            strip = strip_of(m, k)
            unit, scale, value = norm_forward(
                resid[strip] + summed(2, strip), gain2[...], bias2[...]
            )
            unit2[strip] = unit.astype(BF)
            scale2[strip] = scale
            place = k * STRIP - own

            @pl.when((place >= 0) & (place < half))
            def _():
                seg_out[0, m, pl.ds(pl.multiple_of(lax.rem(k * STRIP, half), STRIP), STRIP)] = (
                    value.astype(BF)
                )

        loop(slot // STRIP, norm)

        @pl.when(encoder)
        def _():
            across_copy(seg_out.at[0, m], memory, 0, m).start()

    loop(2, finish_forward)

    question = dp // QSLOTS
    spot = dp - question * QSLOTS

    def feed_backward(m):
        rows = rows_of(m)

        @pl.when(encoder)
        def _():
            across_copy(half_send.at[0, m], d_out, 2, m).wait_recv()
            forward_copy(d_out, 3, m).start()
            forward_copy(d_out, 3, m).wait()

        @pl.when(decoder)
        def _():
            wait_rows(cotangent, d_out, 6, m)

        keep = jnp.where(spot < counts[m, question], 1.0, 0.0)
        keep = jnp.where(decoder, keep, 1.0)

        def norm(k):
            strip = strip_of(m, k)
            grad = norm_backward(
                d_out[strip].astype(F32) * keep,
                unit2[strip].astype(F32),
                scale2[strip],
                gain2[...],
                sums,
                2,
            )
            resid[strip] = grad
            d_branch[strip] = grad.astype(BF)

        loop(slot // STRIP, norm)
        for n in range(parts):
            grad = dot_nn(d_branch[rows], w_down[:, n * CHUNK : (n + 1) * CHUNK])
            d_hidden[n, rows] = (grad * slope[n, rows].astype(F32)).astype(BF)
        project_out(jnp.concatenate([d_hidden[n, rows] for n in range(parts)], 1), w_up, m)
        exchange(3, 0, m).start()

    loop(2, feed_backward)
    if ring:
        total.begin()

    def cross_backward(m):
        rows = rows_of(m)

        def norm(k):
            strip = strip_of(m, k)
            grad = norm_backward(
                resid[strip] + summed(0, strip),
                unit3[strip].astype(F32),
                scale3[strip],
                gain3[...],
                sums,
                4,
            )
            resid[strip] = grad
            d_cross[strip] = grad.astype(BF)

        loop(slot // STRIP, norm)
        d_mix[rows] = dot_nn(d_cross[rows], w_cross_out[...]).astype(BF)
        loop(
            CHUNK // PAIR,
            lambda j: attend_backward(cross_proj, d_mix, d_cross_proj, rows, lanes_of(j), None),
        )

        def memory_part(offset):
            piece = half_of(m, offset)
            return jnp.concatenate([d_cross_proj[1, piece], d_cross_proj[2, piece]], 1)

        def memory_weight(n):
            cols = slice(n * CHUNK, (n + 1) * CHUNK)
            return jnp.concatenate([w_cross[1, cols], w_cross[2, cols]], 1)

        for n in range(sent.shape[1] // CHUNK):
            cols = slice(n * CHUNK, (n + 1) * CHUNK)
            half_send[0, m, :, cols] = dot_nt(memory_part(other), memory_weight(n)).astype(BF)
        half_exchange(0, m).start()
        for n in range(sent.shape[1] // CHUNK):
            cols = slice(n * CHUNK, (n + 1) * CHUNK)
            half_own[m, :, cols] = dot_nt(memory_part(own), memory_weight(n))
        project_out(d_cross_proj[0, rows], w_cross[0], m)
        exchange(4, 1, m).start()
        half_exchange(0, m).wait()
        half_send[0, m] = (half_own[m] + half_got[0, m].astype(F32)).astype(BF)
        across_copy(half_send.at[0, m], d_out, 2, m).start()

    def attention_back(m):
        rows = rows_of(m)

        def norm_rows(buffer):
            def norm(k):
                strip = strip_of(m, k)
                grad = norm_backward(
                    resid[strip] + summed(buffer, strip),
                    unit1[strip].astype(F32),
                    scale1[strip],
                    gain1[...],
                    sums,
                    0,
                )
                resid[strip] = grad
                d_attn[strip] = grad.astype(BF)

            loop(slot // STRIP, norm)

        @pl.when(decoder)
        def _():
            exchange(4, 1, m).wait()

        @pl.when(encoder)
        def _():
            exchange(3, 0, m).wait()

        norm_rows(jnp.where(decoder, 1, 0))
        d_mix[rows] = dot_nn(d_attn[rows], w_out[...]).astype(BF)
        loop(
            CHUNK // PAIR, lambda j: attend_backward(proj, d_mix, d_proj, rows, lanes_of(j), limit)
        )

        def input_part(offset):
            piece = half_of(m, offset)
            return jnp.concatenate([d_proj[t, piece] for t in range(3)], 1)

        def input_weight(n):
            cols = slice(n * CHUNK, (n + 1) * CHUNK)
            return jnp.concatenate([w_qkv[t, cols] for t in range(3)], 1)

        for n in range(sent.shape[1] // CHUNK):
            cols = slice(n * CHUNK, (n + 1) * CHUNK)
            half_send[1, m, :, cols] = dot_nt(input_part(other), input_weight(n)).astype(BF)
        half_exchange(1, m).start()
        for n in range(sent.shape[1] // CHUNK):
            cols = slice(n * CHUNK, (n + 1) * CHUNK)
            half_own[m, :, cols] = dot_nt(input_part(own), input_weight(n))

    @pl.when(decoder)
    def _():
        def both(m):
            exchange(3, 0, m).wait()
            cross_backward(m)

        loop(2, both)

    loop(2, attention_back)

    def finish_backward(m):
        half_exchange(1, m).wait()
        in_grad[0, m] = (
            resid[half_of(m, own)] + half_own[m] + half_got[1, m].astype(F32)
        ).astype(BF)

    loop(2, finish_backward)

    @pl.when(encoder)
    def _():
        for m in range(2):
            across_copy(seg_out.at[0, m], memory, 0, m).wait_send()

    @pl.when(decoder)
    def _():
        for m in range(2):
            across_copy(half_send.at[0, m], d_out, 2, m).wait_send()

    if ring:
        total.norms(sums, norm_out, second_out)
        total.cross_part()
        total.run()
        total.drain()
        return

    for i in range(6):
        norm_out[i : i + 1] = jnp.sum(sums[i], 0, keepdims=True)
    norm_out[6:8] = jnp.zeros_like(norm_out[6:8])
    copies = [
        pltpu.make_async_copy(a_fac, first_out, out_sem.at[0]),
        pltpu.make_async_copy(b_fac, second_out, out_sem.at[1]),
    ]
    for copy in copies:
        copy.start()
    for copy in copies:
        copy.wait()


def body(
    sections,
    ring,
    inputs,
    target_inputs,
    cotangent,
    slot_counts,
    w_qkv,
    w_out,
    norm1_gain,
    norm1_bias,
    w_up,
    w_down,
    norm2_gain,
    norm2_bias,
    cross_qkv,
    cross_out,
    norm3_gain,
    norm3_bias,
):
    micro, half, depth = inputs.shape
    rows = micro * 2 * half
    heads = w_out.shape[2]
    width = w_up.shape[2]
    parts = width // CHUNK
    chunks = 2 * parts + 8
    hbm = pl.BlockSpec(memory_space=pl.ANY)
    vmem = pl.BlockSpec(memory_space=VM)
    smem = pl.BlockSpec(memory_space=pltpu.SMEM)
    shape = jax.ShapeDtypeStruct
    if ring:
        results = (
            shape((8, depth // ring), F32),
            shape((chunks - 2, depth // ring, CHUNK), F32),
            shape((8, depth // ring), F32),
        )
        places = (vmem, hbm, vmem)
    else:
        results = (
            shape((8, depth), F32),
            shape((7, rows, depth), BF),
            shape((chunks, rows, CHUNK), BF),
        )
        places = (vmem, hbm, hbm)
    dma = pltpu.SemaphoreType.DMA
    regular = pltpu.SemaphoreType.REGULAR
    tile = (depth // ring, CHUNK) if ring else None
    share = (
        [
            VM((GradientShare.AHEAD * 4,) + tile, BF),
            VM(tile, F32),
            VM((9, 8, depth), F32),
            dma((GradientShare.AHEAD * 4,)),
            dma((GradientShare.AHEAD * 4,)),
            dma((GradientShare.DEPTH * 4,)),
            dma((2, GradientShare.WINDOW * 4)),
            dma((4,)),
            dma((4,)),
            dma((9,)),
            dma((9,)),
            dma((GradientShare.FINAL,)),
            regular,
            regular,
            regular,
            regular,
        ]
        if ring
        else []
    )
    seg_out, in_grad, norms, first, second = pl.pallas_call(
        functools.partial(layer_kernel, sections, ring),
        out_shape=(
            shape((1, micro, half, depth), BF),
            shape((1, micro, half, depth), BF),
        )
        + results,
        in_specs=[hbm, hbm, hbm, smem, hbm, hbm, vmem, vmem, hbm, hbm, vmem, vmem, hbm, hbm, vmem, vmem],
        out_specs=(vmem, vmem) + places,
        scratch_shapes=[
            VM((3, depth, heads), BF),
            VM((depth, heads), BF),
            VM((depth, width), BF),
            VM((depth, width), BF),
            VM((3, depth, heads), BF),
            VM((depth, heads), BF),
            VM((7, rows, depth), BF),
            VM((chunks, rows, CHUNK), BF),
            VM((3, rows, heads), BF),
            VM((3, rows, heads), BF),
            VM((rows, depth), BF),
            VM((rows, depth), BF),
            VM((rows, depth), BF),
            VM((rows, 1), F32),
            VM((rows, 1), F32),
            VM((rows, 1), F32),
            VM((rows, depth), F32),
            VM((parts, rows, CHUNK), BF),
            VM((rows, depth), BF),
            VM((rows, heads), BF),
            VM((rows, depth), BF),
            VM((3, rows, depth), BF),
            VM((2, micro, half, depth), BF),
            VM((micro, half, depth), F32),
            VM((2, micro, half, depth), BF),
            VM((6, 8, depth), F32),
            pltpu.SemaphoreType.DMA((6,)),
            pltpu.SemaphoreType.DMA((12,)),
            pltpu.SemaphoreType.DMA((5, micro)),
            pltpu.SemaphoreType.DMA((5, micro)),
            pltpu.SemaphoreType.DMA((6, micro)),
            pltpu.SemaphoreType.DMA((6, micro)),
            pltpu.SemaphoreType.DMA((2,)),
        ]
        + share,
        compiler_params=pltpu.CompilerParams(
            collective_id=0, has_side_effects=True, vmem_limit_bytes=60 * 2**20
        ),
        name="layers",
    )(
        inputs,
        target_inputs,
        cotangent,
        slot_counts,
        w_qkv,
        w_out,
        norm1_gain,
        norm1_bias,
        w_up,
        w_down,
        norm2_gain,
        norm2_bias,
        cross_qkv,
        cross_out,
        norm3_gain[None],
        norm3_bias[None],
    )
    if ring:
        own = lambda first_one, count: jnp.swapaxes(
            first[first_one : first_one + count], 0, 1
        ).reshape(1, depth // ring, count * CHUNK)
        cross = first[2 * parts + 4 :].reshape(4, depth // ring // 2, CHUNK)
        lanes = depth // ring // 2
        return (
            seg_out,
            in_grad,
            first[None, 2 * parts + 1 : 2 * parts + 4],
            first[2 * parts : 2 * parts + 1],
            norms[0:1],
            norms[1:2],
            own(parts, parts),
            own(0, parts),
            norms[2:3],
            norms[3:4],
            cross[:3],
            cross[3],
            second[4, :lanes],
            second[5, :lanes],
        )
    a_fac, b_fac = first, second
    decoder = lax.axis_index("section") == sections - 1

    def weight_grad(left, first, count):
        return jnp.einsum(
            "nd,tnc->tdc", a_fac[left], b_fac[first : first + count], preferred_element_type=F32
        ).astype(BF)

    def shared(grad, axes, dim):
        return lax.psum_scatter(grad, axes, scatter_dimension=dim, tiled=True)

    def wide(grad):
        return jnp.swapaxes(grad, 0, 1).reshape(depth, -1)

    grad_down = shared(wide(weight_grad(0, 0, parts)), "dp", 0)
    grad_up = shared(wide(weight_grad(1, parts, parts)), "dp", 0)
    grad_out = shared(weight_grad(2, 2 * parts, 1)[0], "dp", 0)
    grad_qkv = shared(weight_grad(3, 2 * parts + 1, 3), "dp", 1)
    cross = jnp.concatenate(
        [
            weight_grad(4, 2 * parts + 4, 1),
            weight_grad(5, 2 * parts + 5, 2),
            weight_grad(6, 2 * parts + 7, 1),
        ],
        0,
    )
    cross = shared(jnp.where(decoder, cross, jnp.zeros_like(cross)), ("section", "dp"), 1)
    small = shared(norms[:4], "dp", 1)
    norm3 = jnp.where(decoder, norms[4:6], jnp.zeros_like(norms[4:6]))
    norm3 = shared(norm3, ("section", "dp"), 1)
    return (
        seg_out,
        in_grad,
        grad_qkv[None].astype(F32),
        grad_out[None].astype(F32),
        small[0:1],
        small[1:2],
        grad_up[None].astype(F32),
        grad_down[None].astype(F32),
        small[2:3],
        small[3:4],
        cross[:3].astype(F32),
        cross[3].astype(F32),
        norm3[0],
        norm3[1],
    )


def solution(mesh):
    ring = 8 if mesh.shape["dp"] == 8 else 0
    return jax.shard_map(
        functools.partial(body, mesh.shape["section"], ring),
        mesh=mesh,
        in_specs=(
            P(None, ("dp", "mp"), None),
            P(None, ("dp", "mp"), None),
            P(None, ("dp", "mp"), None),
            P(),
            P("section", None, None, "mp"),
            P("section", None, "mp"),
            P("section", None),
            P("section", None),
            P("section", None, "mp"),
            P("section", None, "mp"),
            P("section", None),
            P("section", None),
            P(None, None, "mp"),
            P(None, "mp"),
            P(),
            P(),
        ),
        out_specs=(
            P("section", None, ("dp", "mp"), None),
            P("section", None, ("dp", "mp"), None),
            P("section", None, "dp", "mp"),
            P("section", "dp", "mp"),
            P("section", "dp"),
            P("section", "dp"),
            P("section", "dp", "mp"),
            P("section", "dp", "mp"),
            P("section", "dp"),
            P("section", "dp"),
            P(None, ("section", "dp"), "mp"),
            P(("section", "dp"), "mp"),
            P(("section", "dp")),
            P(("section", "dp")),
        ),
        check_vma=False,
    )
```

```python
import functools

import jax
import jax.numpy as jnp
from jax import lax
from jax.experimental import pallas as pl
from jax.experimental.pallas import tpu as pltpu
from jax.sharding import PartitionSpec as P

HEAD = 64
SLOT = 256
QSLOTS = 4
CHUNK = 512
PAIR = 2 * HEAD
STRIP = 64
EPS = 1e-5
NEG = -1000000000.0
MESH = pl.DeviceIdType.MESH
BF = jnp.bfloat16
F32 = jnp.float32
VM = pltpu.VMEM


def dot_nn(a, b):
    return lax.dot_general(a, b, (((1,), (0,)), ((), ())), preferred_element_type=F32)


def dot_nt(a, b):
    return lax.dot_general(a, b, (((1,), (1,)), ((), ())), preferred_element_type=F32)


def dot_tn(a, b):
    return lax.dot_general(a, b, (((0,), (0,)), ((), ())), preferred_element_type=F32)


def loop(count, body):
    def step(i, carry):
        body(i)
        return carry

    lax.fori_loop(0, count, step, 0)


def head_masks():
    lane = lax.broadcasted_iota(jnp.int32, (1, PAIR), 1)
    first = jnp.where(lane < HEAD, 1.0, 0.0).astype(BF)
    second = jnp.where(lane < HEAD, 0.0, 1.0).astype(BF)
    return first, second


def probs_of(query, keys, mask, limit):
    scores = dot_nt(query * (mask * (HEAD**-0.5)).astype(BF), keys)
    if limit is not None:
        row = lax.broadcasted_iota(jnp.int32, scores.shape, 0)
        col = lax.broadcasted_iota(jnp.int32, scores.shape, 1)
        scores = jnp.where(row + limit >= col, scores, NEG)
    expo = jnp.exp(scores - jnp.max(scores, -1, keepdims=True))
    return expo / jnp.sum(expo, -1, keepdims=True)


def attend_forward(proj, mixed, rows, lanes, limit):
    query, keys, values = proj[0, rows, lanes], proj[1, rows, lanes], proj[2, rows, lanes]
    masks = head_masks()
    low = [probs_of(query, keys, mask, limit).astype(BF) for mask in masks]
    mixed[rows, lanes] = dot_nn(
        jnp.concatenate(low, 1), jnp.concatenate([values * mask for mask in masks], 0)
    ).astype(BF)


def attend_backward(proj, d_mixed, d_proj, rows, lanes, limit):
    query, keys, values = proj[0, rows, lanes], proj[1, rows, lanes], proj[2, rows, lanes]
    grad = d_mixed[rows, lanes]
    masks = head_masks()
    low, d_scores = [], []
    for mask in masks:
        weights = probs_of(query, keys, mask, limit)
        d_weights = dot_nt(grad * mask, values)
        inner = jnp.sum(weights * d_weights, -1, keepdims=True)
        d_scores.append((weights * (d_weights - inner)).astype(BF))
        low.append(weights.astype(BF))
    scale = HEAD**-0.5
    d_proj[2, rows, lanes] = dot_tn(
        jnp.concatenate(low, 0), jnp.concatenate([grad * mask for mask in masks], 0)
    ).astype(BF)
    d_proj[0, rows, lanes] = (
        dot_nn(jnp.concatenate(d_scores, 1), jnp.concatenate([keys * mask for mask in masks], 0))
        * scale
    ).astype(BF)
    d_proj[1, rows, lanes] = (
        dot_tn(jnp.concatenate(d_scores, 0), jnp.concatenate([query * mask for mask in masks], 0))
        * scale
    ).astype(BF)


def norm_forward(value, gain, bias):
    center = value - jnp.mean(value, -1, keepdims=True)
    scale = lax.rsqrt(jnp.mean(center * center, -1, keepdims=True) + EPS)
    unit = center * scale
    return unit, scale, unit * gain + bias


def norm_backward(grad, unit, scale, gain, sums, which):
    fold = lambda v: jnp.sum(v.reshape(v.shape[0] // 8, 8, v.shape[1]), 0)
    sums[which] += fold(grad * unit)
    sums[which + 1] += fold(grad)
    d_unit = grad * gain
    first = jnp.mean(d_unit, -1, keepdims=True)
    second = jnp.mean(d_unit * unit, -1, keepdims=True)
    return scale * (d_unit - first - unit * second)


class GradientShare:
    AHEAD = 8
    WINDOW = 6
    DEPTH = 6
    FINAL = 8

    def __init__(self, size, section, dp, core, decoder, a_fac, b_fac, tiles, w_up, w_down, w_cross, slope, resid, *share):
        (self.pair_got, self.acc, self.nb, self.pair_send, self.pair_recv, self.line_send, self.line_recv,
         self.cross_send, self.cross_recv, self.norm_send, self.norm_recv, self.final_sem,
         self.pair_credit, self.left_credit, self.right_credit, self.cross_credit) = share
        self.line = size // 2
        self.section, self.dp, self.core = section, dp, core
        self.decoder, self.encoder = decoder, jnp.logical_not(decoder)
        self.z, self.y = dp // 2, lax.rem(dp, 2)
        self.a_fac, self.b_fac, self.tiles = a_fac, b_fac, tiles
        self.w_up, self.w_down, self.w_cross, self.slope, self.resid = w_up, w_down, w_cross, slope, resid
        self.rows = a_fac.shape[2] // size
        self.own_chunks = b_fac.shape[0] - 4
        self.chunks = self.own_chunks + 2
        self.partner = (section, dp + 1 - 2 * self.y, core)
        self.right = (section, dp + 2, core)
        self.left = (section, dp - 2, core)
        self.across = (1 - section, dp, core)
        self.has_left, self.has_right = self.z > 0, self.z < self.line - 1

    def greet(self, barrier):
        pl.semaphore_signal(barrier, inc=1, device_id=self.partner, device_id_type=MESH)

        @pl.when(self.has_left)
        def _():
            pl.semaphore_signal(barrier, inc=1, device_id=self.left, device_id_type=MESH)

        @pl.when(self.has_right)
        def _():
            pl.semaphore_signal(barrier, inc=1, device_id=self.right, device_id_type=MESH)

        return 1 + jnp.where(self.has_left, 1, 0) + jnp.where(self.has_right, 1, 0)

    def tile_rows(self, k):
        return pl.ds(pl.multiple_of(k * self.rows, self.rows), self.rows)

    def cols(self, k):
        return pl.ds(pl.multiple_of(k * CHUNK, CHUNK), CHUNK)

    def pair_slot(self, i, k):
        return self.w_down.at[self.tile_rows(lax.rem(i, self.AHEAD)), self.cols(k)]

    def pair_copy(self, i, k):
        slot = lax.rem(i, self.AHEAD) * self.line + k
        return pltpu.make_async_remote_copy(
            src_ref=self.pair_slot(i, k),
            dst_ref=self.pair_got.at[slot],
            send_sem=self.pair_send.at[slot],
            recv_sem=self.pair_recv.at[slot],
            device_id=self.partner,
            device_id_type=MESH,
        )

    def line_slot(self, i, k):
        slot = lax.rem(i, self.DEPTH) * self.line + k
        return self.w_cross.at[slot // 8, self.tile_rows(lax.rem(slot, 8))]

    def line_place(self, side, i, k, z):
        return lax.rem(i, self.WINDOW) * (self.line + 1) + (self.line - z + k if side else k - z)

    def line_got(self, place):
        return self.w_up.at[self.tile_rows(place // 4), self.cols(lax.rem(place, 4))]

    def line_copy(self, side, i, k, receiver):
        place = self.line_place(side, i, k, receiver)
        return pltpu.make_async_remote_copy(
            src_ref=self.line_slot(i, k),
            dst_ref=self.line_got(place),
            send_sem=self.line_send.at[lax.rem(i, self.DEPTH) * self.line + k],
            recv_sem=self.line_recv.at[place],
            device_id=self.left if side else self.right,
            device_id_type=MESH,
        )

    def cross_copy(self, q):
        return pltpu.make_async_remote_copy(
            src_ref=self.slope.at[q],
            dst_ref=self.slope.at[q],
            send_sem=self.cross_send.at[q],
            recv_sem=self.cross_recv.at[q],
            device_id=self.across,
            device_id_type=MESH,
        )

    def own_tile(self, i, k, y):
        main = i < self.own_chunks

        @pl.when(main)
        def _():
            left = jnp.minimum(i // 4, 2) + jnp.where(i > 8, 1, 0)
            shard = k * 2 + y
            self.acc[...] = dot_tn(self.a_fac[left, :, self.tile_rows(shard)], self.b_fac[i])

        first = (i - self.own_chunks) * 2
        small = self.rows // 2

        @pl.when(jnp.logical_not(main) & self.decoder)
        def _():
            base = self.a_fac.shape[2] // 2
            for e in range(2):
                q = first + e
                block = dot_tn(
                    self.a_fac[4 + (q + 1) // 2, :, pl.ds(pl.multiple_of(base + k * self.rows, self.rows), self.rows)],
                    self.b_fac[self.own_chunks + q],
                )
                self.acc[e * small : (e + 1) * small] = jnp.where(y == 0, block[:small], block[small:])

        @pl.when(jnp.logical_not(main) & self.encoder)
        def _():
            for e in range(2):
                place = pl.ds(pl.multiple_of(k * self.rows + y * small, small), small)
                self.acc[e * small : (e + 1) * small] = self.slope[first + e, place].astype(F32)

    def pair_step(self, i):
        @pl.when(i >= self.AHEAD)
        def _():
            pl.semaphore_wait(self.pair_credit, 1)

        @pl.when((i >= self.own_chunks) & self.encoder)
        def _():
            for e in range(2):
                self.cross_copy((i - self.own_chunks) * 2 + e).wait_recv()

        def one(k):
            @pl.when(i >= self.AHEAD)
            def _():
                self.pair_copy(i, k).wait_send()

            self.own_tile(i, k, 1 - self.y)
            slot = self.pair_slot(i, k)
            slot[...] = self.acc[...].astype(BF)
            self.pair_copy(i, k).start()

        loop(self.line, one)

    def begin(self):
        @pl.when(self.has_left)
        def _():
            pl.semaphore_signal(self.right_credit, inc=self.WINDOW, device_id=self.left, device_id_type=MESH)

        @pl.when(self.has_right)
        def _():
            pl.semaphore_signal(self.left_credit, inc=self.WINDOW, device_id=self.right, device_id_type=MESH)

        @pl.when(self.encoder)
        def _():
            pl.semaphore_signal(self.cross_credit, inc=1, device_id=self.across, device_id_type=MESH)

        loop(self.AHEAD, self.pair_step)

    def line_step(self, t):
        last = self.line - 1
        self.within(t - self.z, self.has_right, self.to_right)
        self.within(t - (last - self.z), self.has_left, self.to_left)
        self.within(t - last, True, self.finish)

    def within(self, i, more, body):
        @pl.when((i >= 0) & (i < self.chunks) & more)
        def _():
            body(i)

    def partial(self, i, k):
        self.own_tile(i, k, self.y)
        self.pair_copy(i, k).wait_recv()
        self.acc[...] += self.pair_got[lax.rem(i, self.AHEAD) * self.line + k].astype(F32)

    def arrived(self, side, i, k):
        self.line_copy(side, i, k, self.z).wait_recv()
        self.acc[...] += self.line_got(self.line_place(side, i, k, self.z))[...].astype(F32)

    def send(self, side, i, k, inner):
        receiver = self.z - 1 if side else self.z + 1

        @pl.when(i >= self.DEPTH)
        def _():
            self.line_copy(side, i, k, receiver).wait_send()

        self.partial(i, k)

        @pl.when(inner)
        def _():
            self.arrived(side, i, k)

        slot = self.line_slot(i, k)
        slot[...] = self.acc[...].astype(BF)
        self.line_copy(side, i, k, receiver).start()

    def to_right(self, i):
        pl.semaphore_wait(self.right_credit, 1)

        def one(j):
            k = self.line - 1 - j

            @pl.when(k > self.z)
            def _():
                self.send(0, i, k, self.has_left)

        loop(self.line - 1, one)

    def to_left(self, i):
        pl.semaphore_wait(self.left_credit, 1)

        def one(k):
            @pl.when(k < self.z)
            def _():
                self.send(1, i, k, self.has_right)

        loop(self.line - 1, one)

    def finish(self, i):
        self.partial(i, self.z)

        @pl.when(self.has_left)
        def _():
            self.arrived(0, i, self.z)

        @pl.when(self.has_right)
        def _():
            self.arrived(1, i, self.z)

        @pl.when(i >= self.FINAL)
        def _():
            self.final_copy(i).wait()

        slot = self.final_slot(i)
        slot[...] = self.acc[...]
        self.final_copy(i).start()

        @pl.when(i + self.WINDOW < self.chunks)
        def _():
            @pl.when(self.has_left)
            def _():
                pl.semaphore_signal(self.right_credit, inc=1, device_id=self.left, device_id_type=MESH)

            @pl.when(self.has_right)
            def _():
                pl.semaphore_signal(self.left_credit, inc=1, device_id=self.right, device_id_type=MESH)

        @pl.when(i + self.AHEAD < self.chunks)
        def _():
            pl.semaphore_signal(self.pair_credit, inc=1, device_id=self.partner, device_id_type=MESH)
            self.pair_step(i + self.AHEAD)

    def final_slot(self, i):
        slot = lax.rem(i, self.FINAL)
        return self.resid.at[self.tile_rows(slot // 2), self.cols(lax.rem(slot, 2))]

    def final_copy(self, i):
        return pltpu.make_async_copy(
            self.final_slot(i), self.tiles.at[i], self.final_sem.at[lax.rem(i, self.FINAL)]
        )

    def cross_part(self):
        @pl.when(self.decoder)
        def _():
            pl.semaphore_wait(self.cross_credit, 1)

            def one(q):
                def tile(k):
                    self.slope[q, self.tile_rows(k)] = dot_tn(
                        self.a_fac[4 + (q + 1) // 2, :, self.tile_rows(k)],
                        self.b_fac[self.own_chunks + q],
                    ).astype(BF)

                loop(4, tile)
                self.cross_copy(q).start()

            loop(4, one)

    def norm_copy(self, src, dst, device):
        return pltpu.make_async_remote_copy(
            src_ref=self.nb.at[src],
            dst_ref=self.nb.at[dst],
            send_sem=self.norm_send.at[dst],
            recv_sem=self.norm_recv.at[dst],
            device_id=device,
            device_id_type=MESH,
        )

    def norms(self, sums, norm_out, norm3_out):
        nb, has_left, has_right = self.nb, self.has_left, self.has_right
        for i in range(6):
            nb[0, i : i + 1] = jnp.sum(sums[i], 0, keepdims=True)
        nb[0, 6:8] = jnp.zeros_like(nb[0, 6:8])
        to_right = self.norm_copy(3, 1, self.right)
        to_left = self.norm_copy(4, 2, self.left)
        nb[3] = nb[0]
        nb[4] = nb[0]
        nb[5] = nb[0]

        @pl.when(jnp.logical_not(has_left))
        def _():
            to_right.start()

        @pl.when(jnp.logical_not(has_right))
        def _():
            to_left.start()

        @pl.when(has_left)
        def _():
            to_right.wait_recv()
            nb[5] += nb[1]

            @pl.when(has_right)
            def _():
                nb[3] += nb[1]
                to_right.start()

        @pl.when(has_right)
        def _():
            to_left.wait_recv()
            nb[5] += nb[2]

            @pl.when(has_left)
            def _():
                nb[4] += nb[2]
                to_left.start()

        self.norm_copy(5, 6, self.partner).start()
        self.norm_out, self.norm3_out = norm_out, norm3_out

    def finish_norms(self):
        nb = self.nb
        self.norm_copy(5, 6, self.partner).wait()

        @pl.when(self.has_right)
        def _():
            self.norm_copy(3, 1, self.right).wait_send()

        @pl.when(self.has_left)
        def _():
            self.norm_copy(4, 2, self.left).wait_send()

        nb[7] = nb[5] + nb[6]
        hand = self.norm_copy(7, 8, self.across)

        @pl.when(self.decoder)
        def _():
            hand.start()
            nb[8] = nb[7]

        self.norm_out[...] = nb[7, :, pl.ds(pl.multiple_of(self.dp * 128, 128), 128)]

        @pl.when(self.encoder)
        def _():
            hand.wait_recv()

        place = self.section * self.line * 2 + self.dp
        block = nb[8, :, pl.ds(pl.multiple_of(place // 2 * 128, 128), 128)]
        self.norm3_out[...] = jnp.where(self.y == 0, block, pltpu.roll(block, 64, 1))

        @pl.when(self.decoder)
        def _():
            hand.wait_send()

    def run(self):
        loop(self.chunks, self.line_step)
        self.finish_norms()
        loop(self.line - 1, lambda p: self.line_step(self.chunks + p))

    def drain(self):
        for slot in range(self.AHEAD):
            for k in range(self.line):
                self.pair_copy(slot, k).wait_send()

        for slot in range(self.DEPTH):
            for k in range(self.line):

                @pl.when(self.z != k)
                def _():
                    self.line_copy(0, slot, k, 0).wait_send()

        for slot in range(self.FINAL):
            self.final_copy(slot).wait()

        @pl.when(self.decoder)
        def _():
            for q in range(4):
                self.cross_copy(q).wait_send()


def layer_kernel(
    sections,
    ring,
    inputs,
    targets,
    cotangent,
    counts,
    qkv_hbm,
    out_hbm,
    gain1,
    bias1,
    up_hbm,
    down_hbm,
    gain2,
    bias2,
    cross_hbm,
    cross_out_hbm,
    gain3,
    bias3,
    seg_out,
    in_grad,
    norm_out,
    first_out,
    second_out,
    w_qkv,
    w_out,
    w_up,
    w_down,
    w_cross,
    w_cross_out,
    a_fac,
    b_fac,
    proj,
    cross_proj,
    unit1,
    unit2,
    unit3,
    scale1,
    scale2,
    scale3,
    resid,
    slope,
    d_out,
    d_mix,
    sent,
    got,
    half_send,
    half_own,
    half_got,
    sums,
    load_sem,
    x_sem,
    ex_send,
    ex_recv,
    hop_send,
    hop_recv,
    out_sem,
    *share,
):
    section = lax.axis_index("section")
    dp = lax.axis_index("dp")
    core = lax.axis_index("mp")
    decoder = section == sections - 1
    encoder = section != sections - 1
    mate = (section, dp, 1 - core)
    across = (1 - section, dp, core)
    half = seg_out.shape[2]
    slot = 2 * half
    limit = jnp.where(decoder, 0, slot)
    width = w_up.shape[1]
    parts = width // CHUNK
    own = core * half
    other = (1 - core) * half

    d_branch, crossed, d_attn, layer_in, normed_low, memory, d_cross = (a_fac.at[i] for i in range(7))
    act = b_fac.at[0:parts]
    d_hidden = b_fac.at[parts : 2 * parts]
    mixed = b_fac.at[2 * parts]
    d_proj = b_fac.at[2 * parts + 1 : 2 * parts + 4]
    d_cross_proj = b_fac.at[2 * parts + 4 : 2 * parts + 7]
    cross_mixed = b_fac.at[2 * parts + 7]

    def rows_of(m):
        return pl.ds(pl.multiple_of(m * slot, slot), slot)

    def half_of(m, offset):
        return pl.ds(pl.multiple_of(m * slot + offset, half), half)

    def strip_of(m, k):
        return pl.ds(pl.multiple_of(m * slot + k * STRIP, STRIP), STRIP)

    def lanes_of(j):
        return pl.ds(pl.multiple_of(j * PAIR, PAIR), PAIR)

    barrier = pltpu.get_barrier_semaphore()
    for device in (mate, across):
        pl.semaphore_signal(barrier, inc=1, device_id=device, device_id_type=MESH)
    if ring:
        total = GradientShare(ring, section, dp, core, decoder, a_fac, b_fac, first_out, w_up, w_down, w_cross, slope, resid, *share)
        greeted = 2 + total.greet(barrier)
    else:
        greeted = 2

    loads = [
        pltpu.make_async_copy(src, dst, load_sem.at[i])
        for i, (src, dst) in enumerate(
            (
                (qkv_hbm.at[0], w_qkv),
                (out_hbm.at[0], w_out),
                (up_hbm.at[0], w_up),
                (down_hbm.at[0], w_down),
                (cross_hbm, w_cross),
                (cross_out_hbm, w_cross_out),
            )
        )
    ]

    def local_rows(src, dst, m, sem):
        return pltpu.make_async_copy(src.at[m], dst.at[half_of(m, own)], sem)

    def mate_rows(src, dst, m, send, recv):
        return pltpu.make_async_remote_copy(
            src_ref=src.at[m],
            dst_ref=dst.at[half_of(m, own)],
            send_sem=send,
            recv_sem=recv,
            device_id=mate,
            device_id_type=MESH,
        )

    def start_rows(src, dst, base):
        for m in range(2):
            local_rows(src, dst, m, x_sem.at[base + m]).start()
        for m in range(2):
            mate_rows(src, dst, m, x_sem.at[base + 2 + m], x_sem.at[base + 4 + m]).start()

    def wait_rows(src, dst, base, m):
        local_rows(src, dst, m, x_sem.at[base + m]).wait()
        mate_rows(src, dst, m, x_sem.at[base + 2 + m], x_sem.at[base + 4 + m]).wait()

    @pl.when(encoder)
    def _():
        for m in range(2):
            local_rows(inputs, layer_in, m, x_sem.at[m]).start()

    @pl.when(decoder)
    def _():
        for m in range(2):
            local_rows(targets, layer_in, m, x_sem.at[m]).start()

    loads[0].start()
    loads[1].start()
    pl.semaphore_wait(barrier, greeted)

    def mate_start(src, dst, base):
        for m in range(2):
            mate_rows(src, dst, m, x_sem.at[base + 2 + m], x_sem.at[base + 4 + m]).start()

    @pl.when(encoder)
    def _():
        mate_start(inputs, layer_in, 0)

    @pl.when(decoder)
    def _():
        mate_start(targets, layer_in, 0)

    for copy in loads[2:]:
        copy.start()

    @pl.when(decoder)
    def _():
        start_rows(cotangent, d_out, 6)

    sums[...] = jnp.zeros_like(sums)

    def exchange(which, buffer, m):
        return pltpu.make_async_remote_copy(
            src_ref=sent.at[rows_of(m)],
            dst_ref=got.at[buffer, rows_of(m)],
            send_sem=ex_send.at[which, m],
            recv_sem=ex_recv.at[which, m],
            device_id=mate,
            device_id_type=MESH,
        )

    def half_exchange(which, m):
        return pltpu.make_async_remote_copy(
            src_ref=half_send.at[which, m],
            dst_ref=half_got.at[which, m],
            send_sem=hop_send.at[4 + which, m],
            recv_sem=hop_recv.at[4 + which, m],
            device_id=mate,
            device_id_type=MESH,
        )

    def across_copy(src, dst, which, m):
        return pltpu.make_async_remote_copy(
            src_ref=src,
            dst_ref=dst.at[half_of(m, own)],
            send_sem=hop_send.at[which, m],
            recv_sem=hop_recv.at[which, m],
            device_id=across,
            device_id_type=MESH,
        )

    def forward_copy(ref, which, m):
        return pltpu.make_async_remote_copy(
            src_ref=ref.at[half_of(m, own)],
            dst_ref=ref.at[half_of(m, own)],
            send_sem=hop_send.at[which, m],
            recv_sem=hop_recv.at[which, m],
            device_id=mate,
            device_id_type=MESH,
        )

    def project_out(value, weight, m):
        for n in range(sent.shape[1] // CHUNK):
            cols = slice(n * CHUNK, (n + 1) * CHUNK)
            sent[rows_of(m), cols] = dot_nt(value, weight[cols, :]).astype(BF)

    def summed(buffer, strip):
        return sent[strip].astype(F32) + got[buffer, strip].astype(F32)

    loads[0].wait()

    def attention_in(m):
        @pl.when(encoder)
        def _():
            wait_rows(inputs, layer_in, 0, m)

        @pl.when(decoder)
        def _():
            wait_rows(targets, layer_in, 0, m)

        rows = rows_of(m)
        for t in range(3):
            proj[t, rows] = dot_nn(layer_in[rows], w_qkv[t]).astype(BF)
        loop(CHUNK // PAIR, lambda j: attend_forward(proj, mixed, rows, lanes_of(j), limit))
        project_out(mixed[rows], w_out, m)
        exchange(0, 0, m).start()

    loads[1].wait()
    loop(2, attention_in)
    for copy in loads[2:]:
        copy.wait()

    def after_attention(m):
        exchange(0, 0, m).wait()

        def norm(k):
            strip = strip_of(m, k)
            unit, scale, value = norm_forward(
                layer_in[strip].astype(F32) + summed(0, strip), gain1[...], bias1[...]
            )
            unit1[strip] = unit.astype(BF)
            scale1[strip] = scale
            resid[strip] = value
            normed_low[strip] = value.astype(BF)
            crossed[strip] = value.astype(BF)

        loop(slot // STRIP, norm)

        @pl.when(decoder)
        def _():
            rows = rows_of(m)
            cross_proj[0, rows] = dot_nn(normed_low[rows], w_cross[0]).astype(BF)
            across_copy(seg_out.at[0, m], memory, 0, m).wait_recv()
            forward_copy(memory, 1, m).start()
            forward_copy(memory, 1, m).wait()
            for t in range(1, 3):
                cross_proj[t, rows] = dot_nn(memory[rows], w_cross[t]).astype(BF)
            loop(
                CHUNK // PAIR,
                lambda j: attend_forward(cross_proj, cross_mixed, rows, lanes_of(j), None),
            )
            project_out(cross_mixed[rows], w_cross_out, m)
            exchange(1, 1, m).start()

    loop(2, after_attention)

    def feed_forward(m):
        rows = rows_of(m)

        @pl.when(decoder)
        def _():
            exchange(1, 1, m).wait()

            def norm(k):
                strip = strip_of(m, k)
                unit, scale, value = norm_forward(
                    resid[strip] + summed(1, strip), gain3[...], bias3[...]
                )
                unit3[strip] = unit.astype(BF)
                scale3[strip] = scale
                resid[strip] = value
                crossed[strip] = value.astype(BF)

            loop(slot // STRIP, norm)

        for n in range(parts):
            pre = dot_nn(crossed[rows], w_up[:, n * CHUNK : (n + 1) * CHUNK])
            rise = 0.5 + 0.5 * lax.erf(pre * (0.5**0.5))
            act[n, rows] = (pre * rise).astype(BF)
            slope[n, rows] = (rise + pre * jnp.exp(-0.5 * pre * pre) * 0.3989422804014327).astype(BF)
        project_out(jnp.concatenate([act[n, rows] for n in range(parts)], 1), w_down, m)
        exchange(2, 2, m).start()

    loop(2, feed_forward)

    def finish_forward(m):
        exchange(2, 2, m).wait()

        def norm(k):
            strip = strip_of(m, k)
            unit, scale, value = norm_forward(
                resid[strip] + summed(2, strip), gain2[...], bias2[...]
            )
            unit2[strip] = unit.astype(BF)
            scale2[strip] = scale
            place = k * STRIP - own

            @pl.when((place >= 0) & (place < half))
            def _():
                seg_out[0, m, pl.ds(pl.multiple_of(lax.rem(k * STRIP, half), STRIP), STRIP)] = (
                    value.astype(BF)
                )

        loop(slot // STRIP, norm)

        @pl.when(encoder)
        def _():
            across_copy(seg_out.at[0, m], memory, 0, m).start()

    loop(2, finish_forward)

    question = dp // QSLOTS
    spot = dp - question * QSLOTS

    def feed_backward(m):
        rows = rows_of(m)

        @pl.when(encoder)
        def _():
            across_copy(half_send.at[0, m], d_out, 2, m).wait_recv()
            forward_copy(d_out, 3, m).start()
            forward_copy(d_out, 3, m).wait()

        @pl.when(decoder)
        def _():
            wait_rows(cotangent, d_out, 6, m)

        keep = jnp.where(spot < counts[m, question], 1.0, 0.0)
        keep = jnp.where(decoder, keep, 1.0)

        def norm(k):
            strip = strip_of(m, k)
            grad = norm_backward(
                d_out[strip].astype(F32) * keep,
                unit2[strip].astype(F32),
                scale2[strip],
                gain2[...],
                sums,
                2,
            )
            resid[strip] = grad
            d_branch[strip] = grad.astype(BF)

        loop(slot // STRIP, norm)
        for n in range(parts):
            grad = dot_nn(d_branch[rows], w_down[:, n * CHUNK : (n + 1) * CHUNK])
            d_hidden[n, rows] = (grad * slope[n, rows].astype(F32)).astype(BF)
        project_out(jnp.concatenate([d_hidden[n, rows] for n in range(parts)], 1), w_up, m)
        exchange(3, 0, m).start()

    loop(2, feed_backward)
    if ring:
        total.begin()

    def cross_backward(m):
        rows = rows_of(m)

        def norm(k):
            strip = strip_of(m, k)
            grad = norm_backward(
                resid[strip] + summed(0, strip),
                unit3[strip].astype(F32),
                scale3[strip],
                gain3[...],
                sums,
                4,
            )
            resid[strip] = grad
            d_cross[strip] = grad.astype(BF)

        loop(slot // STRIP, norm)
        d_mix[rows] = dot_nn(d_cross[rows], w_cross_out[...]).astype(BF)
        loop(
            CHUNK // PAIR,
            lambda j: attend_backward(cross_proj, d_mix, d_cross_proj, rows, lanes_of(j), None),
        )

        def memory_part(offset):
            piece = half_of(m, offset)
            return jnp.concatenate([d_cross_proj[1, piece], d_cross_proj[2, piece]], 1)

        def memory_weight(n):
            cols = slice(n * CHUNK, (n + 1) * CHUNK)
            return jnp.concatenate([w_cross[1, cols], w_cross[2, cols]], 1)

        for n in range(sent.shape[1] // CHUNK):
            cols = slice(n * CHUNK, (n + 1) * CHUNK)
            half_send[0, m, :, cols] = dot_nt(memory_part(other), memory_weight(n)).astype(BF)
        half_exchange(0, m).start()
        for n in range(sent.shape[1] // CHUNK):
            cols = slice(n * CHUNK, (n + 1) * CHUNK)
            half_own[m, :, cols] = dot_nt(memory_part(own), memory_weight(n))
        project_out(d_cross_proj[0, rows], w_cross[0], m)
        exchange(4, 1, m).start()
        half_exchange(0, m).wait()
        half_send[0, m] = (half_own[m] + half_got[0, m].astype(F32)).astype(BF)
        across_copy(half_send.at[0, m], d_out, 2, m).start()

    def attention_back(m):
        rows = rows_of(m)

        def norm_rows(buffer):
            def norm(k):
                strip = strip_of(m, k)
                grad = norm_backward(
                    resid[strip] + summed(buffer, strip),
                    unit1[strip].astype(F32),
                    scale1[strip],
                    gain1[...],
                    sums,
                    0,
                )
                resid[strip] = grad
                d_attn[strip] = grad.astype(BF)

            loop(slot // STRIP, norm)

        @pl.when(decoder)
        def _():
            exchange(4, 1, m).wait()

        @pl.when(encoder)
        def _():
            exchange(3, 0, m).wait()

        norm_rows(jnp.where(decoder, 1, 0))
        d_mix[rows] = dot_nn(d_attn[rows], w_out[...]).astype(BF)
        loop(
            CHUNK // PAIR, lambda j: attend_backward(proj, d_mix, d_proj, rows, lanes_of(j), limit)
        )

        def input_part(offset):
            piece = half_of(m, offset)
            return jnp.concatenate([d_proj[t, piece] for t in range(3)], 1)

        def input_weight(n):
            cols = slice(n * CHUNK, (n + 1) * CHUNK)
            return jnp.concatenate([w_qkv[t, cols] for t in range(3)], 1)

        for n in range(sent.shape[1] // CHUNK):
            cols = slice(n * CHUNK, (n + 1) * CHUNK)
            half_send[1, m, :, cols] = dot_nt(input_part(other), input_weight(n)).astype(BF)
        half_exchange(1, m).start()
        for n in range(sent.shape[1] // CHUNK):
            cols = slice(n * CHUNK, (n + 1) * CHUNK)
            half_own[m, :, cols] = dot_nt(input_part(own), input_weight(n))

    @pl.when(decoder)
    def _():
        def both(m):
            exchange(3, 0, m).wait()
            cross_backward(m)

        loop(2, both)

    loop(2, attention_back)

    def finish_backward(m):
        half_exchange(1, m).wait()
        in_grad[0, m] = (
            resid[half_of(m, own)] + half_own[m] + half_got[1, m].astype(F32)
        ).astype(BF)

    loop(2, finish_backward)

    @pl.when(encoder)
    def _():
        for m in range(2):
            across_copy(seg_out.at[0, m], memory, 0, m).wait_send()

    @pl.when(decoder)
    def _():
        for m in range(2):
            across_copy(half_send.at[0, m], d_out, 2, m).wait_send()

    if ring:
        total.norms(sums, norm_out, second_out)
        total.cross_part()
        total.run()
        total.drain()
        return

    for i in range(6):
        norm_out[i : i + 1] = jnp.sum(sums[i], 0, keepdims=True)
    norm_out[6:8] = jnp.zeros_like(norm_out[6:8])
    copies = [
        pltpu.make_async_copy(a_fac, first_out, out_sem.at[0]),
        pltpu.make_async_copy(b_fac, second_out, out_sem.at[1]),
    ]
    for copy in copies:
        copy.start()
    for copy in copies:
        copy.wait()


def body(
    sections,
    ring,
    inputs,
    target_inputs,
    cotangent,
    slot_counts,
    w_qkv,
    w_out,
    norm1_gain,
    norm1_bias,
    w_up,
    w_down,
    norm2_gain,
    norm2_bias,
    cross_qkv,
    cross_out,
    norm3_gain,
    norm3_bias,
):
    micro, half, depth = inputs.shape
    rows = micro * 2 * half
    heads = w_out.shape[2]
    width = w_up.shape[2]
    parts = width // CHUNK
    chunks = 2 * parts + 8
    hbm = pl.BlockSpec(memory_space=pl.ANY)
    vmem = pl.BlockSpec(memory_space=VM)
    smem = pl.BlockSpec(memory_space=pltpu.SMEM)
    shape = jax.ShapeDtypeStruct
    if ring:
        results = (
            shape((8, depth // ring), F32),
            shape((chunks - 2, depth // ring, CHUNK), F32),
            shape((8, depth // ring), F32),
        )
        places = (vmem, hbm, vmem)
    else:
        results = (
            shape((8, depth), F32),
            shape((7, rows, depth), BF),
            shape((chunks, rows, CHUNK), BF),
        )
        places = (vmem, hbm, hbm)
    dma = pltpu.SemaphoreType.DMA
    regular = pltpu.SemaphoreType.REGULAR
    tile = (depth // ring, CHUNK) if ring else None
    share = (
        [
            VM((GradientShare.AHEAD * 4,) + tile, BF),
            VM(tile, F32),
            VM((9, 8, depth), F32),
            dma((GradientShare.AHEAD * 4,)),
            dma((GradientShare.AHEAD * 4,)),
            dma((GradientShare.DEPTH * 4,)),
            dma((GradientShare.WINDOW * 5,)),
            dma((4,)),
            dma((4,)),
            dma((9,)),
            dma((9,)),
            dma((GradientShare.FINAL,)),
            regular,
            regular,
            regular,
            regular,
        ]
        if ring
        else []
    )
    seg_out, in_grad, norms, first, second = pl.pallas_call(
        functools.partial(layer_kernel, sections, ring),
        out_shape=(
            shape((1, micro, half, depth), BF),
            shape((1, micro, half, depth), BF),
        )
        + results,
        in_specs=[hbm, hbm, hbm, smem, hbm, hbm, vmem, vmem, hbm, hbm, vmem, vmem, hbm, hbm, vmem, vmem],
        out_specs=(vmem, vmem) + places,
        scratch_shapes=[
            VM((3, depth, heads), BF),
            VM((depth, heads), BF),
            VM((depth, width), BF),
            VM((depth, width), BF),
            VM((3, depth, heads), BF),
            VM((depth, heads), BF),
            VM((7, rows, depth), BF),
            VM((chunks, rows, CHUNK), BF),
            VM((3, rows, heads), BF),
            VM((3, rows, heads), BF),
            VM((rows, depth), BF),
            VM((rows, depth), BF),
            VM((rows, depth), BF),
            VM((rows, 1), F32),
            VM((rows, 1), F32),
            VM((rows, 1), F32),
            VM((rows, depth), F32),
            VM((parts, rows, CHUNK), BF),
            VM((rows, depth), BF),
            VM((rows, heads), BF),
            VM((rows, depth), BF),
            VM((3, rows, depth), BF),
            VM((2, micro, half, depth), BF),
            VM((micro, half, depth), F32),
            VM((2, micro, half, depth), BF),
            VM((6, 8, depth), F32),
            pltpu.SemaphoreType.DMA((6,)),
            pltpu.SemaphoreType.DMA((12,)),
            pltpu.SemaphoreType.DMA((5, micro)),
            pltpu.SemaphoreType.DMA((5, micro)),
            pltpu.SemaphoreType.DMA((6, micro)),
            pltpu.SemaphoreType.DMA((6, micro)),
            pltpu.SemaphoreType.DMA((2,)),
        ]
        + share,
        compiler_params=pltpu.CompilerParams(
            collective_id=0, has_side_effects=True, vmem_limit_bytes=60 * 2**20
        ),
        name="layers",
    )(
        inputs,
        target_inputs,
        cotangent,
        slot_counts,
        w_qkv,
        w_out,
        norm1_gain,
        norm1_bias,
        w_up,
        w_down,
        norm2_gain,
        norm2_bias,
        cross_qkv,
        cross_out,
        norm3_gain[None],
        norm3_bias[None],
    )
    if ring:
        own = lambda first_one, count: jnp.swapaxes(
            first[first_one : first_one + count], 0, 1
        ).reshape(1, depth // ring, count * CHUNK)
        cross = first[2 * parts + 4 :].reshape(4, depth // ring // 2, CHUNK)
        lanes = depth // ring // 2
        return (
            seg_out,
            in_grad,
            first[None, 2 * parts + 1 : 2 * parts + 4],
            first[2 * parts : 2 * parts + 1],
            norms[0:1],
            norms[1:2],
            own(parts, parts),
            own(0, parts),
            norms[2:3],
            norms[3:4],
            cross[:3],
            cross[3],
            second[4, :lanes],
            second[5, :lanes],
        )
    a_fac, b_fac = first, second
    decoder = lax.axis_index("section") == sections - 1

    def weight_grad(left, first, count):
        return jnp.einsum(
            "nd,tnc->tdc", a_fac[left], b_fac[first : first + count], preferred_element_type=F32
        ).astype(BF)

    def shared(grad, axes, dim):
        return lax.psum_scatter(grad, axes, scatter_dimension=dim, tiled=True)

    def wide(grad):
        return jnp.swapaxes(grad, 0, 1).reshape(depth, -1)

    grad_down = shared(wide(weight_grad(0, 0, parts)), "dp", 0)
    grad_up = shared(wide(weight_grad(1, parts, parts)), "dp", 0)
    grad_out = shared(weight_grad(2, 2 * parts, 1)[0], "dp", 0)
    grad_qkv = shared(weight_grad(3, 2 * parts + 1, 3), "dp", 1)
    cross = jnp.concatenate(
        [
            weight_grad(4, 2 * parts + 4, 1),
            weight_grad(5, 2 * parts + 5, 2),
            weight_grad(6, 2 * parts + 7, 1),
        ],
        0,
    )
    cross = shared(jnp.where(decoder, cross, jnp.zeros_like(cross)), ("section", "dp"), 1)
    small = shared(norms[:4], "dp", 1)
    norm3 = jnp.where(decoder, norms[4:6], jnp.zeros_like(norms[4:6]))
    norm3 = shared(norm3, ("section", "dp"), 1)
    return (
        seg_out,
        in_grad,
        grad_qkv[None].astype(F32),
        grad_out[None].astype(F32),
        small[0:1],
        small[1:2],
        grad_up[None].astype(F32),
        grad_down[None].astype(F32),
        small[2:3],
        small[3:4],
        cross[:3].astype(F32),
        cross[3].astype(F32),
        norm3[0],
        norm3[1],
    )


def solution(mesh):
    ring = 8 if mesh.shape["dp"] == 8 else 0
    return jax.shard_map(
        functools.partial(body, mesh.shape["section"], ring),
        mesh=mesh,
        in_specs=(
            P(None, ("dp", "mp"), None),
            P(None, ("dp", "mp"), None),
            P(None, ("dp", "mp"), None),
            P(),
            P("section", None, None, "mp"),
            P("section", None, "mp"),
            P("section", None),
            P("section", None),
            P("section", None, "mp"),
            P("section", None, "mp"),
            P("section", None),
            P("section", None),
            P(None, None, "mp"),
            P(None, "mp"),
            P(),
            P(),
        ),
        out_specs=(
            P("section", None, ("dp", "mp"), None),
            P("section", None, ("dp", "mp"), None),
            P("section", None, "dp", "mp"),
            P("section", "dp", "mp"),
            P("section", "dp"),
            P("section", "dp"),
            P("section", "dp", "mp"),
            P("section", "dp", "mp"),
            P("section", "dp"),
            P("section", "dp"),
            P(None, ("section", "dp"), "mp"),
            P(("section", "dp"), "mp"),
            P(("section", "dp")),
            P(("section", "dp")),
        ),
        check_vma=False,
    )
```

```python
import functools

import jax
import jax.numpy as jnp
from jax import lax
from jax.experimental import pallas as pl
from jax.experimental.pallas import tpu as pltpu
from jax.sharding import PartitionSpec as P

HEAD = 64
SLOT = 256
QSLOTS = 4
CHUNK = 512
PAIR = 2 * HEAD
STRIP = 64
EPS = 1e-5
NEG = -1000000000.0
MESH = pl.DeviceIdType.MESH
BF = jnp.bfloat16
F32 = jnp.float32
VM = pltpu.VMEM


def dot_nn(a, b):
    return lax.dot_general(a, b, (((1,), (0,)), ((), ())), preferred_element_type=F32)


def dot_nt(a, b):
    return lax.dot_general(a, b, (((1,), (1,)), ((), ())), preferred_element_type=F32)


def dot_tn(a, b):
    return lax.dot_general(a, b, (((0,), (0,)), ((), ())), preferred_element_type=F32)


def loop(count, body):
    def step(i, carry):
        body(i)
        return carry

    lax.fori_loop(0, count, step, 0)


def head_masks():
    lane = lax.broadcasted_iota(jnp.int32, (1, PAIR), 1)
    first = jnp.where(lane < HEAD, 1.0, 0.0).astype(BF)
    second = jnp.where(lane < HEAD, 0.0, 1.0).astype(BF)
    return first, second


def expos_of(query, keys, mask, limit):
    scores = dot_nt(query * (mask * (HEAD**-0.5)).astype(BF), keys)
    if limit is not None:
        row = lax.broadcasted_iota(jnp.int32, scores.shape, 0)
        col = lax.broadcasted_iota(jnp.int32, scores.shape, 1)
        scores = jnp.where(row + limit >= col, scores, NEG)
    expo = jnp.exp(scores - jnp.max(scores, -1, keepdims=True))
    return expo, 1.0 / jnp.sum(expo, -1, keepdims=True)


def attend_forward(proj, mixed, rows, limit):
    masks = head_masks()
    for j in range(CHUNK // PAIR):
        lanes = slice(j * PAIR, (j + 1) * PAIR)
        query, keys, values = proj[0, rows, lanes], proj[1, rows, lanes], proj[2, rows, lanes]
        low = []
        for mask in masks:
            expo, share = expos_of(query, keys, mask, limit)
            low.append((expo * share).astype(BF))
        mixed[rows, lanes] = dot_nn(
            jnp.concatenate(low, 1), jnp.concatenate([values * mask for mask in masks], 0)
        ).astype(BF)


def attend_backward(proj, d_mixed, d_proj, rows, limit):
    masks = head_masks()
    scale = HEAD**-0.5
    for j in range(CHUNK // PAIR):
        lanes = slice(j * PAIR, (j + 1) * PAIR)
        query, keys, values = proj[0, rows, lanes], proj[1, rows, lanes], proj[2, rows, lanes]
        grad = d_mixed[rows, lanes]
        low, d_scores = [], []
        for mask in masks:
            expo, share = expos_of(query, keys, mask, limit)
            weights = expo * share
            d_weights = dot_nt(grad * mask, values)
            inner = jnp.sum(weights * d_weights, -1, keepdims=True)
            d_scores.append((weights * (d_weights - inner)).astype(BF))
            low.append(weights.astype(BF))
        d_proj[2, rows, lanes] = dot_tn(
            jnp.concatenate(low, 0), jnp.concatenate([grad * mask for mask in masks], 0)
        ).astype(BF)
        d_proj[0, rows, lanes] = (
            dot_nn(
                jnp.concatenate(d_scores, 1), jnp.concatenate([keys * mask for mask in masks], 0)
            )
            * scale
        ).astype(BF)
        d_proj[1, rows, lanes] = (
            dot_tn(
                jnp.concatenate(d_scores, 0), jnp.concatenate([query * mask for mask in masks], 0)
            )
            * scale
        ).astype(BF)


def norm_forward(value, gain, bias):
    center = value - jnp.mean(value, -1, keepdims=True)
    scale = lax.rsqrt(jnp.mean(center * center, -1, keepdims=True) + EPS)
    unit = center * scale
    return unit, scale, unit * gain + bias


def norm_backward(grad, unit, scale, gain, sums, which):
    fold = lambda v: jnp.sum(v.reshape(v.shape[0] // 8, 8, v.shape[1]), 0)
    sums[which] += fold(grad * unit)
    sums[which + 1] += fold(grad)
    d_unit = grad * gain
    first = jnp.mean(d_unit, -1, keepdims=True)
    second = jnp.mean(d_unit * unit, -1, keepdims=True)
    return scale * (d_unit - first - unit * second)


class GradientShare:
    AHEAD = 8
    WINDOW = 6
    DEPTH = 4
    FINAL = 8
    EARLY = 4

    def __init__(self, size, section, dp, core, decoder, a_fac, b_fac, tiles, w_up, w_down, held, slope, resid, *share):
        (self.pair_got, self.acc, self.nb, self.late_sent, self.late_got, self.late_acc, self.pair_send,
         self.pair_recv, self.line_send, self.line_recv, self.cross_send, self.cross_recv, self.norm_send,
         self.norm_recv, self.late_send, self.late_recv, self.factor_send, self.factor_recv, self.final_sem,
         self.pair_credit, self.left_credit, self.right_credit, self.cross_credit) = share
        self.line = size // 2
        self.section, self.dp, self.core = section, dp, core
        self.decoder, self.encoder = decoder, jnp.logical_not(decoder)
        self.z, self.y = dp // 2, lax.rem(dp, 2)
        self.a_fac, self.b_fac, self.tiles = a_fac, b_fac, tiles
        self.w_up, self.w_down, self.held, self.slope, self.resid = w_up, w_down, held, slope, resid
        self.rows = a_fac.shape[2] // size
        self.own_chunks = b_fac.shape[0] - 4
        self.positions = self.own_chunks + 2 + jnp.where(decoder, 2, 0)
        self.pairs = self.positions - self.EARLY
        self.partner = (section, dp + 1 - 2 * self.y, core)
        self.right = (section, dp + 2, core)
        self.left = (section, dp - 2, core)
        self.across = (1 - section, dp, core)
        self.mate = (section, dp, 1 - core)
        self.has_left, self.has_right = self.z > 0, self.z < self.line - 1

    def greet(self, barrier):
        pl.semaphore_signal(barrier, inc=1, device_id=self.partner, device_id_type=MESH)

        @pl.when(self.has_left)
        def _():
            pl.semaphore_signal(barrier, inc=1, device_id=self.left, device_id_type=MESH)

        @pl.when(self.has_right)
        def _():
            pl.semaphore_signal(barrier, inc=1, device_id=self.right, device_id_type=MESH)

        return 1 + jnp.where(self.has_left, 1, 0) + jnp.where(self.has_right, 1, 0)

    def remote(self, src, dst, send, recv, device):
        return pltpu.make_async_remote_copy(
            src_ref=src, dst_ref=dst, send_sem=send, recv_sem=recv, device_id=device, device_id_type=MESH
        )

    def tile_rows(self, k):
        return pl.ds(pl.multiple_of(k * self.rows, self.rows), self.rows)

    def cols(self, k):
        return pl.ds(pl.multiple_of(k * CHUNK, CHUNK), CHUNK)

    def pair_slot(self, j, k):
        return self.w_down.at[self.tile_rows(lax.rem(j, self.AHEAD)), self.cols(k)]

    def pair_copy(self, j, k):
        slot = lax.rem(j, self.AHEAD) * self.line + k
        return self.remote(
            self.pair_slot(j, k), self.pair_got.at[slot], self.pair_send.at[slot], self.pair_recv.at[slot], self.partner
        )

    def line_slot(self, p, k):
        slot = lax.rem(p, self.DEPTH) * self.line + k
        return self.held.at[slot // 8, self.tile_rows(lax.rem(slot, 4)), self.cols(lax.rem(slot // 4, 2))]

    def line_place(self, side, p, k, z):
        return lax.rem(p, self.WINDOW) * (self.line + 1) + (self.line - z + k if side else k - z)

    def line_got(self, place):
        return self.w_up.at[self.tile_rows(place // 4), self.cols(lax.rem(place, 4))]

    def line_copy(self, side, p, k, receiver):
        place = self.line_place(side, p, k, receiver)
        return self.remote(
            self.line_slot(p, k),
            self.line_got(place),
            self.line_send.at[lax.rem(p, self.DEPTH) * self.line + k],
            self.line_recv.at[place],
            self.left if side else self.right,
        )

    def cross_copy(self, q):
        return self.remote(
            self.slope.at[q], self.slope.at[q], self.cross_send.at[q], self.cross_recv.at[q], self.across
        )

    def late_copy(self, e):
        return self.remote(
            self.late_sent.at[e], self.late_got.at[e], self.late_send.at[e], self.late_recv.at[e], self.partner
        )

    def act_copy(self, n, m):
        rows = pl.ds(pl.multiple_of(m * SLOT, SLOT), SLOT)
        return self.remote(
            self.b_fac.at[n, rows],
            self.a_fac.at[5 + n // 2, rows, pl.ds(n % 2 * CHUNK, CHUNK)],
            self.factor_send.at[n * 2 + m],
            self.factor_recv.at[n * 2 + m],
            self.partner,
        )

    def branch_copy(self, k):
        rows = pl.ds(pl.multiple_of(self.core * SLOT, SLOT), SLOT)
        return self.remote(
            self.a_fac.at[0, rows, self.tile_rows(k * 2 + 1 - self.y)],
            self.a_fac.at[4, rows, pl.ds(k * self.rows, self.rows)],
            self.factor_send.at[8 + k],
            self.factor_recv.at[8 + k],
            self.partner,
        )

    def branch_forward(self):
        rows = pl.ds(pl.multiple_of(self.core * SLOT, SLOT), SLOT)
        part = self.a_fac.at[4, rows, pl.ds(0, CHUNK)]
        return self.remote(part, part, self.factor_send.at[12], self.factor_recv.at[12], self.mate)

    def send_act(self, m):
        @pl.when(self.encoder)
        def _():
            for n in range(4):
                self.act_copy(n, m).start()

    def send_branch(self, m):
        @pl.when(self.encoder & (self.core == m))
        def _():
            for k in range(4):
                self.branch_copy(k).start()

    def take_factors(self):
        for k in range(4):
            self.branch_copy(k).wait_recv()
        self.branch_forward().start()
        for m in range(2):
            for n in range(4):
                self.act_copy(n, m).wait()
        for k in range(4):
            self.branch_copy(k).wait_send()
        self.branch_forward().wait()

    def own_tile(self, i, k, y):
        main = i < self.own_chunks

        @pl.when(main)
        def _():
            left = jnp.minimum(i // 4, 2) + jnp.where(i > 8, 1, 0)
            shard = k * 2 + y
            self.acc[...] = dot_tn(self.a_fac[left, :, self.tile_rows(shard)], self.b_fac[i])

        @pl.when((i < 4) & self.encoder)
        def _():
            self.acc[...] += dot_tn(
                self.a_fac[4, :, self.tile_rows(k)], self.a_fac[5 + i // 2, :, self.cols(lax.rem(i, 2))]
            )

        first = (i - self.own_chunks) * 2
        small = self.rows // 2

        @pl.when(jnp.logical_not(main) & self.decoder)
        def _():
            base = self.a_fac.shape[2] // 2
            for e in range(2):
                q = first + e
                block = dot_tn(
                    self.a_fac[4 + (q + 1) // 2, :, pl.ds(pl.multiple_of(base + k * self.rows, self.rows), self.rows)],
                    self.b_fac[self.own_chunks + q],
                )
                self.acc[e * small : (e + 1) * small] = jnp.where(y == 0, block[:small], block[small:])

        @pl.when(jnp.logical_not(main) & self.encoder)
        def _():
            for e in range(2):
                place = pl.ds(pl.multiple_of(k * self.rows + y * small, small), small)
                self.acc[e * small : (e + 1) * small] = self.slope[first + e, place].astype(F32)

    def pair_step(self, j):
        i = j + jnp.where(self.decoder, 2, 4)

        @pl.when(j >= self.AHEAD)
        def _():
            pl.semaphore_wait(self.pair_credit, 1)

        @pl.when((i >= self.own_chunks) & self.encoder)
        def _():
            for e in range(2):
                self.cross_copy((i - self.own_chunks) * 2 + e).wait_recv()

        def one(k):
            @pl.when(j >= self.AHEAD)
            def _():
                self.pair_copy(j, k).wait_send()

            self.own_tile(i, k, 1 - self.y)
            slot = self.pair_slot(j, k)
            slot[...] = self.acc[...].astype(BF)
            self.pair_copy(j, k).start()

        loop(self.line, one)

    def begin(self):
        @pl.when(self.has_left)
        def _():
            pl.semaphore_signal(self.right_credit, inc=self.WINDOW, device_id=self.left, device_id_type=MESH)

        @pl.when(self.has_right)
        def _():
            pl.semaphore_signal(self.left_credit, inc=self.WINDOW, device_id=self.right, device_id_type=MESH)

        @pl.when(self.encoder)
        def _():
            pl.semaphore_signal(self.cross_credit, inc=1, device_id=self.across, device_id_type=MESH)

    def between(self, m):
        for e in range(2):
            self.pair_step(2 * m + e)
        self.line_step(m)

    def before(self, m):
        @pl.when(self.encoder & (m == 0))
        def _():
            self.take_factors()

        first = jnp.where(self.decoder, 4 + m, 2 * m)
        last = jnp.where(self.decoder, 5 + m, 2 * m + 2)
        lax.fori_loop(first, last, lambda j, carry: (self.pair_step(j), carry)[1], 0)
        self.line_step(jnp.where(self.decoder, 2 + m, m))

    def line_step(self, t):
        last = self.line - 1
        self.within(t - self.z, self.has_right, self.to_right)
        self.within(t - (last - self.z), self.has_left, self.to_left)
        self.within(t - last, True, self.finish)

    def within(self, p, more, body):
        @pl.when((p >= 0) & (p < self.positions) & more)
        def _():
            body(p)

    def partial(self, p, k):
        early = p < self.EARLY
        line_first = early & self.decoder
        i = jnp.where(line_first, p // 2, p - jnp.where(self.decoder, 2, 0))
        y = jnp.where(line_first & (lax.rem(p, 2) == 0), 1 - self.y, self.y)
        self.own_tile(i, k, y)

        @pl.when(jnp.logical_not(early))
        def _():
            j = p - self.EARLY
            self.pair_copy(j, k).wait_recv()
            self.acc[...] += self.pair_got[lax.rem(j, self.AHEAD) * self.line + k].astype(F32)

    def arrived(self, side, p, k):
        self.line_copy(side, p, k, self.z).wait_recv()
        self.acc[...] += self.line_got(self.line_place(side, p, k, self.z))[...].astype(F32)

    def send(self, side, p, k, inner):
        receiver = self.z - 1 if side else self.z + 1

        @pl.when(p >= self.DEPTH)
        def _():
            self.line_copy(side, p, k, receiver).wait_send()

        self.partial(p, k)

        @pl.when(inner)
        def _():
            self.arrived(side, p, k)

        slot = self.line_slot(p, k)
        slot[...] = self.acc[...].astype(BF)
        self.line_copy(side, p, k, receiver).start()

    def to_right(self, p):
        pl.semaphore_wait(self.right_credit, 1)

        def one(j):
            k = self.line - 1 - j

            @pl.when(k > self.z)
            def _():
                self.send(0, p, k, self.has_left)

        loop(self.line - 1, one)

    def to_left(self, p):
        pl.semaphore_wait(self.left_credit, 1)

        def one(k):
            @pl.when(k < self.z)
            def _():
                self.send(1, p, k, self.has_right)

        loop(self.line - 1, one)

    def finish(self, p):
        self.partial(p, self.z)

        @pl.when(self.has_left)
        def _():
            self.arrived(0, p, self.z)

        @pl.when(self.has_right)
        def _():
            self.arrived(1, p, self.z)

        line_first = (p < self.EARLY) & self.decoder

        @pl.when(line_first & (lax.rem(p, 2) == 0))
        def _():
            self.late_sent[p // 2] = self.acc[...].astype(BF)
            self.late_copy(p // 2).start()

        @pl.when(line_first & (lax.rem(p, 2) == 1))
        def _():
            self.late_acc[p // 2] = self.acc[...]

        @pl.when(jnp.logical_not(line_first))
        def _():
            i = p - jnp.where(self.decoder, 2, 0)

            @pl.when(i >= self.FINAL + jnp.where(self.decoder, 2, 0))
            def _():
                self.final_copy(i).wait()

            slot = self.final_slot(i)
            slot[...] = self.acc[...]
            self.final_copy(i).start()

        @pl.when(p + self.WINDOW < self.positions)
        def _():
            @pl.when(self.has_left)
            def _():
                pl.semaphore_signal(self.right_credit, inc=1, device_id=self.left, device_id_type=MESH)

            @pl.when(self.has_right)
            def _():
                pl.semaphore_signal(self.left_credit, inc=1, device_id=self.right, device_id_type=MESH)

        @pl.when((p >= self.EARLY) & (p - self.EARLY + self.AHEAD < self.pairs))
        def _():
            pl.semaphore_signal(self.pair_credit, inc=1, device_id=self.partner, device_id_type=MESH)
            self.pair_step(p - self.EARLY + self.AHEAD)

    def final_slot(self, i):
        slot = lax.rem(i, self.FINAL)
        return self.resid.at[self.tile_rows(slot // 2), self.cols(lax.rem(slot, 2))]

    def final_copy(self, i):
        return pltpu.make_async_copy(
            self.final_slot(i), self.tiles.at[i], self.final_sem.at[lax.rem(i, self.FINAL)]
        )

    def cross_part(self):
        @pl.when(self.decoder)
        def _():
            pl.semaphore_wait(self.cross_credit, 1)

            def one(q):
                def tile(k):
                    self.slope[q, self.tile_rows(k)] = dot_tn(
                        self.a_fac[4 + (q + 1) // 2, :, self.tile_rows(k)],
                        self.b_fac[self.own_chunks + q],
                    ).astype(BF)

                loop(4, tile)
                self.cross_copy(q).start()

            loop(4, one)

    def norm_copy(self, src, dst, device):
        return self.remote(self.nb.at[src], self.nb.at[dst], self.norm_send.at[dst], self.norm_recv.at[dst], device)

    def start_norms(self, sums):
        nb, has_left, has_right = self.nb, self.has_left, self.has_right
        for i in range(6):
            nb[0, i : i + 1] = jnp.sum(sums[i], 0, keepdims=True)
        nb[0, 6:8] = jnp.zeros_like(nb[0, 6:8])
        nb[3] = nb[0]
        nb[4] = nb[0]
        nb[5] = nb[0]

        @pl.when(jnp.logical_not(has_left))
        def _():
            self.norm_copy(3, 1, self.right).start()

        @pl.when(jnp.logical_not(has_right))
        def _():
            self.norm_copy(4, 2, self.left).start()

    def middle_norms(self):
        nb, has_left, has_right = self.nb, self.has_left, self.has_right
        to_right = self.norm_copy(3, 1, self.right)
        to_left = self.norm_copy(4, 2, self.left)

        @pl.when(has_left)
        def _():
            to_right.wait_recv()
            nb[5] += nb[1]

            @pl.when(has_right)
            def _():
                nb[3] += nb[1]
                to_right.start()

        @pl.when(has_right)
        def _():
            to_left.wait_recv()
            nb[5] += nb[2]

            @pl.when(has_left)
            def _():
                nb[4] += nb[2]
                to_left.start()

        self.norm_copy(5, 6, self.partner).start()

    def finish_norms(self, norm_out, norm3_out):
        nb = self.nb
        self.norm_copy(5, 6, self.partner).wait()

        @pl.when(self.has_right)
        def _():
            self.norm_copy(3, 1, self.right).wait_send()

        @pl.when(self.has_left)
        def _():
            self.norm_copy(4, 2, self.left).wait_send()

        nb[7] = nb[5] + nb[6]
        hand = self.norm_copy(7, 8, self.across)

        @pl.when(self.decoder)
        def _():
            hand.start()
            nb[8] = nb[7]

        norm_out[...] = nb[7, :, pl.ds(pl.multiple_of(self.dp * 128, 128), 128)]

        @pl.when(self.encoder)
        def _():
            hand.wait_recv()

        place = self.section * self.line * 2 + self.dp
        block = nb[8, :, pl.ds(pl.multiple_of(place // 2 * 128, 128), 128)]
        norm3_out[...] = jnp.where(self.y == 0, block, pltpu.roll(block, 64, 1))

        @pl.when(self.decoder)
        def _():
            hand.wait_send()

    def run(self, sums, norm_out, norm3_out):
        self.start_norms(sums)
        first = jnp.where(self.decoder, 6, 4)
        lax.fori_loop(first, self.AHEAD, lambda j, carry: (self.pair_step(j), carry)[1], 0)
        self.cross_part()

        def step(t, carry):
            self.line_step(t)

            @pl.when(t == 5)
            def _():
                self.middle_norms()

            @pl.when(t == self.positions - 1)
            def _():
                self.finish_norms(norm_out, norm3_out)

            return carry

        lax.fori_loop(jnp.where(self.decoder, 4, 2), self.positions + self.line - 1, step, 0)

    def drain(self):
        @pl.when(self.decoder)
        def _():
            for e in range(2):
                self.late_copy(e).wait()
                self.final_copy(e).wait()
                slot = self.final_slot(e)
                slot[...] = self.late_acc[e] + self.late_got[e].astype(F32)
                self.final_copy(e).start()

        for slot in range(self.AHEAD):
            for k in range(self.line):
                self.pair_copy(slot, k).wait_send()

        for slot in range(self.DEPTH):
            for k in range(self.line):

                @pl.when(self.z != k)
                def _():
                    self.line_copy(0, slot, k, 0).wait_send()

        for slot in range(self.FINAL):
            self.final_copy(slot).wait()

        @pl.when(self.decoder)
        def _():
            for q in range(4):
                self.cross_copy(q).wait_send()


def layer_kernel(
    sections,
    ring,
    inputs,
    targets,
    cotangent,
    counts,
    qkv_hbm,
    out_hbm,
    gain1,
    bias1,
    up_hbm,
    down_hbm,
    gain2,
    bias2,
    cross_hbm,
    cross_out_hbm,
    gain3,
    bias3,
    seg_out,
    in_grad,
    norm_out,
    first_out,
    second_out,
    w_qkv,
    w_out,
    w_up,
    w_down,
    w_cross,
    w_cross_out,
    a_fac,
    b_fac,
    proj,
    cross_proj,
    unit1,
    held,
    unit3,
    scale1,
    scale2,
    scale3,
    resid,
    slope,
    d_mix,
    sent,
    got,
    half_send,
    half_own,
    half_got,
    low_out,
    sums,
    load_sem,
    x_sem,
    ex_send,
    ex_recv,
    hop_send,
    hop_recv,
    out_sem,
    *share,
):
    section = lax.axis_index("section")
    dp = lax.axis_index("dp")
    core = lax.axis_index("mp")
    decoder = section == sections - 1
    encoder = section != sections - 1
    mate = (section, dp, 1 - core)
    across = (1 - section, dp, core)
    half = seg_out.shape[2]
    slot = 2 * half
    limit = jnp.where(decoder, 0, slot)
    width = w_up.shape[1]
    parts = width // CHUNK
    two, three = jnp.where(decoder, 0, 1), jnp.where(decoder, 1, 0)
    own = core * half
    other = (1 - core) * half

    d_branch, crossed, d_attn, layer_in, normed_low, memory, d_cross = (a_fac.at[i] for i in range(7))
    act = b_fac.at[0:parts]
    d_hidden = b_fac.at[parts : 2 * parts]
    mixed = b_fac.at[2 * parts]
    d_proj = b_fac.at[2 * parts + 1 : 2 * parts + 4]
    d_cross_proj = b_fac.at[2 * parts + 4 : 2 * parts + 7]
    cross_mixed = b_fac.at[2 * parts + 7]

    unit2, d_out = held.at[0], held.at[1]

    def rows_of(m):
        return pl.ds(pl.multiple_of(m * slot, slot), slot)

    def half_of(m, offset):
        return pl.ds(pl.multiple_of(m * slot + offset, half), half)

    def strip_of(m, k):
        return pl.ds(pl.multiple_of(m * slot + k * STRIP, STRIP), STRIP)

    def strips(body):
        for k in range(slot // STRIP):
            body(k)

    barrier = pltpu.get_barrier_semaphore()
    for device in (mate, across):
        pl.semaphore_signal(barrier, inc=1, device_id=device, device_id_type=MESH)
    if ring:
        total = GradientShare(
            ring, section, dp, core, decoder, a_fac, b_fac, first_out, w_up, w_down, held, slope, resid, *share
        )
        greeted = 2 + total.greet(barrier)
    else:
        greeted = 2

    loads = [
        pltpu.make_async_copy(src, dst, load_sem.at[i])
        for i, (src, dst) in enumerate(
            (
                (qkv_hbm.at[0], w_qkv),
                (out_hbm.at[0], w_out),
                (up_hbm.at[0], w_up),
                (down_hbm.at[0], w_down),
                (cross_hbm, w_cross),
                (cross_out_hbm, w_cross_out),
            )
        )
    ]

    def local_rows(src, dst, m, sem):
        return pltpu.make_async_copy(src.at[m], dst.at[half_of(m, own)], sem)

    def mate_rows(src, dst, m, send, recv):
        return pltpu.make_async_remote_copy(
            src_ref=src.at[m],
            dst_ref=dst.at[half_of(m, own)],
            send_sem=send,
            recv_sem=recv,
            device_id=mate,
            device_id_type=MESH,
        )

    def start_rows(src, dst, base):
        for m in range(2):
            local_rows(src, dst, m, x_sem.at[base + m]).start()
        for m in range(2):
            mate_rows(src, dst, m, x_sem.at[base + 2 + m], x_sem.at[base + 4 + m]).start()

    def wait_rows(src, dst, base, m):
        local_rows(src, dst, m, x_sem.at[base + m]).wait()
        mate_rows(src, dst, m, x_sem.at[base + 2 + m], x_sem.at[base + 4 + m]).wait()

    @pl.when(encoder)
    def _():
        for m in range(2):
            local_rows(inputs, layer_in, m, x_sem.at[m]).start()

    @pl.when(decoder)
    def _():
        for m in range(2):
            local_rows(targets, layer_in, m, x_sem.at[m]).start()

    loads[0].start()
    loads[1].start()
    pl.semaphore_wait(barrier, greeted)

    def mate_start(src, dst, base):
        for m in range(2):
            mate_rows(src, dst, m, x_sem.at[base + 2 + m], x_sem.at[base + 4 + m]).start()

    @pl.when(encoder)
    def _():
        mate_start(inputs, layer_in, 0)

    @pl.when(decoder)
    def _():
        mate_start(targets, layer_in, 0)

    for copy in loads[2:]:
        copy.start()

    @pl.when(decoder)
    def _():
        start_rows(cotangent, d_out, 6)

    sums[...] = jnp.zeros_like(sums)

    def exchange(which, buffer, m):
        return pltpu.make_async_remote_copy(
            src_ref=sent.at[rows_of(m)],
            dst_ref=got.at[buffer, rows_of(m)],
            send_sem=ex_send.at[which, m],
            recv_sem=ex_recv.at[which, m],
            device_id=mate,
            device_id_type=MESH,
        )

    def half_exchange(which, m):
        return pltpu.make_async_remote_copy(
            src_ref=half_send.at[which, m],
            dst_ref=half_got.at[which, m],
            send_sem=hop_send.at[4 + which, m],
            recv_sem=hop_recv.at[4 + which, m],
            device_id=mate,
            device_id_type=MESH,
        )

    def across_copy(src, dst, which, m):
        return pltpu.make_async_remote_copy(
            src_ref=src,
            dst_ref=dst.at[half_of(m, own)],
            send_sem=hop_send.at[which, m],
            recv_sem=hop_recv.at[which, m],
            device_id=across,
            device_id_type=MESH,
        )

    def forward_copy(ref, which, m):
        return pltpu.make_async_remote_copy(
            src_ref=ref.at[half_of(m, own)],
            dst_ref=ref.at[half_of(m, own)],
            send_sem=hop_send.at[which, m],
            recv_sem=hop_recv.at[which, m],
            device_id=mate,
            device_id_type=MESH,
        )

    def project_out(value, weight, m):
        for n in range(sent.shape[1] // CHUNK):
            cols = slice(n * CHUNK, (n + 1) * CHUNK)
            sent[rows_of(m), cols] = dot_nt(value, weight[cols, :]).astype(BF)

    def summed(buffer, strip):
        return sent[strip].astype(F32) + got[buffer, strip].astype(F32)

    loads[0].wait()

    def attention_in(m):
        @pl.when(encoder)
        def _():
            wait_rows(inputs, layer_in, 0, m)

        @pl.when(decoder)
        def _():
            wait_rows(targets, layer_in, 0, m)

        rows = rows_of(m)
        for t in range(3):
            proj[t, rows] = dot_nn(layer_in[rows], w_qkv[t]).astype(BF)
        attend_forward(proj, mixed, rows, limit)
        project_out(mixed[rows], w_out, m)
        exchange(0, 0, m).start()

    loads[1].wait()
    loop(2, attention_in)
    for copy in loads[2:]:
        copy.wait()

    def after_attention(m):
        exchange(0, 0, m).wait()

        def norm(k):
            strip = strip_of(m, k)
            unit, scale, value = norm_forward(
                layer_in[strip].astype(F32) + summed(0, strip), gain1[...], bias1[...]
            )
            unit1[strip] = unit.astype(BF)
            scale1[strip] = scale
            resid[strip] = value
            low_out[pl.ds(k * STRIP, STRIP)] = value.astype(BF)
            crossed[strip] = value.astype(BF)

        strips(norm)

        @pl.when(decoder)
        def _():
            rows = rows_of(m)
            normed_low[rows] = low_out[...]
            cross_proj[0, rows] = dot_nn(low_out[...], w_cross[0]).astype(BF)
            across_copy(seg_out.at[0, m], memory, 0, m).wait_recv()
            forward_copy(memory, 1, m).start()
            forward_copy(memory, 1, m).wait()
            for t in range(1, 3):
                cross_proj[t, rows] = dot_nn(memory[rows], w_cross[t]).astype(BF)
            attend_forward(cross_proj, cross_mixed, rows, None)
            project_out(cross_mixed[rows], w_cross_out, m)
            exchange(1, 1, m).start()

    loop(2, after_attention)

    def feed_forward(m):
        rows = rows_of(m)

        @pl.when(decoder)
        def _():
            exchange(1, 1, m).wait()

            def norm(k):
                strip = strip_of(m, k)
                unit, scale, value = norm_forward(
                    resid[strip] + summed(1, strip), gain3[...], bias3[...]
                )
                unit3[strip] = unit.astype(BF)
                scale3[strip] = scale
                resid[strip] = value
                crossed[strip] = value.astype(BF)

            strips(norm)

        for n in range(parts):
            pre = dot_nn(crossed[rows], w_up[:, n * CHUNK : (n + 1) * CHUNK])
            rise = 0.5 + 0.5 * lax.erf(pre * (0.5**0.5))
            act[n, rows] = (pre * rise).astype(BF)
            slope[n, rows] = (rise + pre * jnp.exp(-0.5 * pre * pre) * 0.3989422804014327).astype(BF)
        if ring:
            total.send_act(m)
        project_out(jnp.concatenate([act[n, rows] for n in range(parts)], 1), w_down, m)
        exchange(2, two, m).start()

    loop(2, feed_forward)

    def finish_forward(m):
        exchange(2, two, m).wait()

        def norm(k):
            strip = strip_of(m, k)
            unit, scale, value = norm_forward(
                resid[strip] + summed(two, strip), gain2[...], bias2[...]
            )
            unit2[strip] = unit.astype(BF)
            scale2[strip] = scale
            low_out[pl.ds(k * STRIP, STRIP)] = value.astype(BF)

        strips(norm)
        seg_out[0, m] = low_out[pl.ds(pl.multiple_of(own, half), half)]

        @pl.when(encoder)
        def _():
            across_copy(seg_out.at[0, m], memory, 0, m).start()

    loop(2, finish_forward)

    question = dp // QSLOTS
    spot = dp - question * QSLOTS

    def feed_backward(m):
        rows = rows_of(m)

        @pl.when(encoder)
        def _():
            across_copy(half_send.at[0, m], d_out, 2, m).wait_recv()
            forward_copy(d_out, 3, m).start()
            forward_copy(d_out, 3, m).wait()

        @pl.when(decoder)
        def _():
            wait_rows(cotangent, d_out, 6, m)

        keep = jnp.where(spot < counts[m, question], 1.0, 0.0)
        keep = jnp.where(decoder, keep, 1.0)

        def norm(k):
            strip = strip_of(m, k)
            grad = norm_backward(
                d_out[strip].astype(F32) * keep,
                unit2[strip].astype(F32),
                scale2[strip],
                gain2[...],
                sums,
                2,
            )
            resid[strip] = grad
            d_branch[strip] = grad.astype(BF)

        strips(norm)
        if ring:
            total.send_branch(m)
        for n in range(parts):
            grad = dot_nn(d_branch[rows], w_down[:, n * CHUNK : (n + 1) * CHUNK])
            d_hidden[n, rows] = (grad * slope[n, rows].astype(F32)).astype(BF)
        project_out(jnp.concatenate([d_hidden[n, rows] for n in range(parts)], 1), w_up, m)
        exchange(3, three, m).start()

    loop(2, feed_backward)
    if ring:
        total.begin()

    def cross_backward(m):
        rows = rows_of(m)

        def norm(k):
            strip = strip_of(m, k)
            grad = norm_backward(
                resid[strip] + summed(three, strip),
                unit3[strip].astype(F32),
                scale3[strip],
                gain3[...],
                sums,
                4,
            )
            resid[strip] = grad
            d_cross[strip] = grad.astype(BF)

        strips(norm)
        d_mix[rows] = dot_nn(d_cross[rows], w_cross_out[...]).astype(BF)
        attend_backward(cross_proj, d_mix, d_cross_proj, rows, None)

        def memory_part(offset):
            piece = half_of(m, offset)
            return jnp.concatenate([d_cross_proj[1, piece], d_cross_proj[2, piece]], 1)

        def memory_weight(n):
            cols = slice(n * CHUNK, (n + 1) * CHUNK)
            return jnp.concatenate([w_cross[1, cols], w_cross[2, cols]], 1)

        for n in range(sent.shape[1] // CHUNK):
            cols = slice(n * CHUNK, (n + 1) * CHUNK)
            half_send[0, m, :, cols] = dot_nt(memory_part(other), memory_weight(n)).astype(BF)
        half_exchange(0, m).start()
        for n in range(sent.shape[1] // CHUNK):
            cols = slice(n * CHUNK, (n + 1) * CHUNK)
            half_own[m, :, cols] = dot_nt(memory_part(own), memory_weight(n))
        project_out(d_cross_proj[0, rows], w_cross[0], m)
        exchange(4, 0, m).start()
        half_exchange(0, m).wait()
        half_send[0, m] = (half_own[m] + half_got[0, m].astype(F32)).astype(BF)
        across_copy(half_send.at[0, m], d_out, 2, m).start()

    def attention_back(m):
        rows = rows_of(m)

        def norm_rows(buffer):
            def norm(k):
                strip = strip_of(m, k)
                grad = norm_backward(
                    resid[strip] + summed(buffer, strip),
                    unit1[strip].astype(F32),
                    scale1[strip],
                    gain1[...],
                    sums,
                    0,
                )
                resid[strip] = grad
                d_attn[strip] = grad.astype(BF)

            strips(norm)

        @pl.when(decoder)
        def _():
            exchange(4, 0, m).wait()

        @pl.when(encoder)
        def _():
            exchange(3, three, m).wait()

        norm_rows(0)
        d_mix[rows] = dot_nn(d_attn[rows], w_out[...]).astype(BF)
        attend_backward(proj, d_mix, d_proj, rows, limit)

        def input_part(offset):
            piece = half_of(m, offset)
            return jnp.concatenate([d_proj[t, piece] for t in range(3)], 1)

        def input_weight(n):
            cols = slice(n * CHUNK, (n + 1) * CHUNK)
            return jnp.concatenate([w_qkv[t, cols] for t in range(3)], 1)

        for n in range(sent.shape[1] // CHUNK):
            cols = slice(n * CHUNK, (n + 1) * CHUNK)
            half_send[1, m, :, cols] = dot_nt(input_part(other), input_weight(n)).astype(BF)
        half_exchange(1, m).start()
        for n in range(sent.shape[1] // CHUNK):
            cols = slice(n * CHUNK, (n + 1) * CHUNK)
            half_own[m, :, cols] = dot_nt(input_part(own), input_weight(n))

    @pl.when(decoder)
    def _():
        def both(m):
            if ring:
                total.between(m)
            exchange(3, three, m).wait()
            cross_backward(m)

        loop(2, both)

    def last_part(m):
        if ring:
            total.before(m)
        attention_back(m)

    loop(2, last_part)

    def finish_backward(m):
        half_exchange(1, m).wait()
        in_grad[0, m] = (
            resid[half_of(m, own)] + half_own[m] + half_got[1, m].astype(F32)
        ).astype(BF)

    loop(2, finish_backward)

    @pl.when(encoder)
    def _():
        for m in range(2):
            across_copy(seg_out.at[0, m], memory, 0, m).wait_send()

    @pl.when(decoder)
    def _():
        for m in range(2):
            across_copy(half_send.at[0, m], d_out, 2, m).wait_send()

    if ring:
        total.run(sums, norm_out, second_out)
        total.drain()
        return

    for i in range(6):
        norm_out[i : i + 1] = jnp.sum(sums[i], 0, keepdims=True)
    norm_out[6:8] = jnp.zeros_like(norm_out[6:8])
    copies = [
        pltpu.make_async_copy(a_fac, first_out, out_sem.at[0]),
        pltpu.make_async_copy(b_fac, second_out, out_sem.at[1]),
    ]
    for copy in copies:
        copy.start()
    for copy in copies:
        copy.wait()


def unpack_kernel(parts, seg, grads, norms, tiles, norm3, *outs):
    (seg_out, in_grad, qkv, proj_out, gain1, bias1, up, down, gain2, bias2, cross, cross_out, gain3, bias3, sems) = outs
    rows = tiles.shape[1]
    small = rows // 2
    copies = [(seg, seg_out), (grads, in_grad)]
    for n in range(parts):
        cols = slice(n * CHUNK, (n + 1) * CHUNK)
        copies.append((tiles.at[n], down.at[0, :, cols]))
        copies.append((tiles.at[parts + n], up.at[0, :, cols]))
    copies.append((tiles.at[2 * parts], proj_out.at[0]))
    for t in range(3):
        copies.append((tiles.at[2 * parts + 1 + t], qkv.at[0, t]))
    for q in range(4):
        source = tiles.at[2 * parts + 4 + q // 2, pl.ds(q % 2 * small, small)]
        copies.append((source, cross.at[q] if q < 3 else cross_out))
    copies = [pltpu.make_async_copy(src, dst, sems.at[i]) for i, (src, dst) in enumerate(copies)]
    for copy in copies:
        copy.start()
    for i, ref in enumerate((gain1, bias1, gain2, bias2)):
        ref[...] = norms[i : i + 1]
    gain3[...] = norm3[4:5, :small]
    bias3[...] = norm3[5:6, :small]
    for copy in copies:
        copy.wait()


def body(
    sections,
    ring,
    inputs,
    target_inputs,
    cotangent,
    slot_counts,
    w_qkv,
    w_out,
    norm1_gain,
    norm1_bias,
    w_up,
    w_down,
    norm2_gain,
    norm2_bias,
    cross_qkv,
    cross_out,
    norm3_gain,
    norm3_bias,
):
    micro, half, depth = inputs.shape
    rows = micro * 2 * half
    heads = w_out.shape[2]
    width = w_up.shape[2]
    parts = width // CHUNK
    chunks = 2 * parts + 8
    hbm = pl.BlockSpec(memory_space=pl.ANY)
    vmem = pl.BlockSpec(memory_space=VM)
    smem = pl.BlockSpec(memory_space=pltpu.SMEM)
    shape = jax.ShapeDtypeStruct
    if ring:
        results = (
            shape((8, depth // ring), F32),
            shape((chunks - 2, depth // ring, CHUNK), F32),
            shape((8, depth // ring), F32),
        )
        places = (vmem, hbm, vmem)
    else:
        results = (
            shape((8, depth), F32),
            shape((7, rows, depth), BF),
            shape((chunks, rows, CHUNK), BF),
        )
        places = (vmem, hbm, hbm)
    dma = pltpu.SemaphoreType.DMA
    regular = pltpu.SemaphoreType.REGULAR
    tile = (depth // ring, CHUNK) if ring else None
    share = (
        [
            VM((GradientShare.AHEAD * 4,) + tile, BF),
            VM(tile, F32),
            VM((9, 8, depth), F32),
            VM((2,) + tile, BF),
            VM((2,) + tile, BF),
            VM((2,) + tile, F32),
            dma((GradientShare.AHEAD * 4,)),
            dma((GradientShare.AHEAD * 4,)),
            dma((GradientShare.DEPTH * 4,)),
            dma((GradientShare.WINDOW * 5,)),
            dma((4,)),
            dma((4,)),
            dma((9,)),
            dma((9,)),
            dma((2,)),
            dma((2,)),
            dma((13,)),
            dma((13,)),
            dma((GradientShare.FINAL,)),
            regular,
            regular,
            regular,
            regular,
        ]
        if ring
        else []
    )
    seg_out, in_grad, norms, first, second = pl.pallas_call(
        functools.partial(layer_kernel, sections, ring),
        out_shape=(
            shape((1, micro, half, depth), BF),
            shape((1, micro, half, depth), BF),
        )
        + results,
        in_specs=[hbm, hbm, hbm, smem, hbm, hbm, vmem, vmem, hbm, hbm, vmem, vmem, hbm, hbm, vmem, vmem],
        out_specs=(vmem, vmem) + places,
        scratch_shapes=[
            VM((3, depth, heads), BF),
            VM((depth, heads), BF),
            VM((depth, width), BF),
            VM((depth, width), BF),
            VM((3, depth, heads), BF),
            VM((depth, heads), BF),
            VM((7, rows, depth), BF),
            VM((chunks, rows, CHUNK), BF),
            VM((3, rows, heads), BF),
            VM((3, rows, heads), BF),
            VM((rows, depth), BF),
            VM((2, rows, depth), BF),
            VM((rows, depth), BF),
            VM((rows, 1), F32),
            VM((rows, 1), F32),
            VM((rows, 1), F32),
            VM((rows, depth), F32),
            VM((parts, rows, CHUNK), BF),
            VM((rows, heads), BF),
            VM((rows, depth), BF),
            VM((2, rows, depth), BF),
            VM((2, micro, half, depth), BF),
            VM((micro, half, depth), F32),
            VM((2, micro, half, depth), BF),
            VM((2 * half, depth), BF),
            VM((6, 8, depth), F32),
            pltpu.SemaphoreType.DMA((6,)),
            pltpu.SemaphoreType.DMA((12,)),
            pltpu.SemaphoreType.DMA((5, micro)),
            pltpu.SemaphoreType.DMA((5, micro)),
            pltpu.SemaphoreType.DMA((6, micro)),
            pltpu.SemaphoreType.DMA((6, micro)),
            pltpu.SemaphoreType.DMA((2,)),
        ]
        + share,
        compiler_params=pltpu.CompilerParams(
            collective_id=0, has_side_effects=True, vmem_limit_bytes=60 * 2**20
        ),
        name="layers",
    )(
        inputs,
        target_inputs,
        cotangent,
        slot_counts,
        w_qkv,
        w_out,
        norm1_gain,
        norm1_bias,
        w_up,
        w_down,
        norm2_gain,
        norm2_bias,
        cross_qkv,
        cross_out,
        norm3_gain[None],
        norm3_bias[None],
    )
    if ring:
        lanes = depth // ring
        row = shape((1, lanes), F32)
        small = shape((1, lanes // 2), F32)
        outs = pl.pallas_call(
            functools.partial(unpack_kernel, parts),
            out_shape=(
                shape(seg_out.shape, BF),
                shape(in_grad.shape, BF),
                shape((1, 3, lanes, heads), F32),
                shape((1, lanes, heads), F32),
                row,
                row,
                shape((1, lanes, width), F32),
                shape((1, lanes, width), F32),
                row,
                row,
                shape((3, lanes // 2, heads), F32),
                shape((lanes // 2, heads), F32),
                small,
                small,
            ),
            in_specs=[hbm, hbm, vmem, hbm, vmem],
            out_specs=(vmem,) * 14,
            scratch_shapes=[pltpu.SemaphoreType.DMA((2 * parts + 10,))],
            name="unpack",
        )(seg_out, in_grad, norms, first, second)
        return outs[:12] + (outs[12][0], outs[13][0])
    a_fac, b_fac = first, second
    decoder = lax.axis_index("section") == sections - 1

    def weight_grad(left, first, count):
        return jnp.einsum(
            "nd,tnc->tdc", a_fac[left], b_fac[first : first + count], preferred_element_type=F32
        ).astype(BF)

    def shared(grad, axes, dim):
        return lax.psum_scatter(grad, axes, scatter_dimension=dim, tiled=True)

    def wide(grad):
        return jnp.swapaxes(grad, 0, 1).reshape(depth, -1)

    grad_down = shared(wide(weight_grad(0, 0, parts)), "dp", 0)
    grad_up = shared(wide(weight_grad(1, parts, parts)), "dp", 0)
    grad_out = shared(weight_grad(2, 2 * parts, 1)[0], "dp", 0)
    grad_qkv = shared(weight_grad(3, 2 * parts + 1, 3), "dp", 1)
    cross = jnp.concatenate(
        [
            weight_grad(4, 2 * parts + 4, 1),
            weight_grad(5, 2 * parts + 5, 2),
            weight_grad(6, 2 * parts + 7, 1),
        ],
        0,
    )
    cross = shared(jnp.where(decoder, cross, jnp.zeros_like(cross)), ("section", "dp"), 1)
    small = shared(norms[:4], "dp", 1)
    norm3 = jnp.where(decoder, norms[4:6], jnp.zeros_like(norms[4:6]))
    norm3 = shared(norm3, ("section", "dp"), 1)
    return (
        seg_out,
        in_grad,
        grad_qkv[None].astype(F32),
        grad_out[None].astype(F32),
        small[0:1],
        small[1:2],
        grad_up[None].astype(F32),
        grad_down[None].astype(F32),
        small[2:3],
        small[3:4],
        cross[:3].astype(F32),
        cross[3].astype(F32),
        norm3[0],
        norm3[1],
    )


def solution(mesh):
    ring = 8 if mesh.shape["dp"] == 8 else 0
    return jax.shard_map(
        functools.partial(body, mesh.shape["section"], ring),
        mesh=mesh,
        in_specs=(
            P(None, ("dp", "mp"), None),
            P(None, ("dp", "mp"), None),
            P(None, ("dp", "mp"), None),
            P(),
            P("section", None, None, "mp"),
            P("section", None, "mp"),
            P("section", None),
            P("section", None),
            P("section", None, "mp"),
            P("section", None, "mp"),
            P("section", None),
            P("section", None),
            P(None, None, "mp"),
            P(None, "mp"),
            P(),
            P(),
        ),
        out_specs=(
            P("section", None, ("dp", "mp"), None),
            P("section", None, ("dp", "mp"), None),
            P("section", None, "dp", "mp"),
            P("section", "dp", "mp"),
            P("section", "dp"),
            P("section", "dp"),
            P("section", "dp", "mp"),
            P("section", "dp", "mp"),
            P("section", "dp"),
            P("section", "dp"),
            P(None, ("section", "dp"), "mp"),
            P(("section", "dp"), "mp"),
            P(("section", "dp")),
            P(("section", "dp")),
        ),
        check_vma=False,
    )
```

```python
import functools

import jax
import jax.numpy as jnp
from jax import lax
from jax.experimental import pallas as pl
from jax.experimental.pallas import tpu as pltpu
from jax.sharding import PartitionSpec as P

HEAD = 64
SLOT = 256
QSLOTS = 4
CHUNK = 512
PAIR = 2 * HEAD
STRIP = 64
EPS = 1e-5
NEG = -1000000000.0
MESH = pl.DeviceIdType.MESH
BF = jnp.bfloat16
F32 = jnp.float32
VM = pltpu.VMEM


def dot_nn(a, b):
    return lax.dot_general(a, b, (((1,), (0,)), ((), ())), preferred_element_type=F32)


def dot_nt(a, b):
    return lax.dot_general(a, b, (((1,), (1,)), ((), ())), preferred_element_type=F32)


def dot_tn(a, b):
    return lax.dot_general(a, b, (((0,), (0,)), ((), ())), preferred_element_type=F32)


def loop(count, body):
    def step(i, carry):
        body(i)
        return carry

    lax.fori_loop(0, count, step, 0)


def head_masks():
    lane = lax.broadcasted_iota(jnp.int32, (1, PAIR), 1)
    first = jnp.where(lane < HEAD, 1.0, 0.0).astype(BF)
    second = jnp.where(lane < HEAD, 0.0, 1.0).astype(BF)
    return first, second


def expos_of(query, keys, mask, limit):
    scores = dot_nt(keys, query * (mask * (HEAD**-0.5)).astype(BF))
    if limit is not None:
        key = lax.broadcasted_iota(jnp.int32, scores.shape, 0)
        place = lax.broadcasted_iota(jnp.int32, scores.shape, 1)
        scores = jnp.where(place + limit >= key, scores, NEG)
    expo = jnp.exp(scores - jnp.max(scores, 0, keepdims=True))
    return expo, 1.0 / jnp.sum(expo, 0, keepdims=True)


def attend_forward(proj, mixed, rows, limit):
    masks = head_masks()
    for j in range(CHUNK // PAIR):
        lanes = slice(j * PAIR, (j + 1) * PAIR)
        query, keys, values = proj[0, rows, lanes], proj[1, rows, lanes], proj[2, rows, lanes]
        low = []
        for mask in masks:
            expo, share = expos_of(query, keys, mask, limit)
            low.append((expo * share).astype(BF))
        turned = dot_tn(jnp.concatenate([values * mask for mask in masks], 0), jnp.concatenate(low, 0))
        mixed[rows, lanes] = turned.T.astype(BF)


def attend_backward(proj, d_mixed, d_proj, rows, limit):
    masks = head_masks()
    scale = HEAD**-0.5
    for j in range(CHUNK // PAIR):
        lanes = slice(j * PAIR, (j + 1) * PAIR)
        query, keys, values = proj[0, rows, lanes], proj[1, rows, lanes], proj[2, rows, lanes]
        grad = d_mixed[rows, lanes]
        low, d_scores = [], []
        for mask in masks:
            expo, share = expos_of(query, keys, mask, limit)
            weights = expo * share
            d_weights = dot_nt(values, grad * mask)
            inner = jnp.sum(weights * d_weights, 0, keepdims=True)
            d_scores.append((weights * (d_weights - inner)).astype(BF))
            low.append(weights.astype(BF))
        d_proj[2, rows, lanes] = dot_nn(
            jnp.concatenate(low, 1), jnp.concatenate([grad * mask for mask in masks], 0)
        ).astype(BF)
        d_proj[1, rows, lanes] = (
            dot_nn(
                jnp.concatenate(d_scores, 1), jnp.concatenate([query * mask for mask in masks], 0)
            )
            * scale
        ).astype(BF)
        turned = dot_tn(
            jnp.concatenate([keys * mask for mask in masks], 0), jnp.concatenate(d_scores, 0)
        )
        d_proj[0, rows, lanes] = (turned.T * scale).astype(BF)


def norm_forward(value, gain, bias):
    center = value - jnp.mean(value, -1, keepdims=True)
    scale = lax.rsqrt(jnp.mean(center * center, -1, keepdims=True) + EPS)
    unit = center * scale
    return unit, scale, unit * gain + bias


def norm_backward(grad, unit, scale, gain, sums, which):
    fold = lambda v: jnp.sum(v.reshape(v.shape[0] // 8, 8, v.shape[1]), 0)
    sums[which] += fold(grad * unit)
    sums[which + 1] += fold(grad)
    d_unit = grad * gain
    first = jnp.mean(d_unit, -1, keepdims=True)
    second = jnp.mean(d_unit * unit, -1, keepdims=True)
    return scale * (d_unit - first - unit * second)


class GradientShare:
    AHEAD = 8
    WINDOW = 6
    DEPTH = 4
    FINAL = 8
    EARLY = 4

    def __init__(self, size, section, dp, core, decoder, a_fac, b_fac, tiles, w_up, w_down, held, slope, resid, acc, *share):
        self.acc = acc
        (self.pair_got, self.nb, self.late_sent, self.late_got, self.late_acc, self.pair_send,
         self.pair_recv, self.line_send, self.line_recv, self.cross_send, self.cross_recv, self.norm_send,
         self.norm_recv, self.late_send, self.late_recv, self.factor_send, self.factor_recv, self.final_sem,
         self.pair_credit, self.left_credit, self.right_credit, self.cross_credit) = share
        self.line = size // 2
        self.section, self.dp, self.core = section, dp, core
        self.decoder, self.encoder = decoder, jnp.logical_not(decoder)
        self.z, self.y = dp // 2, lax.rem(dp, 2)
        self.a_fac, self.b_fac, self.tiles = a_fac, b_fac, tiles
        self.w_up, self.w_down, self.held, self.slope, self.resid = w_up, w_down, held, slope, resid
        self.rows = a_fac.shape[2] // size
        self.own_chunks = b_fac.shape[0] - 4
        self.positions = self.own_chunks + 2 + jnp.where(decoder, 2, 0)
        self.pairs = self.positions - self.EARLY
        self.partner = (section, dp + 1 - 2 * self.y, core)
        self.right = (section, dp + 2, core)
        self.left = (section, dp - 2, core)
        self.across = (1 - section, dp, core)
        self.mate = (section, dp, 1 - core)
        self.has_left, self.has_right = self.z > 0, self.z < self.line - 1

    def greet(self, barrier):
        pl.semaphore_signal(barrier, inc=1, device_id=self.partner, device_id_type=MESH)

        @pl.when(self.has_left)
        def _():
            pl.semaphore_signal(barrier, inc=1, device_id=self.left, device_id_type=MESH)

        @pl.when(self.has_right)
        def _():
            pl.semaphore_signal(barrier, inc=1, device_id=self.right, device_id_type=MESH)

        return 1 + jnp.where(self.has_left, 1, 0) + jnp.where(self.has_right, 1, 0)

    def remote(self, src, dst, send, recv, device):
        return pltpu.make_async_remote_copy(
            src_ref=src, dst_ref=dst, send_sem=send, recv_sem=recv, device_id=device, device_id_type=MESH
        )

    def tile_rows(self, k):
        return pl.ds(pl.multiple_of(k * self.rows, self.rows), self.rows)

    def cols(self, k):
        return pl.ds(pl.multiple_of(k * CHUNK, CHUNK), CHUNK)

    def pair_slot(self, j, k):
        return self.w_down.at[self.tile_rows(lax.rem(j, self.AHEAD)), self.cols(k)]

    def pair_copy(self, j, k):
        slot = lax.rem(j, self.AHEAD) * self.line + k
        return self.remote(
            self.pair_slot(j, k), self.pair_got.at[slot], self.pair_send.at[slot], self.pair_recv.at[slot], self.partner
        )

    def line_slot(self, p, k):
        slot = lax.rem(p, self.DEPTH) * self.line + k
        return self.held.at[slot // 8, self.tile_rows(lax.rem(slot, 4)), self.cols(lax.rem(slot // 4, 2))]

    def line_place(self, side, p, k, z):
        return lax.rem(p, self.WINDOW) * (self.line + 1) + (self.line - z + k if side else k - z)

    def line_got(self, place):
        return self.w_up.at[self.tile_rows(place // 4), self.cols(lax.rem(place, 4))]

    def line_copy(self, side, p, k, receiver):
        place = self.line_place(side, p, k, receiver)
        return self.remote(
            self.line_slot(p, k),
            self.line_got(place),
            self.line_send.at[lax.rem(p, self.DEPTH) * self.line + k],
            self.line_recv.at[place],
            self.left if side else self.right,
        )

    def cross_copy(self, q):
        return self.remote(
            self.slope.at[q], self.slope.at[q], self.cross_send.at[q], self.cross_recv.at[q], self.across
        )

    def late_copy(self, e):
        return self.remote(
            self.late_sent.at[e], self.late_got.at[e], self.late_send.at[e], self.late_recv.at[e], self.partner
        )

    def act_copy(self, n, m):
        rows = pl.ds(pl.multiple_of(m * SLOT, SLOT), SLOT)
        return self.remote(
            self.b_fac.at[n, rows],
            self.a_fac.at[5 + n // 2, rows, pl.ds(n % 2 * CHUNK, CHUNK)],
            self.factor_send.at[n * 2 + m],
            self.factor_recv.at[n * 2 + m],
            self.partner,
        )

    def branch_copy(self, k):
        rows = pl.ds(pl.multiple_of(self.core * SLOT, SLOT), SLOT)
        return self.remote(
            self.a_fac.at[0, rows, self.tile_rows(k * 2 + 1 - self.y)],
            self.a_fac.at[4, rows, pl.ds(k * self.rows, self.rows)],
            self.factor_send.at[8 + k],
            self.factor_recv.at[8 + k],
            self.partner,
        )

    def branch_forward(self):
        rows = pl.ds(pl.multiple_of(self.core * SLOT, SLOT), SLOT)
        part = self.a_fac.at[4, rows, pl.ds(0, CHUNK)]
        return self.remote(part, part, self.factor_send.at[12], self.factor_recv.at[12], self.mate)

    def send_act(self, m):
        @pl.when(self.encoder)
        def _():
            for n in range(4):
                self.act_copy(n, m).start()

    def send_branch(self, m):
        @pl.when(self.encoder & (self.core == m))
        def _():
            for k in range(4):
                self.branch_copy(k).start()

    def take_factors(self):
        for k in range(4):
            self.branch_copy(k).wait_recv()
        self.branch_forward().start()
        for m in range(2):
            for n in range(4):
                self.act_copy(n, m).wait()
        for k in range(4):
            self.branch_copy(k).wait_send()
        self.branch_forward().wait()

    def left_of(self, i):
        return jnp.minimum(i // 4, 2) + jnp.where(i > 8, 1, 0)

    def cross_tile(self, i, k, y):
        first = (i - self.own_chunks) * 2
        small = self.rows // 2
        base = self.a_fac.shape[2] // 2

        def product(e):
            q = first + e
            block = dot_tn(
                self.a_fac[4 + (q + 1) // 2, :, pl.ds(pl.multiple_of(base + k * self.rows, self.rows), self.rows)],
                self.b_fac[self.own_chunks + q],
            )
            return jnp.where(y == 0, block[:small], block[small:])

        def given(e):
            place = pl.ds(pl.multiple_of(k * self.rows + y * small, small), small)
            return self.slope[first + e, place].astype(F32)

        return product, given

    def cross_into(self, ref, i, k, y):
        product, given = self.cross_tile(i, k, y)
        small = self.rows // 2

        @pl.when(self.decoder)
        def _():
            for e in range(2):
                ref[e * small : (e + 1) * small] = product(e).astype(ref.dtype)

        @pl.when(self.encoder)
        def _():
            for e in range(2):
                ref[e * small : (e + 1) * small] = given(e).astype(ref.dtype)

    def pair_step(self, j):
        i = j + jnp.where(self.decoder, 2, 4)

        @pl.when(j >= self.AHEAD)
        def _():
            pl.semaphore_wait(self.pair_credit, 1)
            for k in range(self.line):
                self.pair_copy(j, k).wait_send()

        @pl.when(i < self.own_chunks)
        def _():
            left = self.left_of(i)
            factor = jnp.concatenate(
                [self.a_fac[left, :, self.tile_rows(k * 2 + 1 - self.y)] for k in range(self.line)], 1
            )
            block = dot_tn(factor, self.b_fac[i]).astype(BF)
            for k in range(self.line):
                slot = self.pair_slot(j, k)
                slot[...] = block[k * self.rows : (k + 1) * self.rows]

        @pl.when(i >= self.own_chunks)
        def _():
            @pl.when(self.encoder)
            def _():
                for e in range(2):
                    self.cross_copy((i - self.own_chunks) * 2 + e).wait_recv()

            loop(self.line, lambda k: self.cross_into(self.pair_slot(j, k), i, k, 1 - self.y))

        for k in (0, 3, 1, 2):
            self.pair_copy(j, k).start()

    def begin(self):
        @pl.when(self.has_left)
        def _():
            pl.semaphore_signal(self.right_credit, inc=self.WINDOW, device_id=self.left, device_id_type=MESH)

        @pl.when(self.has_right)
        def _():
            pl.semaphore_signal(self.left_credit, inc=self.WINDOW, device_id=self.right, device_id_type=MESH)

        @pl.when(self.encoder)
        def _():
            pl.semaphore_signal(self.cross_credit, inc=1, device_id=self.across, device_id_type=MESH)

    def between(self, m):
        @pl.when(m == 0)
        def _():
            loop(2, self.pair_step)

        self.line_step(m)

    def before(self, m):
        @pl.when(self.encoder & (m == 0))
        def _():
            self.take_factors()

        self.line_step(jnp.where(self.decoder, 2, 0) + 2 * m)
        first = jnp.where(self.decoder, 2, 0) + 2 * m
        lax.fori_loop(first, first + 2, lambda j, carry: (self.pair_step(j), carry)[1], 0)

    def middle(self, m):
        self.line_step(jnp.where(self.decoder, 3, 1) + 2 * m)

    def entry(self, t, e):
        last = self.line - 1
        on = last - self.z
        k = jnp.where(e == last, self.z, jnp.where(e < on, last - e, e - on))
        hops = jnp.where(k > self.z, self.z, last - self.z)
        p = t - jnp.where(e == last, last, hops)
        valid = (p >= 0) & (p < self.positions)
        line_first = (p < self.EARLY) & self.decoder
        i = jnp.where(line_first, p // 2, p - jnp.where(self.decoder, 2, 0))
        y = jnp.where(line_first & (lax.rem(p, 2) == 0), 1 - self.y, self.y)
        return k, p, valid, i, y

    def line_step(self, t):
        last = self.line - 1

        def held_at(p):
            return (p >= 0) & (p < self.positions)

        @pl.when(held_at(t - self.z) & self.has_right)
        def _():
            pl.semaphore_wait(self.right_credit, 1)

        @pl.when(held_at(t - (last - self.z)) & self.has_left)
        def _():
            pl.semaphore_wait(self.left_credit, 1)

        for e in range(self.line):
            k, p, valid, i, y = self.entry(t, e)
            i = jnp.clip(i, 0, self.own_chunks - 1)
            self.acc[e] = dot_tn(self.a_fac[self.left_of(i), :, self.tile_rows(k * 2 + y)], self.b_fac[i])

        @pl.when(self.encoder & (t < self.EARLY + last))
        def _():
            for e in range(self.line):
                k, p, valid, i, y = self.entry(t, e)
                n = jnp.clip(i, 0, self.EARLY - 1)
                part = dot_tn(
                    self.a_fac[4, :, self.tile_rows(k)], self.a_fac[5 + n // 2, :, self.cols(lax.rem(n, 2))]
                )
                self.acc[e] += jnp.where(i < self.EARLY, part, 0.0)

        def one(e):
            k, p, valid, i, y = self.entry(t, e)

            @pl.when(valid)
            def _():
                acc = self.acc.at[e]

                @pl.when(i >= self.own_chunks)
                def _():
                    self.cross_into(acc, i, k, y)

                @pl.when(p >= self.EARLY)
                def _():
                    j = p - self.EARLY
                    self.pair_copy(j, k).wait_recv()
                    acc[...] += self.pair_got[lax.rem(j, self.AHEAD) * self.line + k].astype(F32)

                @pl.when(e < last)
                def _():
                    self.send(p, k, acc)

                @pl.when(e == last)
                def _():
                    self.finish(p, acc)

        loop(self.line, one)

    def arrived(self, side, p, k):
        self.line_copy(side, p, k, self.z).wait_recv()
        return self.line_got(self.line_place(side, p, k, self.z))[...].astype(F32)

    def send(self, p, k, acc):
        slot = self.line_slot(p, k)

        def to(side, receiver, inner):
            copy = self.line_copy(side, p, k, receiver)

            @pl.when(p >= self.DEPTH)
            def _():
                copy.wait_send()

            @pl.when(inner)
            def _():
                slot[...] = (acc[...] + self.arrived(side, p, k)).astype(BF)

            @pl.when(jnp.logical_not(inner))
            def _():
                slot[...] = acc[...].astype(BF)

            copy.start()

        @pl.when(k > self.z)
        def _():
            to(0, self.z + 1, self.has_left)

        @pl.when(k < self.z)
        def _():
            to(1, self.z - 1, self.has_right)

    def finish(self, p, acc):
        @pl.when(self.has_left)
        def _():
            acc[...] += self.arrived(0, p, self.z)

        @pl.when(self.has_right)
        def _():
            acc[...] += self.arrived(1, p, self.z)

        line_first = (p < self.EARLY) & self.decoder

        @pl.when(line_first & (lax.rem(p, 2) == 0))
        def _():
            self.late_sent[p // 2] = acc[...].astype(BF)
            self.late_copy(p // 2).start()

        @pl.when(line_first & (lax.rem(p, 2) == 1))
        def _():
            self.late_acc[p // 2] = acc[...]

        @pl.when(jnp.logical_not(line_first))
        def _():
            i = p - jnp.where(self.decoder, 2, 0)

            @pl.when(i >= self.FINAL + jnp.where(self.decoder, 2, 0))
            def _():
                self.final_copy(i).wait()

            first = self.encoder & (i == 0)

            @pl.when(first)
            def _():
                self.late_acc[0] = acc[...]
                pltpu.make_async_copy(self.late_acc.at[0], self.tiles.at[0], self.final_sem.at[0]).start()

            @pl.when(jnp.logical_not(first))
            def _():
                slot = self.final_slot(i)
                slot[...] = acc[...]
                self.final_copy(i).start()

        @pl.when(p + self.WINDOW < self.positions)
        def _():
            @pl.when(self.has_left)
            def _():
                pl.semaphore_signal(self.right_credit, inc=1, device_id=self.left, device_id_type=MESH)

            @pl.when(self.has_right)
            def _():
                pl.semaphore_signal(self.left_credit, inc=1, device_id=self.right, device_id_type=MESH)

        @pl.when((p >= self.EARLY) & (p - self.EARLY + self.AHEAD < self.pairs))
        def _():
            pl.semaphore_signal(self.pair_credit, inc=1, device_id=self.partner, device_id_type=MESH)
            self.pair_step(p - self.EARLY + self.AHEAD)

    def final_slot(self, i):
        slot = lax.rem(i, self.FINAL)
        return self.resid.at[self.tile_rows(slot // 2), self.cols(lax.rem(slot, 2))]

    def final_copy(self, i):
        return pltpu.make_async_copy(
            self.final_slot(i), self.tiles.at[i], self.final_sem.at[lax.rem(i, self.FINAL)]
        )

    def cross_part(self):
        @pl.when(self.decoder)
        def _():
            pl.semaphore_wait(self.cross_credit, 1)

            def one(q):
                def tile(k):
                    self.slope[q, self.tile_rows(k)] = dot_tn(
                        self.a_fac[4 + (q + 1) // 2, :, self.tile_rows(k)],
                        self.b_fac[self.own_chunks + q],
                    ).astype(BF)

                loop(4, tile)
                self.cross_copy(q).start()

            loop(4, one)

    def norm_copy(self, src, dst, device):
        return self.remote(self.nb.at[src], self.nb.at[dst], self.norm_send.at[dst], self.norm_recv.at[dst], device)

    def start_norms(self, sums):
        nb, has_left, has_right = self.nb, self.has_left, self.has_right
        for i in range(6):
            nb[0, i : i + 1] = jnp.sum(sums[i], 0, keepdims=True)
        nb[0, 6:8] = jnp.zeros_like(nb[0, 6:8])
        nb[3] = nb[0]
        nb[4] = nb[0]
        nb[5] = nb[0]

        @pl.when(jnp.logical_not(has_left))
        def _():
            self.norm_copy(3, 1, self.right).start()

        @pl.when(jnp.logical_not(has_right))
        def _():
            self.norm_copy(4, 2, self.left).start()

    def middle_norms(self):
        nb, has_left, has_right = self.nb, self.has_left, self.has_right
        to_right = self.norm_copy(3, 1, self.right)
        to_left = self.norm_copy(4, 2, self.left)

        @pl.when(has_left)
        def _():
            to_right.wait_recv()
            nb[5] += nb[1]

            @pl.when(has_right)
            def _():
                nb[3] += nb[1]
                to_right.start()

        @pl.when(has_right)
        def _():
            to_left.wait_recv()
            nb[5] += nb[2]

            @pl.when(has_left)
            def _():
                nb[4] += nb[2]
                to_left.start()

        self.norm_copy(5, 6, self.partner).start()

    def finish_norms(self, norm_out, norm3_out):
        nb = self.nb
        self.norm_copy(5, 6, self.partner).wait()

        @pl.when(self.has_right)
        def _():
            self.norm_copy(3, 1, self.right).wait_send()

        @pl.when(self.has_left)
        def _():
            self.norm_copy(4, 2, self.left).wait_send()

        nb[7] = nb[5] + nb[6]
        hand = self.norm_copy(7, 8, self.across)

        @pl.when(self.decoder)
        def _():
            hand.start()
            nb[8] = nb[7]

        norm_out[...] = nb[7, :, pl.ds(pl.multiple_of(self.dp * 128, 128), 128)]

        @pl.when(self.encoder)
        def _():
            hand.wait_recv()

        place = self.section * self.line * 2 + self.dp
        block = nb[8, :, pl.ds(pl.multiple_of(place // 2 * 128, 128), 128)]
        norm3_out[...] = jnp.where(self.y == 0, block, pltpu.roll(block, 64, 1))

        @pl.when(self.decoder)
        def _():
            hand.wait_send()

    def run(self, sums, norm_out, norm3_out):
        self.start_norms(sums)
        first = jnp.where(self.decoder, 6, 4)
        lax.fori_loop(first, self.AHEAD, lambda j, carry: (self.pair_step(j), carry)[1], 0)
        self.cross_part()

        def step(t, carry):
            self.line_step(t)

            @pl.when(t == 8)
            def _():
                self.middle_norms()

            @pl.when(t == self.positions - 1)
            def _():
                self.finish_norms(norm_out, norm3_out)

            return carry

        lax.fori_loop(jnp.where(self.decoder, 6, 4), self.positions + self.line - 1, step, 0)

    def drain(self):
        @pl.when(self.decoder)
        def _():
            for e in range(2):
                self.late_copy(e).wait()
                self.final_copy(e).wait()
                slot = self.final_slot(e)
                slot[...] = self.late_acc[e] + self.late_got[e].astype(F32)
                self.final_copy(e).start()

        for slot in range(self.AHEAD):
            for k in range(self.line):
                self.pair_copy(slot, k).wait_send()

        for slot in range(self.DEPTH):
            for k in range(self.line):

                @pl.when(self.z != k)
                def _():
                    self.line_copy(0, slot, k, 0).wait_send()

        for slot in range(self.FINAL):
            self.final_copy(slot).wait()

        @pl.when(self.decoder)
        def _():
            for q in range(4):
                self.cross_copy(q).wait_send()


def layer_kernel(
    sections,
    ring,
    inputs,
    targets,
    cotangent,
    counts,
    qkv_hbm,
    out_hbm,
    gain1,
    bias1,
    up_hbm,
    down_hbm,
    gain2,
    bias2,
    cross_hbm,
    cross_out_hbm,
    gain3,
    bias3,
    seg_out,
    in_grad,
    norm_out,
    first_out,
    second_out,
    w_qkv,
    w_out,
    w_up,
    w_down,
    w_cross,
    w_cross_out,
    a_fac,
    b_fac,
    proj,
    cross_proj,
    unit1,
    held,
    unit3,
    scale1,
    scale2,
    scale3,
    resid,
    slope,
    d_mix,
    sent,
    got,
    half_send,
    half_got,
    spare,
    low_out,
    sums,
    load_sem,
    x_sem,
    ex_send,
    ex_recv,
    hop_send,
    hop_recv,
    out_sem,
    *share,
):
    section = lax.axis_index("section")
    dp = lax.axis_index("dp")
    core = lax.axis_index("mp")
    decoder = section == sections - 1
    encoder = section != sections - 1
    mate = (section, dp, 1 - core)
    across = (1 - section, dp, core)
    half = seg_out.shape[2]
    slot = 2 * half
    limit = jnp.where(decoder, 0, slot)
    width = w_up.shape[1]
    parts = width // CHUNK
    two, three = jnp.where(decoder, 0, 1), jnp.where(decoder, 1, 0)
    own = core * half
    other = (1 - core) * half

    d_branch, crossed, d_attn, layer_in, normed_low, memory, d_cross = (a_fac.at[i] for i in range(7))
    act = b_fac.at[0:parts]
    d_hidden = b_fac.at[parts : 2 * parts]
    mixed = b_fac.at[2 * parts]
    d_proj = b_fac.at[2 * parts + 1 : 2 * parts + 4]
    d_cross_proj = b_fac.at[2 * parts + 4 : 2 * parts + 7]
    cross_mixed = b_fac.at[2 * parts + 7]

    unit2, d_out = held.at[0], held.at[1]

    def rows_of(m):
        return pl.ds(pl.multiple_of(m * slot, slot), slot)

    def half_of(m, offset):
        return pl.ds(pl.multiple_of(m * slot + offset, half), half)

    def strip_of(m, k):
        return pl.ds(pl.multiple_of(m * slot + k * STRIP, STRIP), STRIP)

    def strips(body):
        for k in range(slot // STRIP):
            body(k)

    barrier = pltpu.get_barrier_semaphore()
    for device in (mate, across):
        pl.semaphore_signal(barrier, inc=1, device_id=device, device_id_type=MESH)
    if ring:
        total = GradientShare(
            ring, section, dp, core, decoder, a_fac, b_fac, first_out, w_up, w_down, held, slope, resid, spare, *share
        )
        greeted = 2 + total.greet(barrier)
    else:
        greeted = 2

    loads = [
        pltpu.make_async_copy(src, dst, load_sem.at[i])
        for i, (src, dst) in enumerate(
            (
                (qkv_hbm.at[0], w_qkv),
                (out_hbm.at[0], w_out),
                (up_hbm.at[0], w_up),
                (down_hbm.at[0], w_down),
                (cross_hbm, w_cross),
                (cross_out_hbm, w_cross_out),
            )
        )
    ]

    def local_rows(src, dst, m, sem):
        return pltpu.make_async_copy(src.at[m], dst.at[half_of(m, own)], sem)

    def mate_rows(src, dst, m, send, recv):
        return pltpu.make_async_remote_copy(
            src_ref=src.at[m],
            dst_ref=dst.at[half_of(m, own)],
            send_sem=send,
            recv_sem=recv,
            device_id=mate,
            device_id_type=MESH,
        )

    def start_rows(src, dst, base):
        for m in range(2):
            local_rows(src, dst, m, x_sem.at[base + m]).start()
        for m in range(2):
            mate_rows(src, dst, m, x_sem.at[base + 2 + m], x_sem.at[base + 4 + m]).start()

    def wait_rows(src, dst, base, m):
        local_rows(src, dst, m, x_sem.at[base + m]).wait()
        mate_rows(src, dst, m, x_sem.at[base + 2 + m], x_sem.at[base + 4 + m]).wait()

    @pl.when(encoder)
    def _():
        for m in range(2):
            local_rows(inputs, layer_in, m, x_sem.at[m]).start()

    @pl.when(decoder)
    def _():
        for m in range(2):
            local_rows(targets, layer_in, m, x_sem.at[m]).start()

    loads[0].start()
    loads[1].start()
    pl.semaphore_wait(barrier, greeted)

    def mate_start(src, dst, base):
        for m in range(2):
            mate_rows(src, dst, m, x_sem.at[base + 2 + m], x_sem.at[base + 4 + m]).start()

    @pl.when(encoder)
    def _():
        mate_start(inputs, layer_in, 0)

    @pl.when(decoder)
    def _():
        mate_start(targets, layer_in, 0)

    for copy in loads[2:]:
        copy.start()

    @pl.when(decoder)
    def _():
        start_rows(cotangent, d_out, 6)

    sums[...] = jnp.zeros_like(sums)

    def exchange(which, buffer, m):
        return pltpu.make_async_remote_copy(
            src_ref=sent.at[rows_of(m)],
            dst_ref=got.at[buffer, rows_of(m)],
            send_sem=ex_send.at[which, m],
            recv_sem=ex_recv.at[which, m],
            device_id=mate,
            device_id_type=MESH,
        )

    def half_exchange(which, m):
        return pltpu.make_async_remote_copy(
            src_ref=half_send.at[which, m],
            dst_ref=half_got.at[which, m],
            send_sem=hop_send.at[4 + which, m],
            recv_sem=hop_recv.at[4 + which, m],
            device_id=mate,
            device_id_type=MESH,
        )

    def across_copy(src, dst, which, m):
        return pltpu.make_async_remote_copy(
            src_ref=src,
            dst_ref=dst.at[half_of(m, own)],
            send_sem=hop_send.at[which, m],
            recv_sem=hop_recv.at[which, m],
            device_id=across,
            device_id_type=MESH,
        )

    def forward_copy(ref, which, m):
        return pltpu.make_async_remote_copy(
            src_ref=ref.at[half_of(m, own)],
            dst_ref=ref.at[half_of(m, own)],
            send_sem=hop_send.at[which, m],
            recv_sem=hop_recv.at[which, m],
            device_id=mate,
            device_id_type=MESH,
        )

    def project_out(value, weight, m):
        for n in range(sent.shape[1] // CHUNK):
            cols = slice(n * CHUNK, (n + 1) * CHUNK)
            sent[rows_of(m), cols] = dot_nt(value, weight[cols, :]).astype(BF)

    def summed(buffer, strip):
        return sent[strip].astype(F32) + got[buffer, strip].astype(F32)

    loads[0].wait()

    def attention_in(m):
        @pl.when(encoder)
        def _():
            wait_rows(inputs, layer_in, 0, m)

        @pl.when(decoder)
        def _():
            wait_rows(targets, layer_in, 0, m)

        rows = rows_of(m)
        for t in range(3):
            proj[t, rows] = dot_nn(layer_in[rows], w_qkv[t]).astype(BF)
        attend_forward(proj, mixed, rows, limit)
        project_out(mixed[rows], w_out, m)
        exchange(0, 0, m).start()

    loads[1].wait()
    loop(2, attention_in)
    for copy in loads[2:]:
        copy.wait()

    def after_attention(m):
        exchange(0, 0, m).wait()

        def norm(k):
            strip = strip_of(m, k)
            unit, scale, value = norm_forward(
                layer_in[strip].astype(F32) + summed(0, strip), gain1[...], bias1[...]
            )
            unit1[strip] = unit.astype(BF)
            scale1[strip] = scale
            resid[strip] = value
            low_out[pl.ds(k * STRIP, STRIP)] = value.astype(BF)
            crossed[strip] = value.astype(BF)

        strips(norm)

        @pl.when(decoder)
        def _():
            rows = rows_of(m)
            normed_low[rows] = low_out[...]
            cross_proj[0, rows] = dot_nn(low_out[...], w_cross[0]).astype(BF)
            across_copy(seg_out.at[0, m], memory, 0, m).wait_recv()
            forward_copy(memory, 1, m).start()
            forward_copy(memory, 1, m).wait()
            for t in range(1, 3):
                cross_proj[t, rows] = dot_nn(memory[rows], w_cross[t]).astype(BF)
            attend_forward(cross_proj, cross_mixed, rows, None)
            project_out(cross_mixed[rows], w_cross_out, m)
            exchange(1, 1, m).start()


    def feed_forward(m):
        rows = rows_of(m)

        @pl.when(decoder)
        def _():
            exchange(1, 1, m).wait()

            def norm(k):
                strip = strip_of(m, k)
                unit, scale, value = norm_forward(
                    resid[strip] + summed(1, strip), gain3[...], bias3[...]
                )
                unit3[strip] = unit.astype(BF)
                scale3[strip] = scale
                resid[strip] = value
                crossed[strip] = value.astype(BF)

            strips(norm)

        for n in range(parts):
            pre = dot_nn(crossed[rows], w_up[:, n * CHUNK : (n + 1) * CHUNK])
            rise = 0.5 + 0.5 * lax.erf(pre * (0.5**0.5))
            act[n, rows] = (pre * rise).astype(BF)
            slope[n, rows] = (rise + pre * jnp.exp(-0.5 * pre * pre) * 0.3989422804014327).astype(BF)
        if ring:
            total.send_act(m)
        project_out(jnp.concatenate([act[n, rows] for n in range(parts)], 1), w_down, m)
        exchange(2, two, m).start()


    def finish_forward(m):
        exchange(2, two, m).wait()

        def norm(k):
            strip = strip_of(m, k)
            unit, scale, value = norm_forward(
                resid[strip] + summed(two, strip), gain2[...], bias2[...]
            )
            unit2[strip] = unit.astype(BF)
            scale2[strip] = scale
            low_out[pl.ds(k * STRIP, STRIP)] = value.astype(BF)

        strips(norm)
        seg_out[0, m] = low_out[pl.ds(pl.multiple_of(own, half), half)]

        @pl.when(encoder)
        def _():
            across_copy(seg_out.at[0, m], memory, 0, m).start()

    def forward_parts(m):
        after_attention(m)

        @pl.when(m == 1)
        def _():
            finish_forward(0)

        feed_forward(m)

    loop(2, forward_parts)
    finish_forward(1)

    question = dp // QSLOTS
    spot = dp - question * QSLOTS

    def feed_backward(m):
        rows = rows_of(m)

        @pl.when(encoder)
        def _():
            across_copy(half_send.at[0, m], d_out, 2, m).wait_recv()
            forward_copy(d_out, 3, m).start()
            forward_copy(d_out, 3, m).wait()

        @pl.when(decoder)
        def _():
            wait_rows(cotangent, d_out, 6, m)

        keep = jnp.where(spot < counts[m, question], 1.0, 0.0)
        keep = jnp.where(decoder, keep, 1.0)

        def norm(k):
            strip = strip_of(m, k)
            grad = norm_backward(
                d_out[strip].astype(F32) * keep,
                unit2[strip].astype(F32),
                scale2[strip],
                gain2[...],
                sums,
                2,
            )
            resid[strip] = grad
            d_branch[strip] = grad.astype(BF)

        strips(norm)
        if ring:
            total.send_branch(m)
        for n in range(parts):
            grad = dot_nn(d_branch[rows], w_down[:, n * CHUNK : (n + 1) * CHUNK])
            d_hidden[n, rows] = (grad * slope[n, rows].astype(F32)).astype(BF)
        project_out(jnp.concatenate([d_hidden[n, rows] for n in range(parts)], 1), w_up, m)
        exchange(3, three, m).start()

    loop(2, feed_backward)
    if ring:
        total.begin()

    def cross_backward(m):
        rows = rows_of(m)

        def norm(k):
            strip = strip_of(m, k)
            grad = norm_backward(
                resid[strip] + summed(three, strip),
                unit3[strip].astype(F32),
                scale3[strip],
                gain3[...],
                sums,
                4,
            )
            resid[strip] = grad
            d_cross[strip] = grad.astype(BF)

        strips(norm)
        d_mix[rows] = dot_nn(d_cross[rows], w_cross_out[...]).astype(BF)
        attend_backward(cross_proj, d_mix, d_cross_proj, rows, None)

        def memory_part(offset):
            piece = half_of(m, offset)
            return jnp.concatenate([d_cross_proj[1, piece], d_cross_proj[2, piece]], 1)

        def memory_weight(n):
            cols = slice(n * CHUNK, (n + 1) * CHUNK)
            return jnp.concatenate([w_cross[1, cols], w_cross[2, cols]], 1)

        for n in range(sent.shape[1] // CHUNK):
            cols = slice(n * CHUNK, (n + 1) * CHUNK)
            half_send[0, m, :, cols] = dot_nt(memory_part(other), memory_weight(n)).astype(BF)
        half_exchange(0, m).start()
        for n in range(sent.shape[1] // CHUNK):
            cols = slice(n * CHUNK, (n + 1) * CHUNK)
            spare[n] = dot_nt(memory_part(own), memory_weight(n))
        project_out(d_cross_proj[0, rows], w_cross[0], m)
        exchange(4, 0, m).start()
        half_exchange(0, m).wait()
        for n in range(sent.shape[1] // CHUNK):
            cols = slice(n * CHUNK, (n + 1) * CHUNK)
            half_send[0, m, :, cols] = (spare[n] + half_got[0, m, :, cols].astype(F32)).astype(BF)
        across_copy(half_send.at[0, m], d_out, 2, m).start()

    def attention_back(m):
        rows = rows_of(m)

        def norm_rows(buffer):
            def norm(k):
                strip = strip_of(m, k)
                grad = norm_backward(
                    resid[strip] + summed(buffer, strip),
                    unit1[strip].astype(F32),
                    scale1[strip],
                    gain1[...],
                    sums,
                    0,
                )
                resid[strip] = grad
                d_attn[strip] = grad.astype(BF)

            strips(norm)

        @pl.when(decoder)
        def _():
            exchange(4, 0, m).wait()

        @pl.when(encoder)
        def _():
            exchange(3, three, m).wait()

        norm_rows(0)
        d_mix[rows] = dot_nn(d_attn[rows], w_out[...]).astype(BF)
        attend_backward(proj, d_mix, d_proj, rows, limit)

        if ring:
            total.middle(m)

        def input_part(offset):
            piece = half_of(m, offset)
            return jnp.concatenate([d_proj[t, piece] for t in range(3)], 1)

        def input_weight(n):
            cols = slice(n * CHUNK, (n + 1) * CHUNK)
            return jnp.concatenate([w_qkv[t, cols] for t in range(3)], 1)

        for n in range(sent.shape[1] // CHUNK):
            cols = slice(n * CHUNK, (n + 1) * CHUNK)
            half_send[1, m, :, cols] = dot_nt(input_part(other), input_weight(n)).astype(BF)
        half_exchange(1, m).start()
        for n in range(sent.shape[1] // CHUNK):
            cols = slice(n * CHUNK, (n + 1) * CHUNK)
            resid[half_of(m, own), cols] += dot_nt(input_part(own), input_weight(n))

    @pl.when(decoder)
    def _():
        def both(m):
            if ring:
                total.between(m)
            exchange(3, three, m).wait()
            cross_backward(m)

        loop(2, both)

    def last_part(m):
        if ring:
            total.before(m)
        attention_back(m)

    loop(2, last_part)

    def finish_backward(m):
        half_exchange(1, m).wait()
        in_grad[0, m] = (
            resid[half_of(m, own)] + half_got[1, m].astype(F32)
        ).astype(BF)

    loop(2, finish_backward)

    @pl.when(encoder)
    def _():
        for m in range(2):
            across_copy(seg_out.at[0, m], memory, 0, m).wait_send()

    @pl.when(decoder)
    def _():
        for m in range(2):
            across_copy(half_send.at[0, m], d_out, 2, m).wait_send()

    if ring:
        total.run(sums, norm_out, second_out)
        total.drain()
        return

    for i in range(6):
        norm_out[i : i + 1] = jnp.sum(sums[i], 0, keepdims=True)
    norm_out[6:8] = jnp.zeros_like(norm_out[6:8])
    copies = [
        pltpu.make_async_copy(a_fac, first_out, out_sem.at[0]),
        pltpu.make_async_copy(b_fac, second_out, out_sem.at[1]),
    ]
    for copy in copies:
        copy.start()
    for copy in copies:
        copy.wait()


def unpack_kernel(parts, seg, grads, norms, tiles, norm3, *outs):
    (seg_out, in_grad, qkv, proj_out, gain1, bias1, up, down, gain2, bias2, cross, cross_out, gain3, bias3,
     rows16, rows32, come, go) = outs
    rows = tiles.shape[1]
    small = rows // 2
    moves = [(seg.at[0], rows16.at[0], seg_out.at[0]), (grads.at[0], rows16.at[1], in_grad.at[0])]
    whole = [down.at[0, :, n * CHUNK : (n + 1) * CHUNK] for n in range(parts)]
    whole += [up.at[0, :, n * CHUNK : (n + 1) * CHUNK] for n in range(parts)]
    whole += [proj_out.at[0]] + [qkv.at[0, t] for t in range(3)]
    for n, target in enumerate(whole):
        moves.append((tiles.at[n], rows32.at[n], target))
    for q in range(4):
        n, half = 2 * parts + 4 + q // 2, pl.ds(q % 2 * small, small)
        moves.append((tiles.at[n, half], rows32.at[n, half], cross.at[q] if q < 3 else cross_out))
    first = [pltpu.make_async_copy(src, mid, come.at[i]) for i, (src, mid, dst) in enumerate(moves)]
    second = [pltpu.make_async_copy(mid, dst, go.at[i]) for i, (src, mid, dst) in enumerate(moves)]
    for copy in first:
        copy.start()
    for i, ref in enumerate((gain1, bias1, gain2, bias2)):
        ref[...] = norms[i : i + 1]
    gain3[...] = norm3[4:5, :small]
    bias3[...] = norm3[5:6, :small]
    for a, b in zip(first, second):
        a.wait()
        b.start()
    for copy in second:
        copy.wait()


def body(
    sections,
    ring,
    inputs,
    target_inputs,
    cotangent,
    slot_counts,
    w_qkv,
    w_out,
    norm1_gain,
    norm1_bias,
    w_up,
    w_down,
    norm2_gain,
    norm2_bias,
    cross_qkv,
    cross_out,
    norm3_gain,
    norm3_bias,
):
    micro, half, depth = inputs.shape
    rows = micro * 2 * half
    heads = w_out.shape[2]
    width = w_up.shape[2]
    parts = width // CHUNK
    chunks = 2 * parts + 8
    hbm = pl.BlockSpec(memory_space=pl.ANY)
    vmem = pl.BlockSpec(memory_space=VM)
    smem = pl.BlockSpec(memory_space=pltpu.SMEM)
    shape = jax.ShapeDtypeStruct
    if ring:
        results = (
            shape((8, depth // ring), F32),
            shape((chunks - 2, depth // ring, CHUNK), F32),
            shape((8, depth // ring), F32),
        )
        places = (vmem, hbm, vmem)
    else:
        results = (
            shape((8, depth), F32),
            shape((7, rows, depth), BF),
            shape((chunks, rows, CHUNK), BF),
        )
        places = (vmem, hbm, hbm)
    dma = pltpu.SemaphoreType.DMA
    regular = pltpu.SemaphoreType.REGULAR
    tile = (depth // ring, CHUNK) if ring else None
    share = (
        [
            VM((GradientShare.AHEAD * 4,) + tile, BF),
            VM((9, 8, depth), F32),
            VM((2,) + tile, BF),
            VM((2,) + tile, BF),
            VM((2,) + tile, F32),
            dma((GradientShare.AHEAD * 4,)),
            dma((GradientShare.AHEAD * 4,)),
            dma((GradientShare.DEPTH * 4,)),
            dma((GradientShare.WINDOW * 5,)),
            dma((4,)),
            dma((4,)),
            dma((9,)),
            dma((9,)),
            dma((2,)),
            dma((2,)),
            dma((13,)),
            dma((13,)),
            dma((GradientShare.FINAL,)),
            regular,
            regular,
            regular,
            regular,
        ]
        if ring
        else []
    )
    seg_out, in_grad, norms, first, second = pl.pallas_call(
        functools.partial(layer_kernel, sections, ring),
        out_shape=(
            shape((1, micro, half, depth), BF),
            shape((1, micro, half, depth), BF),
        )
        + results,
        in_specs=[hbm, hbm, hbm, smem, hbm, hbm, vmem, vmem, hbm, hbm, vmem, vmem, hbm, hbm, vmem, vmem],
        out_specs=(vmem, vmem) + places,
        scratch_shapes=[
            VM((3, depth, heads), BF),
            VM((depth, heads), BF),
            VM((depth, width), BF),
            VM((depth, width), BF),
            VM((3, depth, heads), BF),
            VM((depth, heads), BF),
            VM((7, rows, depth), BF),
            VM((chunks, rows, CHUNK), BF),
            VM((3, rows, heads), BF),
            VM((3, rows, heads), BF),
            VM((rows, depth), BF),
            VM((2, rows, depth), BF),
            VM((rows, depth), BF),
            VM((rows, 1), F32),
            VM((rows, 1), F32),
            VM((rows, 1), F32),
            VM((rows, depth), F32),
            VM((parts, rows, CHUNK), BF),
            VM((rows, heads), BF),
            VM((rows, depth), BF),
            VM((2, rows, depth), BF),
            VM((2, micro, half, depth), BF),
            VM((2, micro, half, depth), BF),
            VM((4, half, CHUNK), F32),
            VM((2 * half, depth), BF),
            VM((6, 8, depth), F32),
            pltpu.SemaphoreType.DMA((6,)),
            pltpu.SemaphoreType.DMA((12,)),
            pltpu.SemaphoreType.DMA((5, micro)),
            pltpu.SemaphoreType.DMA((5, micro)),
            pltpu.SemaphoreType.DMA((6, micro)),
            pltpu.SemaphoreType.DMA((6, micro)),
            pltpu.SemaphoreType.DMA((2,)),
        ]
        + share,
        compiler_params=pltpu.CompilerParams(
            collective_id=0, has_side_effects=True, vmem_limit_bytes=60 * 2**20
        ),
        name="layers",
    )(
        inputs,
        target_inputs,
        cotangent,
        slot_counts,
        w_qkv,
        w_out,
        norm1_gain,
        norm1_bias,
        w_up,
        w_down,
        norm2_gain,
        norm2_bias,
        cross_qkv,
        cross_out,
        norm3_gain[None],
        norm3_bias[None],
    )
    if ring:
        lanes = depth // ring
        row = shape((1, lanes), F32)
        small = shape((1, lanes // 2), F32)
        outs = pl.pallas_call(
            functools.partial(unpack_kernel, parts),
            out_shape=(
                shape(seg_out.shape, BF),
                shape(in_grad.shape, BF),
                shape((1, 3, lanes, heads), F32),
                shape((1, lanes, heads), F32),
                row,
                row,
                shape((1, lanes, width), F32),
                shape((1, lanes, width), F32),
                row,
                row,
                shape((3, lanes // 2, heads), F32),
                shape((lanes // 2, heads), F32),
                small,
                small,
            ),
            in_specs=[hbm, hbm, vmem, hbm, vmem],
            out_specs=(hbm, hbm, hbm, hbm, vmem, vmem, hbm, hbm, vmem, vmem, hbm, hbm, vmem, vmem),
            scratch_shapes=[
                VM((2, micro, half, depth), BF),
                VM((chunks - 2, lanes, CHUNK), F32),
                dma((2 * parts + 10,)),
                dma((2 * parts + 10,)),
            ],
            name="unpack",
        )(seg_out, in_grad, norms, first, second)
        return outs[:12] + (outs[12][0], outs[13][0])
    a_fac, b_fac = first, second
    decoder = lax.axis_index("section") == sections - 1

    def weight_grad(left, first, count):
        return jnp.einsum(
            "nd,tnc->tdc", a_fac[left], b_fac[first : first + count], preferred_element_type=F32
        ).astype(BF)

    def shared(grad, axes, dim):
        return lax.psum_scatter(grad, axes, scatter_dimension=dim, tiled=True)

    def wide(grad):
        return jnp.swapaxes(grad, 0, 1).reshape(depth, -1)

    grad_down = shared(wide(weight_grad(0, 0, parts)), "dp", 0)
    grad_up = shared(wide(weight_grad(1, parts, parts)), "dp", 0)
    grad_out = shared(weight_grad(2, 2 * parts, 1)[0], "dp", 0)
    grad_qkv = shared(weight_grad(3, 2 * parts + 1, 3), "dp", 1)
    cross = jnp.concatenate(
        [
            weight_grad(4, 2 * parts + 4, 1),
            weight_grad(5, 2 * parts + 5, 2),
            weight_grad(6, 2 * parts + 7, 1),
        ],
        0,
    )
    cross = shared(jnp.where(decoder, cross, jnp.zeros_like(cross)), ("section", "dp"), 1)
    small = shared(norms[:4], "dp", 1)
    norm3 = jnp.where(decoder, norms[4:6], jnp.zeros_like(norms[4:6]))
    norm3 = shared(norm3, ("section", "dp"), 1)
    return (
        seg_out,
        in_grad,
        grad_qkv[None].astype(F32),
        grad_out[None].astype(F32),
        small[0:1],
        small[1:2],
        grad_up[None].astype(F32),
        grad_down[None].astype(F32),
        small[2:3],
        small[3:4],
        cross[:3].astype(F32),
        cross[3].astype(F32),
        norm3[0],
        norm3[1],
    )


def solution(mesh):
    ring = 8 if mesh.shape["dp"] == 8 else 0
    return jax.shard_map(
        functools.partial(body, mesh.shape["section"], ring),
        mesh=mesh,
        in_specs=(
            P(None, ("dp", "mp"), None),
            P(None, ("dp", "mp"), None),
            P(None, ("dp", "mp"), None),
            P(),
            P("section", None, None, "mp"),
            P("section", None, "mp"),
            P("section", None),
            P("section", None),
            P("section", None, "mp"),
            P("section", None, "mp"),
            P("section", None),
            P("section", None),
            P(None, None, "mp"),
            P(None, "mp"),
            P(),
            P(),
        ),
        out_specs=(
            P("section", None, ("dp", "mp"), None),
            P("section", None, ("dp", "mp"), None),
            P("section", None, "dp", "mp"),
            P("section", "dp", "mp"),
            P("section", "dp"),
            P("section", "dp"),
            P("section", "dp", "mp"),
            P("section", "dp", "mp"),
            P("section", "dp"),
            P("section", "dp"),
            P(None, ("section", "dp"), "mp"),
            P(("section", "dp"), "mp"),
            P(("section", "dp")),
            P(("section", "dp")),
        ),
        check_vma=False,
    )
```

```python
import functools

import jax
import jax.numpy as jnp
from jax import lax
from jax.experimental import pallas as pl
from jax.experimental.pallas import tpu as pltpu
from jax.sharding import PartitionSpec as P

HEAD = 64
SLOT = 256
QSLOTS = 4
CHUNK = 512
PAIR = 2 * HEAD
STRIP = 64
EPS = 1e-5
NEG = -1000000000.0
MESH = pl.DeviceIdType.MESH
BF = jnp.bfloat16
F32 = jnp.float32
VM = pltpu.VMEM


def dot_nn(a, b):
    return lax.dot_general(a, b, (((1,), (0,)), ((), ())), preferred_element_type=F32)


def dot_nt(a, b):
    return lax.dot_general(a, b, (((1,), (1,)), ((), ())), preferred_element_type=F32)


def dot_tn(a, b):
    return lax.dot_general(a, b, (((0,), (0,)), ((), ())), preferred_element_type=F32)


def loop(count, body):
    def step(i, carry):
        body(i)
        return carry

    lax.fori_loop(0, count, step, 0)


def head_masks():
    lane = lax.broadcasted_iota(jnp.int32, (1, PAIR), 1)
    first = jnp.where(lane < HEAD, 1.0, 0.0).astype(BF)
    second = jnp.where(lane < HEAD, 0.0, 1.0).astype(BF)
    return first, second


def expos_of(query, keys, mask, limit):
    scores = dot_nt(keys, query * (mask * (HEAD**-0.5)).astype(BF))
    if limit is not None:
        key = lax.broadcasted_iota(jnp.int32, scores.shape, 0)
        place = lax.broadcasted_iota(jnp.int32, scores.shape, 1)
        scores = jnp.where(place + limit >= key, scores, NEG)
    expo = jnp.exp(scores - jnp.max(scores, 0, keepdims=True))
    return expo, 1.0 / jnp.sum(expo, 0, keepdims=True)


def attend_forward(proj, mixed, rows, limit):
    masks = head_masks()
    for j in range(CHUNK // PAIR):
        lanes = slice(j * PAIR, (j + 1) * PAIR)
        query, keys, values = proj[0, rows, lanes], proj[1, rows, lanes], proj[2, rows, lanes]
        low = []
        for mask in masks:
            expo, share = expos_of(query, keys, mask, limit)
            low.append((expo * share).astype(BF))
        turned = dot_tn(jnp.concatenate([values * mask for mask in masks], 0), jnp.concatenate(low, 0))
        mixed[rows, lanes] = turned.T.astype(BF)


def attend_backward(proj, d_mixed, d_proj, rows, limit):
    masks = head_masks()
    scale = HEAD**-0.5
    for j in range(CHUNK // PAIR):
        lanes = slice(j * PAIR, (j + 1) * PAIR)
        query, keys, values = proj[0, rows, lanes], proj[1, rows, lanes], proj[2, rows, lanes]
        grad = d_mixed[rows, lanes]
        low, d_scores = [], []
        for mask in masks:
            expo, share = expos_of(query, keys, mask, limit)
            weights = expo * share
            d_weights = dot_nt(values, grad * mask)
            inner = jnp.sum(weights * d_weights, 0, keepdims=True)
            d_scores.append((weights * (d_weights - inner)).astype(BF))
            low.append(weights.astype(BF))
        d_proj[2, rows, lanes] = dot_nn(
            jnp.concatenate(low, 1), jnp.concatenate([grad * mask for mask in masks], 0)
        ).astype(BF)
        d_proj[1, rows, lanes] = (
            dot_nn(
                jnp.concatenate(d_scores, 1), jnp.concatenate([query * mask for mask in masks], 0)
            )
            * scale
        ).astype(BF)
        turned = dot_tn(
            jnp.concatenate([keys * mask for mask in masks], 0), jnp.concatenate(d_scores, 0)
        )
        d_proj[0, rows, lanes] = (turned.T * scale).astype(BF)


def norm_forward(value, gain, bias):
    center = value - jnp.mean(value, -1, keepdims=True)
    scale = lax.rsqrt(jnp.mean(center * center, -1, keepdims=True) + EPS)
    unit = center * scale
    return unit, scale, unit * gain + bias


def norm_backward(grad, unit, scale, gain, sums, which):
    fold = lambda v: jnp.sum(v.reshape(v.shape[0] // 8, 8, v.shape[1]), 0)
    sums[which] += fold(grad * unit)
    sums[which + 1] += fold(grad)
    d_unit = grad * gain
    first = jnp.mean(d_unit, -1, keepdims=True)
    second = jnp.mean(d_unit * unit, -1, keepdims=True)
    return scale * (d_unit - first - unit * second)


class GradientShare:
    AHEAD = 8
    WINDOW = 6
    DEPTH = 4
    FINAL = 8
    PIECES = 2
    EARLY = 4

    def __init__(self, size, section, dp, core, decoder, a_fac, b_fac, tiles, w_up, w_down, held, slope, resid, acc, *share):
        self.acc = acc
        (self.pair_got, self.nb, self.late_sent, self.late_got, self.late_acc, self.pair_send,
         self.pair_recv, self.line_send, self.line_recv, self.cross_send, self.cross_recv, self.norm_send,
         self.norm_recv, self.late_send, self.late_recv, self.factor_send, self.factor_recv, self.final_sem,
         self.pair_credit, self.left_credit, self.right_credit, self.cross_credit) = share
        self.line = size // 2
        self.section, self.dp, self.core = section, dp, core
        self.decoder, self.encoder = decoder, jnp.logical_not(decoder)
        self.z, self.y = dp // 2, lax.rem(dp, 2)
        self.a_fac, self.b_fac, self.tiles = a_fac, b_fac, tiles
        self.w_up, self.w_down, self.held, self.slope, self.resid = w_up, w_down, held, slope, resid
        self.rows = a_fac.shape[2] // size
        self.own_chunks = b_fac.shape[0] - 4
        self.positions = self.own_chunks + 2 + jnp.where(decoder, 2, 0)
        self.pairs = self.positions - self.EARLY
        self.partner = (section, dp + 1 - 2 * self.y, core)
        self.right = (section, dp + 2, core)
        self.left = (section, dp - 2, core)
        self.across = (1 - section, dp, core)
        self.mate = (section, dp, 1 - core)
        self.has_left, self.has_right = self.z > 0, self.z < self.line - 1

    def greet(self, barrier):
        pl.semaphore_signal(barrier, inc=1, device_id=self.partner, device_id_type=MESH)

        @pl.when(self.has_left)
        def _():
            pl.semaphore_signal(barrier, inc=1, device_id=self.left, device_id_type=MESH)

        @pl.when(self.has_right)
        def _():
            pl.semaphore_signal(barrier, inc=1, device_id=self.right, device_id_type=MESH)

        return 1 + jnp.where(self.has_left, 1, 0) + jnp.where(self.has_right, 1, 0)

    def remote(self, src, dst, send, recv, device):
        return pltpu.make_async_remote_copy(
            src_ref=src, dst_ref=dst, send_sem=send, recv_sem=recv, device_id=device, device_id_type=MESH
        )

    def tile_rows(self, k):
        return pl.ds(pl.multiple_of(k * self.rows, self.rows), self.rows)

    def cols(self, k):
        return pl.ds(pl.multiple_of(k * CHUNK, CHUNK), CHUNK)

    def pair_slot(self, j, k):
        return self.w_down.at[self.tile_rows(lax.rem(j, self.AHEAD)), self.cols(k)]

    def pair_copy(self, j, k):
        slot = lax.rem(j, self.AHEAD) * self.line + k
        return self.remote(
            self.pair_slot(j, k), self.pair_got.at[slot], self.pair_send.at[slot], self.pair_recv.at[slot], self.partner
        )

    def line_slot(self, p, k):
        slot = lax.rem(p, self.DEPTH) * self.line + k
        return self.held.at[slot // 8, self.tile_rows(lax.rem(slot, 4)), self.cols(lax.rem(slot // 4, 2))]

    def line_place(self, side, p, k, z):
        return lax.rem(p, self.WINDOW) * (self.line + 1) + (self.line - z + k if side else k - z)

    def line_got(self, place):
        return self.w_up.at[self.tile_rows(place // 4), self.cols(lax.rem(place, 4))]

    def piece(self, h):
        return pl.ds(h * (self.rows // self.PIECES), self.rows // self.PIECES)

    def line_copy(self, side, p, k, receiver, h):
        place = self.line_place(side, p, k, receiver)
        return self.remote(
            self.line_slot(p, k).at[self.piece(h)],
            self.line_got(place).at[self.piece(h)],
            self.line_send.at[lax.rem(p, self.DEPTH) * self.line + k, h],
            self.line_recv.at[place, h],
            self.left if side else self.right,
        )

    def cross_copy(self, q):
        return self.remote(
            self.slope.at[q], self.slope.at[q], self.cross_send.at[q], self.cross_recv.at[q], self.across
        )

    def late_copy(self, e):
        return self.remote(
            self.late_sent.at[e], self.late_got.at[e], self.late_send.at[e], self.late_recv.at[e], self.partner
        )

    def act_copy(self, n, m):
        rows = pl.ds(pl.multiple_of(m * SLOT, SLOT), SLOT)
        return self.remote(
            self.b_fac.at[n, rows],
            self.a_fac.at[5 + n // 2, rows, pl.ds(n % 2 * CHUNK, CHUNK)],
            self.factor_send.at[n * 2 + m],
            self.factor_recv.at[n * 2 + m],
            self.partner,
        )

    def branch_copy(self, k):
        rows = pl.ds(pl.multiple_of(self.core * SLOT, SLOT), SLOT)
        return self.remote(
            self.a_fac.at[0, rows, self.tile_rows(k * 2 + 1 - self.y)],
            self.a_fac.at[4, rows, pl.ds(k * self.rows, self.rows)],
            self.factor_send.at[8 + k],
            self.factor_recv.at[8 + k],
            self.partner,
        )

    def branch_forward(self):
        rows = pl.ds(pl.multiple_of(self.core * SLOT, SLOT), SLOT)
        part = self.a_fac.at[4, rows, pl.ds(0, CHUNK)]
        return self.remote(part, part, self.factor_send.at[12], self.factor_recv.at[12], self.mate)

    def send_act(self, m):
        @pl.when(self.encoder)
        def _():
            for n in range(4):
                self.act_copy(n, m).start()

    def send_branch(self, m):
        @pl.when(self.encoder & (self.core == m))
        def _():
            for k in range(4):
                self.branch_copy(k).start()

    def pass_factors(self):
        for k in range(4):
            self.branch_copy(k).wait_recv()
        self.branch_forward().start()

    def take_factors(self):
        for m in range(2):
            for n in range(4):
                self.act_copy(n, m).wait()
        for k in range(4):
            self.branch_copy(k).wait_send()
        self.branch_forward().wait()

    def left_of(self, i):
        return jnp.minimum(i // 4, 2) + jnp.where(i > 8, 1, 0)

    def cross_tile(self, i, k, y):
        first = (i - self.own_chunks) * 2
        small = self.rows // 2
        base = self.a_fac.shape[2] // 2

        def product(e):
            q = first + e
            block = dot_tn(
                self.a_fac[4 + (q + 1) // 2, :, pl.ds(pl.multiple_of(base + k * self.rows, self.rows), self.rows)],
                self.b_fac[self.own_chunks + q],
            )
            return jnp.where(y == 0, block[:small], block[small:])

        def given(e):
            place = pl.ds(pl.multiple_of(k * self.rows + y * small, small), small)
            return self.slope[first + e, place].astype(F32)

        return product, given

    def cross_into(self, ref, i, k, y):
        product, given = self.cross_tile(i, k, y)
        small = self.rows // 2

        @pl.when(self.decoder)
        def _():
            for e in range(2):
                ref[e * small : (e + 1) * small] = product(e).astype(ref.dtype)

        @pl.when(self.encoder)
        def _():
            for e in range(2):
                ref[e * small : (e + 1) * small] = given(e).astype(ref.dtype)

    def pair_step(self, j):
        i = j + jnp.where(self.decoder, 2, 4)

        @pl.when(j >= self.AHEAD)
        def _():
            pl.semaphore_wait(self.pair_credit, 1)
            for k in range(self.line):
                self.pair_copy(j, k).wait_send()

        @pl.when(i < self.own_chunks)
        def _():
            left = self.left_of(i)
            factor = jnp.concatenate(
                [self.a_fac[left, :, self.tile_rows(k * 2 + 1 - self.y)] for k in range(self.line)], 1
            )
            block = dot_tn(factor, self.b_fac[i]).astype(BF)
            for k in range(self.line):
                slot = self.pair_slot(j, k)
                slot[...] = block[k * self.rows : (k + 1) * self.rows]

        @pl.when(i >= self.own_chunks)
        def _():
            @pl.when(self.encoder)
            def _():
                for e in range(2):
                    self.cross_copy((i - self.own_chunks) * 2 + e).wait_recv()

            loop(self.line, lambda k: self.cross_into(self.pair_slot(j, k), i, k, 1 - self.y))

        for k in (0, 3, 1, 2):
            self.pair_copy(j, k).start()

    def begin(self):
        @pl.when(self.has_left)
        def _():
            pl.semaphore_signal(self.right_credit, inc=self.WINDOW, device_id=self.left, device_id_type=MESH)

        @pl.when(self.has_right)
        def _():
            pl.semaphore_signal(self.left_credit, inc=self.WINDOW, device_id=self.right, device_id_type=MESH)

        @pl.when(self.encoder)
        def _():
            pl.semaphore_signal(self.cross_credit, inc=1, device_id=self.across, device_id_type=MESH)

    def between(self):
        loop(2, self.pair_step)
        self.line_step(0)

    def before(self, m):
        opening = self.encoder & (m == 0)

        @pl.when(opening)
        def _():
            self.pass_factors()

        first = jnp.where(self.decoder, 2, 0) + 2 * m
        lax.fori_loop(first, first + 2, lambda j, carry: (self.pair_step(j), carry)[1], 0)

        @pl.when(opening)
        def _():
            self.take_factors()

        self.line_step(jnp.where(self.decoder, 1, 0) + 2 * m)

    def middle(self, m):
        self.line_step(jnp.where(self.decoder, 2, 1) + 2 * m)

    def entry(self, t, e):
        last = self.line - 1
        on = last - self.z
        k = jnp.where(e == last, self.z, jnp.where(e < on, last - e, e - on))
        hops = jnp.where(k > self.z, self.z, last - self.z)
        p = t - jnp.where(e == last, last, hops)
        valid = (p >= 0) & (p < self.positions)
        line_first = (p < self.EARLY) & self.decoder
        i = jnp.where(line_first, p // 2, p - jnp.where(self.decoder, 2, 0))
        y = jnp.where(line_first & (lax.rem(p, 2) == 0), 1 - self.y, self.y)
        return k, p, valid, i, y

    def line_step(self, t):
        last = self.line - 1

        def held_at(p):
            return (p >= 0) & (p < self.positions)

        @pl.when(held_at(t - self.z) & self.has_right)
        def _():
            pl.semaphore_wait(self.right_credit, 1)

        @pl.when(held_at(t - (last - self.z)) & self.has_left)
        def _():
            pl.semaphore_wait(self.left_credit, 1)

        for e in range(self.line):
            k, p, valid, i, y = self.entry(t, e)
            i = jnp.clip(i, 0, self.own_chunks - 1)
            self.acc[e] = dot_tn(self.a_fac[self.left_of(i), :, self.tile_rows(k * 2 + y)], self.b_fac[i])

        @pl.when(self.encoder & (t < self.EARLY + last))
        def _():
            for e in range(self.line):
                k, p, valid, i, y = self.entry(t, e)
                n = jnp.clip(i, 0, self.EARLY - 1)
                part = dot_tn(
                    self.a_fac[4, :, self.tile_rows(k)], self.a_fac[5 + n // 2, :, self.cols(lax.rem(n, 2))]
                )
                self.acc[e] += jnp.where(i < self.EARLY, part, 0.0)

        def one(e):
            k, p, valid, i, y = self.entry(t, e)

            @pl.when(valid)
            def _():
                acc = self.acc.at[e]

                @pl.when(i >= self.own_chunks)
                def _():
                    self.cross_into(acc, i, k, y)

                @pl.when(p >= self.EARLY)
                def _():
                    j = p - self.EARLY
                    self.pair_copy(j, k).wait_recv()
                    acc[...] += self.pair_got[lax.rem(j, self.AHEAD) * self.line + k].astype(F32)

                @pl.when(e < last)
                def _():
                    self.send(p, k, acc)

                @pl.when(e == last)
                def _():
                    self.finish(p, acc)

        loop(self.line, one)

    def arrived(self, side, p, k, h):
        self.line_copy(side, p, k, self.z, h).wait_recv()
        return self.line_got(self.line_place(side, p, k, self.z))[self.piece(h)].astype(F32)

    def send(self, p, k, acc):
        slot = self.line_slot(p, k)

        def to(side, receiver, inner):
            copies = [self.line_copy(side, p, k, receiver, h) for h in range(self.PIECES)]

            @pl.when(p >= self.DEPTH)
            def _():
                for copy in copies:
                    copy.wait_send()

            @pl.when(inner)
            def _():
                for h, copy in enumerate(copies):
                    slot[self.piece(h)] = (acc[self.piece(h)] + self.arrived(side, p, k, h)).astype(BF)
                    copy.start()

            @pl.when(jnp.logical_not(inner))
            def _():
                slot[...] = acc[...].astype(BF)
                for copy in copies:
                    copy.start()

        @pl.when(k > self.z)
        def _():
            to(0, self.z + 1, self.has_left)

        @pl.when(k < self.z)
        def _():
            to(1, self.z - 1, self.has_right)

    def finish(self, p, acc):
        @pl.when(self.has_left)
        def _():
            for h in range(self.PIECES):
                acc[self.piece(h)] += self.arrived(0, p, self.z, h)

        @pl.when(self.has_right)
        def _():
            for h in range(self.PIECES):
                acc[self.piece(h)] += self.arrived(1, p, self.z, h)

        line_first = (p < self.EARLY) & self.decoder

        @pl.when(line_first & (lax.rem(p, 2) == 0))
        def _():
            self.late_sent[p // 2] = acc[...].astype(BF)
            self.late_copy(p // 2).start()

        @pl.when(line_first & (lax.rem(p, 2) == 1))
        def _():
            self.late_acc[p // 2] = acc[...]

        @pl.when(jnp.logical_not(line_first))
        def _():
            i = p - jnp.where(self.decoder, 2, 0)

            @pl.when(i >= self.FINAL + jnp.where(self.decoder, 2, 0))
            def _():
                self.final_copy(i).wait()

            first = self.encoder & (i == 0)

            @pl.when(first)
            def _():
                self.late_acc[0] = acc[...]
                pltpu.make_async_copy(self.late_acc.at[0], self.tiles.at[0], self.final_sem.at[0]).start()

            @pl.when(jnp.logical_not(first))
            def _():
                slot = self.final_slot(i)
                slot[...] = acc[...]
                self.final_copy(i).start()

        @pl.when(p + self.WINDOW < self.positions)
        def _():
            @pl.when(self.has_left)
            def _():
                pl.semaphore_signal(self.right_credit, inc=1, device_id=self.left, device_id_type=MESH)

            @pl.when(self.has_right)
            def _():
                pl.semaphore_signal(self.left_credit, inc=1, device_id=self.right, device_id_type=MESH)

        @pl.when((p >= self.EARLY) & (p - self.EARLY + self.AHEAD < self.pairs))
        def _():
            pl.semaphore_signal(self.pair_credit, inc=1, device_id=self.partner, device_id_type=MESH)
            self.pair_step(p - self.EARLY + self.AHEAD)

    def final_slot(self, i):
        slot = lax.rem(i, self.FINAL)
        return self.resid.at[self.tile_rows(slot // 2), self.cols(lax.rem(slot, 2))]

    def final_copy(self, i):
        return pltpu.make_async_copy(
            self.final_slot(i), self.tiles.at[i], self.final_sem.at[lax.rem(i, self.FINAL)]
        )

    def cross_part(self):
        @pl.when(self.decoder)
        def _():
            pl.semaphore_wait(self.cross_credit, 1)

            def one(q):
                def tile(k):
                    self.slope[q, self.tile_rows(k)] = dot_tn(
                        self.a_fac[4 + (q + 1) // 2, :, self.tile_rows(k)],
                        self.b_fac[self.own_chunks + q],
                    ).astype(BF)

                loop(4, tile)
                self.cross_copy(q).start()

            loop(4, one)

    def norm_copy(self, src, dst, device):
        return self.remote(self.nb.at[src], self.nb.at[dst], self.norm_send.at[dst], self.norm_recv.at[dst], device)

    def start_norms(self, sums):
        nb, has_left, has_right = self.nb, self.has_left, self.has_right
        for i in range(6):
            nb[0, i : i + 1] = jnp.sum(sums[i], 0, keepdims=True)
        nb[0, 6:8] = jnp.zeros_like(nb[0, 6:8])
        nb[3] = nb[0]
        nb[4] = nb[0]
        nb[5] = nb[0]

        @pl.when(jnp.logical_not(has_left))
        def _():
            self.norm_copy(3, 1, self.right).start()

        @pl.when(jnp.logical_not(has_right))
        def _():
            self.norm_copy(4, 2, self.left).start()

    def middle_norms(self):
        nb, has_left, has_right = self.nb, self.has_left, self.has_right
        to_right = self.norm_copy(3, 1, self.right)
        to_left = self.norm_copy(4, 2, self.left)

        @pl.when(has_left)
        def _():
            to_right.wait_recv()
            nb[5] += nb[1]

            @pl.when(has_right)
            def _():
                nb[3] += nb[1]
                to_right.start()

        @pl.when(has_right)
        def _():
            to_left.wait_recv()
            nb[5] += nb[2]

            @pl.when(has_left)
            def _():
                nb[4] += nb[2]
                to_left.start()

        self.norm_copy(5, 6, self.partner).start()

    def hand_norms(self):
        nb = self.nb
        self.norm_copy(5, 6, self.partner).wait()

        @pl.when(self.has_right)
        def _():
            self.norm_copy(3, 1, self.right).wait_send()

        @pl.when(self.has_left)
        def _():
            self.norm_copy(4, 2, self.left).wait_send()

        nb[7] = nb[5] + nb[6]

        @pl.when(self.decoder)
        def _():
            self.norm_copy(7, 8, self.across).start()
            nb[8] = nb[7]

    def finish_norms(self, norm_out, norm3_out):
        nb = self.nb
        hand = self.norm_copy(7, 8, self.across)
        norm_out[...] = nb[7, :, pl.ds(pl.multiple_of(self.dp * 128, 128), 128)]

        @pl.when(self.encoder)
        def _():
            hand.wait_recv()

        place = self.section * self.line * 2 + self.dp
        block = nb[8, :, pl.ds(pl.multiple_of(place // 2 * 128, 128), 128)]
        norm3_out[...] = jnp.where(self.y == 0, block, pltpu.roll(block, 64, 1))

        @pl.when(self.decoder)
        def _():
            hand.wait_send()

    def run(self, sums, norm_out, norm3_out):
        self.start_norms(sums)
        first = jnp.where(self.decoder, 6, 4)
        lax.fori_loop(first, self.AHEAD, lambda j, carry: (self.pair_step(j), carry)[1], 0)
        self.cross_part()

        def step(t, carry):
            self.line_step(t)

            @pl.when(t == 6)
            def _():
                self.middle_norms()

            @pl.when(t == self.own_chunks + 1)
            def _():
                self.hand_norms()

            return carry

        lax.fori_loop(jnp.where(self.decoder, 5, 4), self.positions + self.line - 1, step, 0)
        self.finish_norms(norm_out, norm3_out)

    def drain(self):
        @pl.when(self.decoder)
        def _():
            for e in range(2):
                self.late_copy(e).wait()
                self.final_copy(e).wait()
                slot = self.final_slot(e)
                slot[...] = self.late_acc[e] + self.late_got[e].astype(F32)
                self.final_copy(e).start()

        for slot in range(self.AHEAD):
            for k in range(self.line):
                self.pair_copy(slot, k).wait_send()

        for slot in range(self.DEPTH):
            for k in range(self.line):

                @pl.when(self.z != k)
                def _():
                    for h in range(self.PIECES):
                        self.line_copy(0, slot, k, 0, h).wait_send()

        for slot in range(self.FINAL):
            self.final_copy(slot).wait()

        @pl.when(self.decoder)
        def _():
            for q in range(4):
                self.cross_copy(q).wait_send()


def layer_kernel(
    sections,
    ring,
    inputs,
    targets,
    cotangent,
    counts,
    qkv_hbm,
    out_hbm,
    gain1,
    bias1,
    up_hbm,
    down_hbm,
    gain2,
    bias2,
    cross_hbm,
    cross_out_hbm,
    gain3,
    bias3,
    seg_hbm,
    grad_hbm,
    norm_out,
    first_out,
    second_out,
    seg_out,
    in_grad,
    w_qkv,
    w_out,
    w_up,
    w_down,
    w_cross,
    w_cross_out,
    a_fac,
    b_fac,
    proj,
    cross_proj,
    unit1,
    held,
    unit3,
    scale1,
    scale2,
    scale3,
    resid,
    slope,
    d_mix,
    sent,
    got,
    half_send,
    half_got,
    spare,
    low_out,
    sums,
    load_sem,
    x_sem,
    ex_send,
    ex_recv,
    hop_send,
    hop_recv,
    out_sem,
    *share,
):
    section = lax.axis_index("section")
    dp = lax.axis_index("dp")
    core = lax.axis_index("mp")
    decoder = section == sections - 1
    encoder = section != sections - 1
    mate = (section, dp, 1 - core)
    across = (1 - section, dp, core)
    half = seg_out.shape[2]
    slot = 2 * half
    limit = jnp.where(decoder, 0, slot)
    width = w_up.shape[1]
    parts = width // CHUNK
    two, three = jnp.where(decoder, 0, 1), jnp.where(decoder, 1, 0)
    own = core * half
    other = (1 - core) * half

    d_branch, crossed, d_attn, layer_in, normed_low, memory, d_cross = (a_fac.at[i] for i in range(7))
    act = b_fac.at[0:parts]
    d_hidden = b_fac.at[parts : 2 * parts]
    mixed = b_fac.at[2 * parts]
    d_proj = b_fac.at[2 * parts + 1 : 2 * parts + 4]
    d_cross_proj = b_fac.at[2 * parts + 4 : 2 * parts + 7]
    cross_mixed = b_fac.at[2 * parts + 7]

    unit2, d_out = held.at[0], held.at[1]

    def rows_of(m):
        return pl.ds(pl.multiple_of(m * slot, slot), slot)

    def half_of(m, offset):
        return pl.ds(pl.multiple_of(m * slot + offset, half), half)

    def strip_of(m, k):
        return pl.ds(pl.multiple_of(m * slot + k * STRIP, STRIP), STRIP)

    def strips(body):
        for k in range(slot // STRIP):
            body(k)

    barrier = pltpu.get_barrier_semaphore()
    for device in (mate, across):
        pl.semaphore_signal(barrier, inc=1, device_id=device, device_id_type=MESH)
    if ring:
        total = GradientShare(
            ring, section, dp, core, decoder, a_fac, b_fac, first_out, w_up, w_down, held, slope, resid, spare, *share
        )
        greeted = 2 + total.greet(barrier)
    else:
        greeted = 2

    loads = [
        pltpu.make_async_copy(src, dst, load_sem.at[i])
        for i, (src, dst) in enumerate(
            (
                (qkv_hbm.at[0], w_qkv),
                (out_hbm.at[0], w_out),
                (up_hbm.at[0], w_up),
                (down_hbm.at[0], w_down),
                (cross_hbm, w_cross),
                (cross_out_hbm, w_cross_out),
            )
        )
    ]

    def local_rows(src, dst, m, sem):
        return pltpu.make_async_copy(src.at[m], dst.at[half_of(m, own)], sem)

    def mate_rows(src, dst, m, send, recv):
        return pltpu.make_async_remote_copy(
            src_ref=src.at[m],
            dst_ref=dst.at[half_of(m, own)],
            send_sem=send,
            recv_sem=recv,
            device_id=mate,
            device_id_type=MESH,
        )

    def start_rows(src, dst, base):
        for m in range(2):
            local_rows(src, dst, m, x_sem.at[base + m]).start()
        for m in range(2):
            mate_rows(src, dst, m, x_sem.at[base + 2 + m], x_sem.at[base + 4 + m]).start()

    def wait_local(src, dst, base, m):
        local_rows(src, dst, m, x_sem.at[base + m]).wait()

    def wait_mate(src, dst, base, m):
        mate_rows(src, dst, m, x_sem.at[base + 2 + m], x_sem.at[base + 4 + m]).wait()

    def wait_rows(src, dst, base, m):
        wait_local(src, dst, base, m)
        wait_mate(src, dst, base, m)

    @pl.when(encoder)
    def _():
        for m in range(2):
            local_rows(inputs, layer_in, m, x_sem.at[m]).start()

    @pl.when(decoder)
    def _():
        for m in range(2):
            local_rows(targets, layer_in, m, x_sem.at[m]).start()

    loads[0].start()
    loads[1].start()
    pl.semaphore_wait(barrier, greeted)

    def mate_start(src, dst, base):
        for m in range(2):
            mate_rows(src, dst, m, x_sem.at[base + 2 + m], x_sem.at[base + 4 + m]).start()

    @pl.when(encoder)
    def _():
        mate_start(inputs, layer_in, 0)

    @pl.when(decoder)
    def _():
        mate_start(targets, layer_in, 0)

    for copy in loads[2:]:
        copy.start()

    @pl.when(decoder)
    def _():
        start_rows(cotangent, d_out, 6)

    sums[...] = jnp.zeros_like(sums)

    def exchange(which, buffer, m):
        return pltpu.make_async_remote_copy(
            src_ref=sent.at[rows_of(m)],
            dst_ref=got.at[buffer, rows_of(m)],
            send_sem=ex_send.at[which, m],
            recv_sem=ex_recv.at[which, m],
            device_id=mate,
            device_id_type=MESH,
        )

    def half_exchange(which, m):
        return pltpu.make_async_remote_copy(
            src_ref=half_send.at[which, m],
            dst_ref=half_got.at[which, m],
            send_sem=hop_send.at[4 + which, m],
            recv_sem=hop_recv.at[4 + which, m],
            device_id=mate,
            device_id_type=MESH,
        )

    def across_copy(src, dst, which, m):
        return pltpu.make_async_remote_copy(
            src_ref=src,
            dst_ref=dst.at[half_of(m, own)],
            send_sem=hop_send.at[which, m],
            recv_sem=hop_recv.at[which, m],
            device_id=across,
            device_id_type=MESH,
        )

    def forward_copy(ref, which, m):
        return pltpu.make_async_remote_copy(
            src_ref=ref.at[half_of(m, own)],
            dst_ref=ref.at[half_of(m, own)],
            send_sem=hop_send.at[which, m],
            recv_sem=hop_recv.at[which, m],
            device_id=mate,
            device_id_type=MESH,
        )

    def project_out(value, weight, m):
        for n in range(sent.shape[1] // CHUNK):
            cols = slice(n * CHUNK, (n + 1) * CHUNK)
            sent[rows_of(m), cols] = dot_nt(value, weight[cols, :]).astype(BF)

    def summed(buffer, strip):
        return sent[strip].astype(F32) + got[buffer, strip].astype(F32)

    loads[0].wait()

    def project(m, offset):
        piece = half_of(m, offset)
        for t in range(3):
            proj[t, piece] = dot_nn(layer_in[piece], w_qkv[t]).astype(BF)

    def own_rows(m):
        @pl.when(encoder)
        def _():
            wait_local(inputs, layer_in, 0, m)

        @pl.when(decoder)
        def _():
            wait_local(targets, layer_in, 0, m)

        project(m, own)

    loop(2, own_rows)

    def attention_in(m):
        @pl.when(encoder)
        def _():
            wait_mate(inputs, layer_in, 0, m)

        @pl.when(decoder)
        def _():
            wait_mate(targets, layer_in, 0, m)

        rows = rows_of(m)
        project(m, other)
        attend_forward(proj, mixed, rows, limit)
        project_out(mixed[rows], w_out, m)
        exchange(0, 0, m).start()

    loads[1].wait()
    loop(2, attention_in)
    for copy in loads[2:]:
        copy.wait()

    def after_attention(m):
        exchange(0, 0, m).wait()

        def norm(k):
            strip = strip_of(m, k)
            unit, scale, value = norm_forward(
                layer_in[strip].astype(F32) + summed(0, strip), gain1[...], bias1[...]
            )
            unit1[strip] = unit.astype(BF)
            scale1[strip] = scale
            resid[strip] = value
            low_out[pl.ds(k * STRIP, STRIP)] = value.astype(BF)
            crossed[strip] = value.astype(BF)

        strips(norm)

        @pl.when(decoder)
        def _():
            rows = rows_of(m)
            normed_low[rows] = low_out[...]
            cross_proj[0, rows] = dot_nn(low_out[...], w_cross[0]).astype(BF)
            across_copy(seg_out.at[0, m], memory, 0, m).wait_recv()
            forward_copy(memory, 1, m).start()
            forward_copy(memory, 1, m).wait()
            for t in range(1, 3):
                cross_proj[t, rows] = dot_nn(memory[rows], w_cross[t]).astype(BF)
            attend_forward(cross_proj, cross_mixed, rows, None)
            project_out(cross_mixed[rows], w_cross_out, m)
            exchange(1, 1, m).start()


    def feed_forward(m):
        rows = rows_of(m)

        @pl.when(decoder)
        def _():
            exchange(1, 1, m).wait()

            def norm(k):
                strip = strip_of(m, k)
                unit, scale, value = norm_forward(
                    resid[strip] + summed(1, strip), gain3[...], bias3[...]
                )
                unit3[strip] = unit.astype(BF)
                scale3[strip] = scale
                resid[strip] = value
                crossed[strip] = value.astype(BF)

            strips(norm)

        for n in range(parts):
            pre = dot_nn(crossed[rows], w_up[:, n * CHUNK : (n + 1) * CHUNK])
            rise = 0.5 + 0.5 * lax.erf(pre * (0.5**0.5))
            act[n, rows] = (pre * rise).astype(BF)
            slope[n, rows] = (rise + pre * jnp.exp(-0.5 * pre * pre) * 0.3989422804014327).astype(BF)
        if ring:
            total.send_act(m)
        project_out(jnp.concatenate([act[n, rows] for n in range(parts)], 1), w_down, m)
        exchange(2, two, m).start()


    def finish_forward(m):
        exchange(2, two, m).wait()

        def norm(k):
            strip = strip_of(m, k)
            unit, scale, value = norm_forward(
                resid[strip] + summed(two, strip), gain2[...], bias2[...]
            )
            unit2[strip] = unit.astype(BF)
            scale2[strip] = scale
            low_out[pl.ds(k * STRIP, STRIP)] = value.astype(BF)

        strips(norm)
        seg_out[0, m] = low_out[pl.ds(pl.multiple_of(own, half), half)]

        @pl.when(encoder)
        def _():
            across_copy(seg_out.at[0, m], memory, 0, m).start()

    def forward_parts(m):
        after_attention(m)

        @pl.when(m == 1)
        def _():
            finish_forward(0)

        feed_forward(m)

    question = dp // QSLOTS
    spot = dp - question * QSLOTS

    def feed_backward(m):
        rows = rows_of(m)

        @pl.when(encoder)
        def _():
            across_copy(half_send.at[0, m], d_out, 2, m).wait_recv()
            forward_copy(d_out, 3, m).start()
            forward_copy(d_out, 3, m).wait()

        @pl.when(decoder)
        def _():
            wait_rows(cotangent, d_out, 6, m)

        keep = jnp.where(spot < counts[m, question], 1.0, 0.0)
        keep = jnp.where(decoder, keep, 1.0)

        def norm(k):
            strip = strip_of(m, k)
            grad = norm_backward(
                d_out[strip].astype(F32) * keep,
                unit2[strip].astype(F32),
                scale2[strip],
                gain2[...],
                sums,
                2,
            )
            resid[strip] = grad
            d_branch[strip] = grad.astype(BF)

        strips(norm)
        if ring:
            total.send_branch(m)
        for n in range(parts):
            grad = dot_nn(d_branch[rows], w_down[:, n * CHUNK : (n + 1) * CHUNK])
            d_hidden[n, rows] = (grad * slope[n, rows].astype(F32)).astype(BF)
        project_out(jnp.concatenate([d_hidden[n, rows] for n in range(parts)], 1), w_up, m)
        exchange(3, three, m).start()

    loop(2, forward_parts)

    @pl.when(decoder)
    def _():
        feed_backward(0)

    finish_forward(1)
    seg_leaves = pltpu.make_async_copy(seg_out, seg_hbm, out_sem.at[2])
    seg_leaves.start()
    lax.fori_loop(jnp.where(decoder, 1, 0), 2, lambda m, carry: (feed_backward(m), carry)[1], 0)
    if ring:
        total.begin()

    def cross_backward(m):
        rows = rows_of(m)

        def norm(k):
            strip = strip_of(m, k)
            grad = norm_backward(
                resid[strip] + summed(three, strip),
                unit3[strip].astype(F32),
                scale3[strip],
                gain3[...],
                sums,
                4,
            )
            resid[strip] = grad
            d_cross[strip] = grad.astype(BF)

        strips(norm)
        d_mix[rows] = dot_nn(d_cross[rows], w_cross_out[...]).astype(BF)

        @pl.when(m == 1)
        def _():
            memory_leaves(0)

        attend_backward(cross_proj, d_mix, d_cross_proj, rows, None)

        def memory_part(offset):
            piece = half_of(m, offset)
            return jnp.concatenate([d_cross_proj[1, piece], d_cross_proj[2, piece]], 1)

        def memory_weight(n):
            cols = slice(n * CHUNK, (n + 1) * CHUNK)
            return jnp.concatenate([w_cross[1, cols], w_cross[2, cols]], 1)

        for n in range(sent.shape[1] // CHUNK):
            cols = slice(n * CHUNK, (n + 1) * CHUNK)
            half_send[0, m, :, cols] = dot_nt(memory_part(other), memory_weight(n)).astype(BF)
        half_exchange(0, m).start()
        for n in range(sent.shape[1] // CHUNK):
            cols = slice(n * CHUNK, (n + 1) * CHUNK)
            spare[2 * m + n] = dot_nt(memory_part(own), memory_weight(n))
        project_out(d_cross_proj[0, rows], w_cross[0], m)
        exchange(4, 0, m).start()
        @pl.when(m == 1)
        def _():
            memory_leaves(1)

    def memory_leaves(m):
        half_exchange(0, m).wait()
        for n in range(sent.shape[1] // CHUNK):
            cols = slice(n * CHUNK, (n + 1) * CHUNK)
            half_send[0, m, :, cols] = (
                spare[2 * m + n] + half_got[0, m, :, cols].astype(F32)
            ).astype(BF)
        across_copy(half_send.at[0, m], d_out, 2, m).start()

    def attention_back(m):
        rows = rows_of(m)

        def norm_rows(buffer):
            def norm(k):
                strip = strip_of(m, k)
                grad = norm_backward(
                    resid[strip] + summed(buffer, strip),
                    unit1[strip].astype(F32),
                    scale1[strip],
                    gain1[...],
                    sums,
                    0,
                )
                resid[strip] = grad
                d_attn[strip] = grad.astype(BF)

            strips(norm)

        @pl.when(decoder)
        def _():
            exchange(4, 0, m).wait()

        @pl.when(encoder)
        def _():
            exchange(3, three, m).wait()

        norm_rows(0)
        d_mix[rows] = dot_nn(d_attn[rows], w_out[...]).astype(BF)
        attend_backward(proj, d_mix, d_proj, rows, limit)

        if ring:
            total.middle(m)

        def input_part(offset):
            piece = half_of(m, offset)
            return jnp.concatenate([d_proj[t, piece] for t in range(3)], 1)

        def input_weight(n):
            cols = slice(n * CHUNK, (n + 1) * CHUNK)
            return jnp.concatenate([w_qkv[t, cols] for t in range(3)], 1)

        for n in range(sent.shape[1] // CHUNK):
            cols = slice(n * CHUNK, (n + 1) * CHUNK)
            half_send[1, m, :, cols] = dot_nt(input_part(other), input_weight(n)).astype(BF)
        half_exchange(1, m).start()
        for n in range(sent.shape[1] // CHUNK):
            cols = slice(n * CHUNK, (n + 1) * CHUNK)
            resid[half_of(m, own), cols] += dot_nt(input_part(own), input_weight(n))

    @pl.when(decoder)
    def _():
        if ring:
            total.between()

        def both(m):
            exchange(3, three, m).wait()
            cross_backward(m)

        loop(2, both)

    def last_part(m):
        if ring:
            total.before(m)
        attention_back(m)

    loop(2, last_part)

    def finish_backward(m):
        half_exchange(1, m).wait()
        in_grad[0, m] = (
            resid[half_of(m, own)] + half_got[1, m].astype(F32)
        ).astype(BF)

    loop(2, finish_backward)
    grad_leaves = pltpu.make_async_copy(in_grad, grad_hbm, out_sem.at[3])
    grad_leaves.start()

    @pl.when(encoder)
    def _():
        for m in range(2):
            across_copy(seg_out.at[0, m], memory, 0, m).wait_send()

    @pl.when(decoder)
    def _():
        for m in range(2):
            across_copy(half_send.at[0, m], d_out, 2, m).wait_send()

    if ring:
        total.run(sums, norm_out, second_out)
        total.drain()
        seg_leaves.wait()
        grad_leaves.wait()
        return

    for i in range(6):
        norm_out[i : i + 1] = jnp.sum(sums[i], 0, keepdims=True)
    norm_out[6:8] = jnp.zeros_like(norm_out[6:8])
    seg_leaves.wait()
    grad_leaves.wait()
    copies = [
        pltpu.make_async_copy(a_fac, first_out, out_sem.at[0]),
        pltpu.make_async_copy(b_fac, second_out, out_sem.at[1]),
    ]
    for copy in copies:
        copy.start()
    for copy in copies:
        copy.wait()


def unpack_kernel(parts, seg, grads, norms, tiles, norm3, *outs):
    (seg_out, in_grad, qkv, proj_out, gain1, bias1, up, down, gain2, bias2, cross, cross_out, gain3, bias3,
     rows16, rows32, come, go) = outs
    rows = tiles.shape[1]
    small = rows // 2
    moves = [(seg.at[0], rows16.at[0], seg_out.at[0]), (grads.at[0], rows16.at[1], in_grad.at[0])]
    whole = [down.at[0, :, n * CHUNK : (n + 1) * CHUNK] for n in range(parts)]
    whole += [up.at[0, :, n * CHUNK : (n + 1) * CHUNK] for n in range(parts)]
    whole += [proj_out.at[0]] + [qkv.at[0, t] for t in range(3)]
    for n, target in enumerate(whole):
        moves.append((tiles.at[n], rows32.at[n], target))
    for q in range(4):
        n, half = 2 * parts + 4 + q // 2, pl.ds(q % 2 * small, small)
        moves.append((tiles.at[n, half], rows32.at[n, half], cross.at[q] if q < 3 else cross_out))
    first = [pltpu.make_async_copy(src, mid, come.at[i]) for i, (src, mid, dst) in enumerate(moves)]
    second = [pltpu.make_async_copy(mid, dst, go.at[i]) for i, (src, mid, dst) in enumerate(moves)]
    for copy in first:
        copy.start()
    for i, ref in enumerate((gain1, bias1, gain2, bias2)):
        ref[...] = norms[i : i + 1]
    gain3[...] = norm3[4:5, :small]
    bias3[...] = norm3[5:6, :small]
    for a, b in zip(first, second):
        a.wait()
        b.start()
    for copy in second:
        copy.wait()


def body(
    sections,
    ring,
    inputs,
    target_inputs,
    cotangent,
    slot_counts,
    w_qkv,
    w_out,
    norm1_gain,
    norm1_bias,
    w_up,
    w_down,
    norm2_gain,
    norm2_bias,
    cross_qkv,
    cross_out,
    norm3_gain,
    norm3_bias,
):
    micro, half, depth = inputs.shape
    rows = micro * 2 * half
    heads = w_out.shape[2]
    width = w_up.shape[2]
    parts = width // CHUNK
    chunks = 2 * parts + 8
    hbm = pl.BlockSpec(memory_space=pl.ANY)
    vmem = pl.BlockSpec(memory_space=VM)
    smem = pl.BlockSpec(memory_space=pltpu.SMEM)
    shape = jax.ShapeDtypeStruct
    if ring:
        results = (
            shape((8, depth // ring), F32),
            shape((chunks - 2, depth // ring, CHUNK), F32),
            shape((8, depth // ring), F32),
        )
        places = (vmem, hbm, vmem)
    else:
        results = (
            shape((8, depth), F32),
            shape((7, rows, depth), BF),
            shape((chunks, rows, CHUNK), BF),
        )
        places = (vmem, hbm, hbm)
    dma = pltpu.SemaphoreType.DMA
    regular = pltpu.SemaphoreType.REGULAR
    tile = (depth // ring, CHUNK) if ring else None
    share = (
        [
            VM((GradientShare.AHEAD * 4,) + tile, BF),
            VM((9, 8, depth), F32),
            VM((2,) + tile, BF),
            VM((2,) + tile, BF),
            VM((2,) + tile, F32),
            dma((GradientShare.AHEAD * 4,)),
            dma((GradientShare.AHEAD * 4,)),
            dma((GradientShare.DEPTH * 4, GradientShare.PIECES)),
            dma((GradientShare.WINDOW * 5, GradientShare.PIECES)),
            dma((4,)),
            dma((4,)),
            dma((9,)),
            dma((9,)),
            dma((2,)),
            dma((2,)),
            dma((13,)),
            dma((13,)),
            dma((GradientShare.FINAL,)),
            regular,
            regular,
            regular,
            regular,
        ]
        if ring
        else []
    )
    seg_out, in_grad, norms, first, second = pl.pallas_call(
        functools.partial(layer_kernel, sections, ring),
        out_shape=(
            shape((1, micro, half, depth), BF),
            shape((1, micro, half, depth), BF),
        )
        + results,
        in_specs=[hbm, hbm, hbm, smem, hbm, hbm, vmem, vmem, hbm, hbm, vmem, vmem, hbm, hbm, vmem, vmem],
        out_specs=(hbm, hbm) + places,
        scratch_shapes=[
            VM((1, micro, half, depth), BF),
            VM((1, micro, half, depth), BF),
            VM((3, depth, heads), BF),
            VM((depth, heads), BF),
            VM((depth, width), BF),
            VM((depth, width), BF),
            VM((3, depth, heads), BF),
            VM((depth, heads), BF),
            VM((7, rows, depth), BF),
            VM((chunks, rows, CHUNK), BF),
            VM((3, rows, heads), BF),
            VM((3, rows, heads), BF),
            VM((rows, depth), BF),
            VM((2, rows, depth), BF),
            VM((rows, depth), BF),
            VM((rows, 1), F32),
            VM((rows, 1), F32),
            VM((rows, 1), F32),
            VM((rows, depth), F32),
            VM((parts, rows, CHUNK), BF),
            VM((rows, heads), BF),
            VM((rows, depth), BF),
            VM((2, rows, depth), BF),
            VM((2, micro, half, depth), BF),
            VM((2, micro, half, depth), BF),
            VM((4, half, CHUNK), F32),
            VM((2 * half, depth), BF),
            VM((6, 8, depth), F32),
            pltpu.SemaphoreType.DMA((6,)),
            pltpu.SemaphoreType.DMA((12,)),
            pltpu.SemaphoreType.DMA((5, micro)),
            pltpu.SemaphoreType.DMA((5, micro)),
            pltpu.SemaphoreType.DMA((6, micro)),
            pltpu.SemaphoreType.DMA((6, micro)),
            pltpu.SemaphoreType.DMA((4,)),
        ]
        + share,
        compiler_params=pltpu.CompilerParams(
            collective_id=0, has_side_effects=True, vmem_limit_bytes=60 * 2**20
        ),
        name="layers",
    )(
        inputs,
        target_inputs,
        cotangent,
        slot_counts,
        w_qkv,
        w_out,
        norm1_gain,
        norm1_bias,
        w_up,
        w_down,
        norm2_gain,
        norm2_bias,
        cross_qkv,
        cross_out,
        norm3_gain[None],
        norm3_bias[None],
    )
    if ring:
        lanes = depth // ring
        row = shape((1, lanes), F32)
        small = shape((1, lanes // 2), F32)
        outs = pl.pallas_call(
            functools.partial(unpack_kernel, parts),
            out_shape=(
                shape(seg_out.shape, BF),
                shape(in_grad.shape, BF),
                shape((1, 3, lanes, heads), F32),
                shape((1, lanes, heads), F32),
                row,
                row,
                shape((1, lanes, width), F32),
                shape((1, lanes, width), F32),
                row,
                row,
                shape((3, lanes // 2, heads), F32),
                shape((lanes // 2, heads), F32),
                small,
                small,
            ),
            in_specs=[hbm, hbm, vmem, hbm, vmem],
            out_specs=(hbm, hbm, hbm, hbm, vmem, vmem, hbm, hbm, vmem, vmem, hbm, hbm, vmem, vmem),
            scratch_shapes=[
                VM((2, micro, half, depth), BF),
                VM((chunks - 2, lanes, CHUNK), F32),
                dma((2 * parts + 10,)),
                dma((2 * parts + 10,)),
            ],
            name="unpack",
        )(seg_out, in_grad, norms, first, second)
        return outs[:12] + (outs[12][0], outs[13][0])
    a_fac, b_fac = first, second
    decoder = lax.axis_index("section") == sections - 1

    def weight_grad(left, first, count):
        return jnp.einsum(
            "nd,tnc->tdc", a_fac[left], b_fac[first : first + count], preferred_element_type=F32
        ).astype(BF)

    def shared(grad, axes, dim):
        return lax.psum_scatter(grad, axes, scatter_dimension=dim, tiled=True)

    def wide(grad):
        return jnp.swapaxes(grad, 0, 1).reshape(depth, -1)

    grad_down = shared(wide(weight_grad(0, 0, parts)), "dp", 0)
    grad_up = shared(wide(weight_grad(1, parts, parts)), "dp", 0)
    grad_out = shared(weight_grad(2, 2 * parts, 1)[0], "dp", 0)
    grad_qkv = shared(weight_grad(3, 2 * parts + 1, 3), "dp", 1)
    cross = jnp.concatenate(
        [
            weight_grad(4, 2 * parts + 4, 1),
            weight_grad(5, 2 * parts + 5, 2),
            weight_grad(6, 2 * parts + 7, 1),
        ],
        0,
    )
    cross = shared(jnp.where(decoder, cross, jnp.zeros_like(cross)), ("section", "dp"), 1)
    small = shared(norms[:4], "dp", 1)
    norm3 = jnp.where(decoder, norms[4:6], jnp.zeros_like(norms[4:6]))
    norm3 = shared(norm3, ("section", "dp"), 1)
    return (
        seg_out,
        in_grad,
        grad_qkv[None].astype(F32),
        grad_out[None].astype(F32),
        small[0:1],
        small[1:2],
        grad_up[None].astype(F32),
        grad_down[None].astype(F32),
        small[2:3],
        small[3:4],
        cross[:3].astype(F32),
        cross[3].astype(F32),
        norm3[0],
        norm3[1],
    )


def solution(mesh):
    ring = 8 if mesh.shape["dp"] == 8 else 0
    return jax.shard_map(
        functools.partial(body, mesh.shape["section"], ring),
        mesh=mesh,
        in_specs=(
            P(None, ("dp", "mp"), None),
            P(None, ("dp", "mp"), None),
            P(None, ("dp", "mp"), None),
            P(),
            P("section", None, None, "mp"),
            P("section", None, "mp"),
            P("section", None),
            P("section", None),
            P("section", None, "mp"),
            P("section", None, "mp"),
            P("section", None),
            P("section", None),
            P(None, None, "mp"),
            P(None, "mp"),
            P(),
            P(),
        ),
        out_specs=(
            P("section", None, ("dp", "mp"), None),
            P("section", None, ("dp", "mp"), None),
            P("section", None, "dp", "mp"),
            P("section", "dp", "mp"),
            P("section", "dp"),
            P("section", "dp"),
            P("section", "dp", "mp"),
            P("section", "dp", "mp"),
            P("section", "dp"),
            P("section", "dp"),
            P(None, ("section", "dp"), "mp"),
            P(("section", "dp"), "mp"),
            P(("section", "dp")),
            P(("section", "dp")),
        ),
        check_vma=False,
    )
```

```python
import functools

import jax
import jax.numpy as jnp
from jax import lax
from jax.experimental import pallas as pl
from jax.experimental.pallas import tpu as pltpu
from jax.sharding import PartitionSpec as P

HEAD = 64
SLOT = 256
QSLOTS = 4
CHUNK = 512
PAIR = 2 * HEAD
STRIP = 64
EPS = 1e-5
NEG = -1000000000.0
MESH = pl.DeviceIdType.MESH
BF = jnp.bfloat16
F32 = jnp.float32
VM = pltpu.VMEM


def dot_nn(a, b):
    return lax.dot_general(a, b, (((1,), (0,)), ((), ())), preferred_element_type=F32)


def dot_nt(a, b):
    return lax.dot_general(a, b, (((1,), (1,)), ((), ())), preferred_element_type=F32)


def dot_tn(a, b):
    return lax.dot_general(a, b, (((0,), (0,)), ((), ())), preferred_element_type=F32)


def loop(count, body):
    def step(i, carry):
        body(i)
        return carry

    lax.fori_loop(0, count, step, 0)


def head_masks():
    lane = lax.broadcasted_iota(jnp.int32, (1, PAIR), 1)
    first = jnp.where(lane < HEAD, 1.0, 0.0).astype(BF)
    second = jnp.where(lane < HEAD, 0.0, 1.0).astype(BF)
    return first, second


def expos_of(query, keys, mask, limit):
    scores = dot_nt(keys, query * (mask * (HEAD**-0.5)).astype(BF))
    if limit is not None:
        key = lax.broadcasted_iota(jnp.int32, scores.shape, 0)
        place = lax.broadcasted_iota(jnp.int32, scores.shape, 1)
        scores = jnp.where(place + limit >= key, scores, NEG)
    expo = jnp.exp(scores - jnp.max(scores, 0, keepdims=True))
    return expo, 1.0 / jnp.sum(expo, 0, keepdims=True)


def attend_forward(proj, mixed, rows, limit):
    masks = head_masks()
    for j in range(CHUNK // PAIR):
        lanes = slice(j * PAIR, (j + 1) * PAIR)
        query, keys, values = proj[0, rows, lanes], proj[1, rows, lanes], proj[2, rows, lanes]
        low = []
        for mask in masks:
            expo, share = expos_of(query, keys, mask, limit)
            low.append((expo * share).astype(BF))
        turned = dot_tn(jnp.concatenate([values * mask for mask in masks], 0), jnp.concatenate(low, 0))
        mixed[rows, lanes] = turned.T.astype(BF)


def attend_backward(proj, d_mixed, d_proj, rows, limit):
    masks = head_masks()
    scale = HEAD**-0.5
    for j in range(CHUNK // PAIR):
        lanes = slice(j * PAIR, (j + 1) * PAIR)
        query, keys, values = proj[0, rows, lanes], proj[1, rows, lanes], proj[2, rows, lanes]
        grad = d_mixed[rows, lanes]
        low, d_scores = [], []
        for mask in masks:
            expo, share = expos_of(query, keys, mask, limit)
            weights = expo * share
            d_weights = dot_nt(values, grad * mask)
            inner = jnp.sum(weights * d_weights, 0, keepdims=True)
            d_scores.append((weights * (d_weights - inner)).astype(BF))
            low.append(weights.astype(BF))
        d_proj[2, rows, lanes] = dot_nn(
            jnp.concatenate(low, 1), jnp.concatenate([grad * mask for mask in masks], 0)
        ).astype(BF)
        d_proj[1, rows, lanes] = (
            dot_nn(
                jnp.concatenate(d_scores, 1), jnp.concatenate([query * mask for mask in masks], 0)
            )
            * scale
        ).astype(BF)
        turned = dot_tn(
            jnp.concatenate([keys * mask for mask in masks], 0), jnp.concatenate(d_scores, 0)
        )
        d_proj[0, rows, lanes] = (turned.T * scale).astype(BF)


def norm_forward(value, gain, bias):
    center = value - jnp.mean(value, -1, keepdims=True)
    scale = lax.rsqrt(jnp.mean(center * center, -1, keepdims=True) + EPS)
    unit = center * scale
    return unit, scale, unit * gain + bias


def norm_backward(grad, unit, scale, gain, sums, which):
    fold = lambda v: jnp.sum(v.reshape(v.shape[0] // 8, 8, v.shape[1]), 0)
    sums[which] += fold(grad * unit)
    sums[which + 1] += fold(grad)
    d_unit = grad * gain
    first = jnp.mean(d_unit, -1, keepdims=True)
    second = jnp.mean(d_unit * unit, -1, keepdims=True)
    return scale * (d_unit - first - unit * second)


class GradientShare:
    AHEAD = 8
    WINDOW = 6
    DEPTH = 4
    FINAL = 8
    PIECES = 2
    EARLY = 4

    def __init__(self, size, section, dp, core, decoder, a_fac, b_fac, tiles, w_up, w_down, held, slope, resid, acc, *share):
        self.acc = acc
        (self.norm_tile, self.tile_sem, self.pair_got, self.nb, self.late_sent, self.late_got, self.late_acc, self.pair_send,
         self.pair_recv, self.line_send, self.line_recv, self.cross_send, self.cross_recv, self.norm_send,
         self.norm_recv, self.late_send, self.late_recv, self.factor_send, self.factor_recv, self.final_sem,
         self.pair_credit, self.left_credit, self.right_credit, self.cross_credit) = share
        self.line = size // 2
        self.section, self.dp, self.core = section, dp, core
        self.decoder, self.encoder = decoder, jnp.logical_not(decoder)
        self.z, self.y = dp // 2, lax.rem(dp, 2)
        self.a_fac, self.b_fac, self.tiles = a_fac, b_fac, tiles
        self.w_up, self.w_down, self.held, self.slope, self.resid = w_up, w_down, held, slope, resid
        self.rows = a_fac.shape[2] // size
        self.own_chunks = b_fac.shape[0] - 4
        self.positions = self.own_chunks + 2 + jnp.where(decoder, 2, 0)
        self.pairs = self.positions - self.EARLY
        self.partner = (section, dp + 1 - 2 * self.y, core)
        self.right = (section, dp + 2, core)
        self.left = (section, dp - 2, core)
        self.across = (1 - section, dp, core)
        self.mate = (section, dp, 1 - core)
        self.has_left, self.has_right = self.z > 0, self.z < self.line - 1

    def greet(self, barrier):
        pl.semaphore_signal(barrier, inc=1, device_id=self.partner, device_id_type=MESH)

        @pl.when(self.has_left)
        def _():
            pl.semaphore_signal(barrier, inc=1, device_id=self.left, device_id_type=MESH)

        @pl.when(self.has_right)
        def _():
            pl.semaphore_signal(barrier, inc=1, device_id=self.right, device_id_type=MESH)

        return 1 + jnp.where(self.has_left, 1, 0) + jnp.where(self.has_right, 1, 0)

    def remote(self, src, dst, send, recv, device):
        return pltpu.make_async_remote_copy(
            src_ref=src, dst_ref=dst, send_sem=send, recv_sem=recv, device_id=device, device_id_type=MESH
        )

    def tile_rows(self, k):
        return pl.ds(pl.multiple_of(k * self.rows, self.rows), self.rows)

    def cols(self, k):
        return pl.ds(pl.multiple_of(k * CHUNK, CHUNK), CHUNK)

    def pair_slot(self, j, k):
        return self.w_down.at[self.tile_rows(lax.rem(j, self.AHEAD)), self.cols(k)]

    def pair_copy(self, j, k):
        slot = lax.rem(j, self.AHEAD) * self.line + k
        return self.remote(
            self.pair_slot(j, k), self.pair_got.at[slot], self.pair_send.at[slot], self.pair_recv.at[slot], self.partner
        )

    def line_slot(self, p, k):
        slot = lax.rem(p, self.DEPTH) * self.line + k
        return self.held.at[slot // 8, self.tile_rows(lax.rem(slot, 4)), self.cols(lax.rem(slot // 4, 2))]

    def line_place(self, side, p, k, z):
        return lax.rem(p, self.WINDOW) * (self.line + 1) + (self.line - z + k if side else k - z)

    def line_got(self, place):
        return self.w_up.at[self.tile_rows(place // 4), self.cols(lax.rem(place, 4))]

    def piece(self, h):
        return pl.ds(h * (self.rows // self.PIECES), self.rows // self.PIECES)

    def line_copy(self, side, p, k, receiver, h):
        place = self.line_place(side, p, k, receiver)
        return self.remote(
            self.line_slot(p, k).at[self.piece(h)],
            self.line_got(place).at[self.piece(h)],
            self.line_send.at[lax.rem(p, self.DEPTH) * self.line + k, h],
            self.line_recv.at[place, h],
            self.left if side else self.right,
        )

    def cross_copy(self, q):
        return self.remote(
            self.slope.at[q], self.slope.at[q], self.cross_send.at[q], self.cross_recv.at[q], self.across
        )

    def late_copy(self, e):
        return self.remote(
            self.late_sent.at[e], self.late_got.at[e], self.late_send.at[e], self.late_recv.at[e], self.partner
        )

    def act_copy(self, n, m):
        rows = pl.ds(pl.multiple_of(m * SLOT, SLOT), SLOT)
        return self.remote(
            self.b_fac.at[n, rows],
            self.a_fac.at[5 + n // 2, rows, pl.ds(n % 2 * CHUNK, CHUNK)],
            self.factor_send.at[n * 2 + m],
            self.factor_recv.at[n * 2 + m],
            self.partner,
        )

    def branch_copy(self, k):
        rows = pl.ds(pl.multiple_of(self.core * SLOT, SLOT), SLOT)
        return self.remote(
            self.a_fac.at[0, rows, self.tile_rows(k * 2 + 1 - self.y)],
            self.a_fac.at[4, rows, pl.ds(k * self.rows, self.rows)],
            self.factor_send.at[8 + k],
            self.factor_recv.at[8 + k],
            self.partner,
        )

    def branch_forward(self):
        rows = pl.ds(pl.multiple_of(self.core * SLOT, SLOT), SLOT)
        part = self.a_fac.at[4, rows, pl.ds(0, CHUNK)]
        return self.remote(part, part, self.factor_send.at[12], self.factor_recv.at[12], self.mate)

    def send_act(self, m):
        @pl.when(self.encoder)
        def _():
            for n in range(4):
                self.act_copy(n, m).start()

    def send_branch(self, m):
        @pl.when(self.encoder & (self.core == m))
        def _():
            for k in range(4):
                self.branch_copy(k).start()

    def pass_factors(self):
        for k in range(4):
            self.branch_copy(k).wait_recv()
        self.branch_forward().start()

    def take_factors(self):
        for m in range(2):
            for n in range(4):
                self.act_copy(n, m).wait()
        for k in range(4):
            self.branch_copy(k).wait_send()
        self.branch_forward().wait()

    def left_of(self, i):
        return jnp.minimum(i // 4, 2) + jnp.where(i > 8, 1, 0)

    def cross_tile(self, i, k, y):
        first = (i - self.own_chunks) * 2
        small = self.rows // 2
        base = self.a_fac.shape[2] // 2

        def product(e):
            q = first + e
            block = dot_tn(
                self.a_fac[4 + (q + 1) // 2, :, pl.ds(pl.multiple_of(base + k * self.rows, self.rows), self.rows)],
                self.b_fac[self.own_chunks + q],
            )
            return jnp.where(y == 0, block[:small], block[small:])

        def given(e):
            place = pl.ds(pl.multiple_of(k * self.rows + y * small, small), small)
            return self.slope[first + e, place].astype(F32)

        return product, given

    def cross_into(self, ref, i, k, y):
        product, given = self.cross_tile(i, k, y)
        small = self.rows // 2

        @pl.when(self.decoder)
        def _():
            for e in range(2):
                ref[e * small : (e + 1) * small] = product(e).astype(ref.dtype)

        @pl.when(self.encoder)
        def _():
            for e in range(2):
                ref[e * small : (e + 1) * small] = given(e).astype(ref.dtype)

    def pair_step(self, j):
        i = j + jnp.where(self.decoder, 2, 4)

        @pl.when(j >= self.AHEAD)
        def _():
            pl.semaphore_wait(self.pair_credit, 1)
            for k in range(self.line):
                self.pair_copy(j, k).wait_send()

        @pl.when(i < self.own_chunks)
        def _():
            left = self.left_of(i)
            factor = jnp.concatenate(
                [self.a_fac[left, :, self.tile_rows(k * 2 + 1 - self.y)] for k in range(self.line)], 1
            )
            block = dot_tn(factor, self.b_fac[i]).astype(BF)
            for k in range(self.line):
                slot = self.pair_slot(j, k)
                slot[...] = block[k * self.rows : (k + 1) * self.rows]

        @pl.when(i >= self.own_chunks)
        def _():
            @pl.when(self.encoder)
            def _():
                for e in range(2):
                    self.cross_copy((i - self.own_chunks) * 2 + e).wait_recv()

            loop(self.line, lambda k: self.cross_into(self.pair_slot(j, k), i, k, 1 - self.y))

        for k in (0, 3, 1, 2):
            self.pair_copy(j, k).start()

    def begin(self):
        @pl.when(self.has_left)
        def _():
            pl.semaphore_signal(self.right_credit, inc=self.WINDOW, device_id=self.left, device_id_type=MESH)

        @pl.when(self.has_right)
        def _():
            pl.semaphore_signal(self.left_credit, inc=self.WINDOW, device_id=self.right, device_id_type=MESH)

        @pl.when(self.encoder)
        def _():
            pl.semaphore_signal(self.cross_credit, inc=1, device_id=self.across, device_id_type=MESH)

    def between(self):
        loop(2, self.pair_step)
        self.line_step(0)

    def before(self, m):
        opening = self.encoder & (m == 0)

        @pl.when(opening)
        def _():
            self.pass_factors()

        first = jnp.where(self.decoder, 2, 0) + 2 * m
        lax.fori_loop(first, first + 2, lambda j, carry: (self.pair_step(j), carry)[1], 0)

        @pl.when(opening)
        def _():
            self.take_factors()

        self.line_step(jnp.where(self.decoder, 1, 0) + 2 * m)

    def middle(self, m):
        self.line_step(jnp.where(self.decoder, 2, 1) + 2 * m)

    def entry(self, t, e):
        last = self.line - 1
        on = last - self.z
        k = jnp.where(e == last, self.z, jnp.where(e < on, last - e, e - on))
        hops = jnp.where(k > self.z, self.z, last - self.z)
        p = t - jnp.where(e == last, last, hops)
        valid = (p >= 0) & (p < self.positions)
        line_first = (p < self.EARLY) & self.decoder
        i = jnp.where(line_first, p // 2, p - jnp.where(self.decoder, 2, 0))
        y = jnp.where(line_first & (lax.rem(p, 2) == 0), 1 - self.y, self.y)
        return k, p, valid, i, y

    def line_step(self, t):
        last = self.line - 1

        def held_at(p):
            return (p >= 0) & (p < self.positions)

        @pl.when(held_at(t - self.z) & self.has_right)
        def _():
            pl.semaphore_wait(self.right_credit, 1)

        @pl.when(held_at(t - (last - self.z)) & self.has_left)
        def _():
            pl.semaphore_wait(self.left_credit, 1)

        for e in range(self.line):
            k, p, valid, i, y = self.entry(t, e)
            i = jnp.clip(i, 0, self.own_chunks - 1)
            self.acc[e] = dot_tn(self.a_fac[self.left_of(i), :, self.tile_rows(k * 2 + y)], self.b_fac[i])

        @pl.when(self.encoder & (t < self.EARLY + last))
        def _():
            for e in range(self.line):
                k, p, valid, i, y = self.entry(t, e)
                n = jnp.clip(i, 0, self.EARLY - 1)
                part = dot_tn(
                    self.a_fac[4, :, self.tile_rows(k)], self.a_fac[5 + n // 2, :, self.cols(lax.rem(n, 2))]
                )
                self.acc[e] += jnp.where(i < self.EARLY, part, 0.0)

        def one(e):
            k, p, valid, i, y = self.entry(t, e)

            @pl.when(valid)
            def _():
                acc = self.acc.at[e]

                @pl.when(i >= self.own_chunks)
                def _():
                    self.cross_into(acc, i, k, y)

                @pl.when(p >= self.EARLY)
                def _():
                    j = p - self.EARLY
                    self.pair_copy(j, k).wait_recv()
                    acc[...] += self.pair_got[lax.rem(j, self.AHEAD) * self.line + k].astype(F32)

                @pl.when(e < last)
                def _():
                    self.send(p, k, acc)

                @pl.when(e == last)
                def _():
                    self.finish(p, acc)

        loop(self.line, one)

    def arrived(self, side, p, k, h):
        self.line_copy(side, p, k, self.z, h).wait_recv()
        return self.line_got(self.line_place(side, p, k, self.z))[self.piece(h)].astype(F32)

    def send(self, p, k, acc):
        slot = self.line_slot(p, k)

        def to(side, receiver, inner):
            copies = [self.line_copy(side, p, k, receiver, h) for h in range(self.PIECES)]

            @pl.when(p >= self.DEPTH)
            def _():
                for copy in copies:
                    copy.wait_send()

            @pl.when(inner)
            def _():
                for h, copy in enumerate(copies):
                    slot[self.piece(h)] = (acc[self.piece(h)] + self.arrived(side, p, k, h)).astype(BF)
                    copy.start()

            @pl.when(jnp.logical_not(inner))
            def _():
                slot[...] = acc[...].astype(BF)
                for copy in copies:
                    copy.start()

        @pl.when(k > self.z)
        def _():
            to(0, self.z + 1, self.has_left)

        @pl.when(k < self.z)
        def _():
            to(1, self.z - 1, self.has_right)

    def finish(self, p, acc):
        @pl.when(self.has_left)
        def _():
            for h in range(self.PIECES):
                acc[self.piece(h)] += self.arrived(0, p, self.z, h)

        @pl.when(self.has_right)
        def _():
            for h in range(self.PIECES):
                acc[self.piece(h)] += self.arrived(1, p, self.z, h)

        line_first = (p < self.EARLY) & self.decoder

        @pl.when(line_first & (lax.rem(p, 2) == 0))
        def _():
            self.late_sent[p // 2] = acc[...].astype(BF)
            self.late_copy(p // 2).start()

        @pl.when(line_first & (lax.rem(p, 2) == 1))
        def _():
            self.late_acc[p // 2] = acc[...]

        @pl.when(jnp.logical_not(line_first))
        def _():
            i = p - jnp.where(self.decoder, 2, 0)

            @pl.when(i >= self.FINAL + jnp.where(self.decoder, 2, 0))
            def _():
                self.final_copy(i).wait()

            first = self.encoder & (i == 0)

            @pl.when(first)
            def _():
                self.late_acc[0] = acc[...]
                pltpu.make_async_copy(self.late_acc.at[0], self.tiles.at[0], self.final_sem.at[0]).start()

            @pl.when(jnp.logical_not(first))
            def _():
                slot = self.final_slot(i)
                slot[...] = acc[...]
                self.final_copy(i).start()

        @pl.when(p + self.WINDOW < self.positions)
        def _():
            @pl.when(self.has_left)
            def _():
                pl.semaphore_signal(self.right_credit, inc=1, device_id=self.left, device_id_type=MESH)

            @pl.when(self.has_right)
            def _():
                pl.semaphore_signal(self.left_credit, inc=1, device_id=self.right, device_id_type=MESH)

        @pl.when((p >= self.EARLY) & (p - self.EARLY + self.AHEAD < self.pairs))
        def _():
            pl.semaphore_signal(self.pair_credit, inc=1, device_id=self.partner, device_id_type=MESH)
            self.pair_step(p - self.EARLY + self.AHEAD)

    def final_slot(self, i):
        slot = lax.rem(i, self.FINAL)
        return self.resid.at[self.tile_rows(slot // 2), self.cols(lax.rem(slot, 2))]

    def final_copy(self, i):
        return pltpu.make_async_copy(
            self.final_slot(i), self.tiles.at[i], self.final_sem.at[lax.rem(i, self.FINAL)]
        )

    def cross_part(self):
        @pl.when(self.decoder)
        def _():
            pl.semaphore_wait(self.cross_credit, 1)

            def one(q):
                def tile(k):
                    self.slope[q, self.tile_rows(k)] = dot_tn(
                        self.a_fac[4 + (q + 1) // 2, :, self.tile_rows(k)],
                        self.b_fac[self.own_chunks + q],
                    ).astype(BF)

                loop(4, tile)
                self.cross_copy(q).start()

            loop(4, one)

    def norm_copy(self, src, dst, device):
        return self.remote(self.nb.at[src], self.nb.at[dst], self.norm_send.at[dst], self.norm_recv.at[dst], device)

    def start_norms(self, sums):
        nb, has_left, has_right = self.nb, self.has_left, self.has_right
        for i in range(6):
            nb[0, i : i + 1] = jnp.sum(sums[i], 0, keepdims=True)
        nb[0, 6:8] = jnp.zeros_like(nb[0, 6:8])
        nb[3] = nb[0]
        nb[4] = nb[0]
        nb[5] = nb[0]

        @pl.when(jnp.logical_not(has_left))
        def _():
            self.norm_copy(3, 1, self.right).start()

        @pl.when(jnp.logical_not(has_right))
        def _():
            self.norm_copy(4, 2, self.left).start()

    def middle_norms(self):
        nb, has_left, has_right = self.nb, self.has_left, self.has_right
        to_right = self.norm_copy(3, 1, self.right)
        to_left = self.norm_copy(4, 2, self.left)

        @pl.when(has_left)
        def _():
            to_right.wait_recv()
            nb[5] += nb[1]

            @pl.when(has_right)
            def _():
                nb[3] += nb[1]
                to_right.start()

        @pl.when(has_right)
        def _():
            to_left.wait_recv()
            nb[5] += nb[2]

            @pl.when(has_left)
            def _():
                nb[4] += nb[2]
                to_left.start()

        self.norm_copy(5, 6, self.partner).start()

    def hand_norms(self):
        nb = self.nb
        self.norm_copy(5, 6, self.partner).wait()

        @pl.when(self.has_right)
        def _():
            self.norm_copy(3, 1, self.right).wait_send()

        @pl.when(self.has_left)
        def _():
            self.norm_copy(4, 2, self.left).wait_send()

        nb[7] = nb[5] + nb[6]

        @pl.when(self.decoder)
        def _():
            self.norm_copy(7, 8, self.across).start()
            nb[8] = nb[7]

    def finish_norms(self, norm_out, norm3_out):
        nb = self.nb
        hand = self.norm_copy(7, 8, self.across)
        self.norm_tile[0] = nb[7, :, pl.ds(pl.multiple_of(self.dp * 128, 128), 128)]

        @pl.when(self.encoder)
        def _():
            hand.wait_recv()

        place = self.section * self.line * 2 + self.dp
        block = nb[8, :, pl.ds(pl.multiple_of(place // 2 * 128, 128), 128)]
        self.norm_tile[1] = jnp.where(self.y == 0, block, pltpu.roll(block, 64, 1))
        for copy in self.norm_leaves(norm_out, norm3_out):
            copy.start()

        @pl.when(self.decoder)
        def _():
            hand.wait_send()

    def norm_leaves(self, *outs):
        return [
            pltpu.make_async_copy(self.norm_tile.at[e], out, self.tile_sem.at[e]) for e, out in enumerate(outs)
        ]

    def norms_left(self, *outs):
        for copy in self.norm_leaves(*outs):
            copy.wait()

    def run(self, sums, norm_out, norm3_out):
        self.start_norms(sums)
        first = jnp.where(self.decoder, 6, 4)
        lax.fori_loop(first, self.AHEAD, lambda j, carry: (self.pair_step(j), carry)[1], 0)
        self.cross_part()

        def step(t, carry):
            self.line_step(t)

            @pl.when(t == 6)
            def _():
                self.middle_norms()

            @pl.when(t == self.own_chunks + 1)
            def _():
                self.hand_norms()

            return carry

        lax.fori_loop(jnp.where(self.decoder, 5, 4), self.positions + self.line - 1, step, 0)
        self.finish_norms(norm_out, norm3_out)

    def drain(self):
        @pl.when(self.decoder)
        def _():
            for e in range(2):
                self.late_copy(e).wait()
                self.final_copy(e).wait()
                slot = self.final_slot(e)
                slot[...] = self.late_acc[e] + self.late_got[e].astype(F32)
                self.final_copy(e).start()

        for slot in range(self.AHEAD):
            for k in range(self.line):
                self.pair_copy(slot, k).wait_send()

        for slot in range(self.DEPTH):
            for k in range(self.line):

                @pl.when(self.z != k)
                def _():
                    for h in range(self.PIECES):
                        self.line_copy(0, slot, k, 0, h).wait_send()

        for slot in range(self.FINAL):
            self.final_copy(slot).wait()

        @pl.when(self.decoder)
        def _():
            for q in range(4):
                self.cross_copy(q).wait_send()


def layer_kernel(
    sections,
    ring,
    inputs,
    targets,
    cotangent,
    counts_hbm,
    qkv_hbm,
    out_hbm,
    gain1_hbm,
    bias1_hbm,
    up_hbm,
    down_hbm,
    gain2_hbm,
    bias2_hbm,
    cross_hbm,
    cross_out_hbm,
    gain3_hbm,
    bias3_hbm,
    seg_hbm,
    grad_hbm,
    norm_out,
    first_out,
    second_out,
    gain1,
    bias1,
    gain2,
    bias2,
    gain3,
    bias3,
    counts,
    seg_out,
    in_grad,
    w_qkv,
    w_out,
    w_up,
    w_down,
    w_cross,
    w_cross_out,
    a_fac,
    b_fac,
    proj,
    cross_proj,
    unit1,
    held,
    unit3,
    scale1,
    scale2,
    scale3,
    resid,
    slope,
    d_mix,
    sent,
    got,
    half_send,
    half_got,
    spare,
    low_out,
    sums,
    load_sem,
    x_sem,
    ex_send,
    ex_recv,
    hop_send,
    hop_recv,
    out_sem,
    *share,
):
    section = lax.axis_index("section")
    dp = lax.axis_index("dp")
    core = lax.axis_index("mp")
    decoder = section == sections - 1
    encoder = section != sections - 1
    mate = (section, dp, 1 - core)
    across = (1 - section, dp, core)
    half = seg_out.shape[2]
    slot = 2 * half
    limit = jnp.where(decoder, 0, slot)
    width = w_up.shape[1]
    parts = width // CHUNK
    two, three = jnp.where(decoder, 0, 1), jnp.where(decoder, 1, 0)
    own = core * half
    other = (1 - core) * half

    d_branch, crossed, d_attn, layer_in, normed_low, memory, d_cross = (a_fac.at[i] for i in range(7))
    act = b_fac.at[0:parts]
    d_hidden = b_fac.at[parts : 2 * parts]
    mixed = b_fac.at[2 * parts]
    d_proj = b_fac.at[2 * parts + 1 : 2 * parts + 4]
    d_cross_proj = b_fac.at[2 * parts + 4 : 2 * parts + 7]
    cross_mixed = b_fac.at[2 * parts + 7]

    unit2, d_out = held.at[0], held.at[1]

    def rows_of(m):
        return pl.ds(pl.multiple_of(m * slot, slot), slot)

    def half_of(m, offset):
        return pl.ds(pl.multiple_of(m * slot + offset, half), half)

    def strip_of(m, k):
        return pl.ds(pl.multiple_of(m * slot + k * STRIP, STRIP), STRIP)

    def strips(body):
        for k in range(slot // STRIP):
            body(k)

    barrier = pltpu.get_barrier_semaphore()
    for device in (mate, across):
        pl.semaphore_signal(barrier, inc=1, device_id=device, device_id_type=MESH)
    if ring:
        total = GradientShare(
            ring, section, dp, core, decoder, a_fac, b_fac, first_out, w_up, w_down, held, slope, resid, spare, *share
        )
        greeted = 2 + total.greet(barrier)
    else:
        greeted = 2

    loads = [
        pltpu.make_async_copy(src, dst, load_sem.at[i])
        for i, (src, dst) in enumerate(
            (
                (qkv_hbm.at[0], w_qkv),
                (out_hbm.at[0], w_out),
                (up_hbm.at[0], w_up),
                (down_hbm.at[0], w_down),
                (cross_hbm, w_cross),
                (cross_out_hbm, w_cross_out),
                (gain1_hbm, gain1),
                (bias1_hbm, bias1),
                (gain2_hbm, gain2),
                (bias2_hbm, bias2),
                (gain3_hbm, gain3),
                (bias3_hbm, bias3),
                (counts_hbm, counts),
            )
        )
    ]

    def local_rows(src, dst, m, sem):
        return pltpu.make_async_copy(src.at[m], dst.at[half_of(m, own)], sem)

    def mate_rows(src, dst, m, send, recv):
        return pltpu.make_async_remote_copy(
            src_ref=src.at[m],
            dst_ref=dst.at[half_of(m, own)],
            send_sem=send,
            recv_sem=recv,
            device_id=mate,
            device_id_type=MESH,
        )

    def start_rows(src, dst, base):
        for m in range(2):
            local_rows(src, dst, m, x_sem.at[base + m]).start()
        for m in range(2):
            mate_rows(src, dst, m, x_sem.at[base + 2 + m], x_sem.at[base + 4 + m]).start()

    def wait_local(src, dst, base, m):
        local_rows(src, dst, m, x_sem.at[base + m]).wait()

    def wait_mate(src, dst, base, m):
        mate_rows(src, dst, m, x_sem.at[base + 2 + m], x_sem.at[base + 4 + m]).wait()

    def wait_rows(src, dst, base, m):
        wait_local(src, dst, base, m)
        wait_mate(src, dst, base, m)

    @pl.when(encoder)
    def _():
        for m in range(2):
            local_rows(inputs, layer_in, m, x_sem.at[m]).start()

    @pl.when(decoder)
    def _():
        for m in range(2):
            local_rows(targets, layer_in, m, x_sem.at[m]).start()

    loads[0].start()
    loads[1].start()
    pl.semaphore_wait(barrier, greeted)

    def mate_start(src, dst, base):
        for m in range(2):
            mate_rows(src, dst, m, x_sem.at[base + 2 + m], x_sem.at[base + 4 + m]).start()

    @pl.when(encoder)
    def _():
        mate_start(inputs, layer_in, 0)

    @pl.when(decoder)
    def _():
        mate_start(targets, layer_in, 0)

    for copy in loads[2:]:
        copy.start()

    @pl.when(decoder)
    def _():
        start_rows(cotangent, d_out, 6)

    sums[...] = jnp.zeros_like(sums)

    def exchange(which, buffer, m):
        return pltpu.make_async_remote_copy(
            src_ref=sent.at[rows_of(m)],
            dst_ref=got.at[buffer, rows_of(m)],
            send_sem=ex_send.at[which, m],
            recv_sem=ex_recv.at[which, m],
            device_id=mate,
            device_id_type=MESH,
        )

    def half_exchange(which, m):
        return pltpu.make_async_remote_copy(
            src_ref=half_send.at[which, m],
            dst_ref=half_got.at[which, m],
            send_sem=hop_send.at[4 + which, m],
            recv_sem=hop_recv.at[4 + which, m],
            device_id=mate,
            device_id_type=MESH,
        )

    def across_copy(src, dst, which, m):
        return pltpu.make_async_remote_copy(
            src_ref=src,
            dst_ref=dst.at[half_of(m, own)],
            send_sem=hop_send.at[which, m],
            recv_sem=hop_recv.at[which, m],
            device_id=across,
            device_id_type=MESH,
        )

    def forward_copy(ref, which, m):
        return pltpu.make_async_remote_copy(
            src_ref=ref.at[half_of(m, own)],
            dst_ref=ref.at[half_of(m, own)],
            send_sem=hop_send.at[which, m],
            recv_sem=hop_recv.at[which, m],
            device_id=mate,
            device_id_type=MESH,
        )

    def project_out(value, weight, m):
        for n in range(sent.shape[1] // CHUNK):
            cols = slice(n * CHUNK, (n + 1) * CHUNK)
            sent[rows_of(m), cols] = dot_nt(value, weight[cols, :]).astype(BF)

    def summed(buffer, strip):
        return sent[strip].astype(F32) + got[buffer, strip].astype(F32)

    loads[0].wait()

    def project(m, offset):
        piece = half_of(m, offset)
        for t in range(3):
            proj[t, piece] = dot_nn(layer_in[piece], w_qkv[t]).astype(BF)

    def own_rows(m):
        @pl.when(encoder)
        def _():
            wait_local(inputs, layer_in, 0, m)

        @pl.when(decoder)
        def _():
            wait_local(targets, layer_in, 0, m)

        project(m, own)

    loop(2, own_rows)

    def attention_in(m):
        @pl.when(encoder)
        def _():
            wait_mate(inputs, layer_in, 0, m)

        @pl.when(decoder)
        def _():
            wait_mate(targets, layer_in, 0, m)

        rows = rows_of(m)
        project(m, other)
        attend_forward(proj, mixed, rows, limit)
        project_out(mixed[rows], w_out, m)
        exchange(0, 0, m).start()

    loads[1].wait()
    loop(2, attention_in)
    for copy in loads[2:]:
        copy.wait()

    def after_attention(m):
        exchange(0, 0, m).wait()

        def norm(k):
            strip = strip_of(m, k)
            unit, scale, value = norm_forward(
                layer_in[strip].astype(F32) + summed(0, strip), gain1[...], bias1[...]
            )
            unit1[strip] = unit.astype(BF)
            scale1[strip] = scale
            resid[strip] = value
            low_out[pl.ds(k * STRIP, STRIP)] = value.astype(BF)
            crossed[strip] = value.astype(BF)

        strips(norm)

        @pl.when(decoder)
        def _():
            rows = rows_of(m)
            normed_low[rows] = low_out[...]
            cross_proj[0, rows] = dot_nn(low_out[...], w_cross[0]).astype(BF)
            across_copy(seg_out.at[0, m], memory, 0, m).wait_recv()
            forward_copy(memory, 1, m).start()
            forward_copy(memory, 1, m).wait()
            for t in range(1, 3):
                cross_proj[t, rows] = dot_nn(memory[rows], w_cross[t]).astype(BF)
            attend_forward(cross_proj, cross_mixed, rows, None)
            project_out(cross_mixed[rows], w_cross_out, m)
            exchange(1, 1, m).start()


    def feed_forward(m):
        rows = rows_of(m)

        @pl.when(decoder)
        def _():
            exchange(1, 1, m).wait()

            def norm(k):
                strip = strip_of(m, k)
                unit, scale, value = norm_forward(
                    resid[strip] + summed(1, strip), gain3[...], bias3[...]
                )
                unit3[strip] = unit.astype(BF)
                scale3[strip] = scale
                resid[strip] = value
                crossed[strip] = value.astype(BF)

            strips(norm)

        for n in range(parts):
            pre = dot_nn(crossed[rows], w_up[:, n * CHUNK : (n + 1) * CHUNK])
            rise = 0.5 + 0.5 * lax.erf(pre * (0.5**0.5))
            act[n, rows] = (pre * rise).astype(BF)
            slope[n, rows] = (rise + pre * jnp.exp(-0.5 * pre * pre) * 0.3989422804014327).astype(BF)
        if ring:
            total.send_act(m)
        project_out(jnp.concatenate([act[n, rows] for n in range(parts)], 1), w_down, m)
        exchange(2, two, m).start()


    def finish_forward(m):
        exchange(2, two, m).wait()

        def norm(k):
            strip = strip_of(m, k)
            unit, scale, value = norm_forward(
                resid[strip] + summed(two, strip), gain2[...], bias2[...]
            )
            unit2[strip] = unit.astype(BF)
            scale2[strip] = scale
            low_out[pl.ds(k * STRIP, STRIP)] = value.astype(BF)

        strips(norm)
        seg_out[0, m] = low_out[pl.ds(pl.multiple_of(own, half), half)]

        @pl.when(encoder)
        def _():
            across_copy(seg_out.at[0, m], memory, 0, m).start()

    def forward_parts(m):
        after_attention(m)

        @pl.when(m == 1)
        def _():
            finish_forward(0)

        feed_forward(m)

    question = dp // QSLOTS
    spot = dp - question * QSLOTS

    def feed_backward(m):
        rows = rows_of(m)

        @pl.when(encoder)
        def _():
            across_copy(half_send.at[0, m], d_out, 2, m).wait_recv()
            forward_copy(d_out, 3, m).start()
            forward_copy(d_out, 3, m).wait()

        @pl.when(decoder)
        def _():
            wait_rows(cotangent, d_out, 6, m)

        keep = jnp.where(spot < counts[m, question], 1.0, 0.0)
        keep = jnp.where(decoder, keep, 1.0)

        def norm(k):
            strip = strip_of(m, k)
            grad = norm_backward(
                d_out[strip].astype(F32) * keep,
                unit2[strip].astype(F32),
                scale2[strip],
                gain2[...],
                sums,
                2,
            )
            resid[strip] = grad
            d_branch[strip] = grad.astype(BF)

        strips(norm)
        if ring:
            total.send_branch(m)
        for n in range(parts):
            grad = dot_nn(d_branch[rows], w_down[:, n * CHUNK : (n + 1) * CHUNK])
            d_hidden[n, rows] = (grad * slope[n, rows].astype(F32)).astype(BF)
        project_out(jnp.concatenate([d_hidden[n, rows] for n in range(parts)], 1), w_up, m)
        exchange(3, three, m).start()

    loop(2, forward_parts)

    @pl.when(decoder)
    def _():
        feed_backward(0)

    finish_forward(1)
    seg_leaves = pltpu.make_async_copy(seg_out, seg_hbm, out_sem.at[2])
    seg_leaves.start()
    lax.fori_loop(jnp.where(decoder, 1, 0), 2, lambda m, carry: (feed_backward(m), carry)[1], 0)
    if ring:
        total.begin()

    def cross_backward(m):
        rows = rows_of(m)

        def norm(k):
            strip = strip_of(m, k)
            grad = norm_backward(
                resid[strip] + summed(three, strip),
                unit3[strip].astype(F32),
                scale3[strip],
                gain3[...],
                sums,
                4,
            )
            resid[strip] = grad
            d_cross[strip] = grad.astype(BF)

        strips(norm)
        d_mix[rows] = dot_nn(d_cross[rows], w_cross_out[...]).astype(BF)

        @pl.when(m == 1)
        def _():
            memory_leaves(0)

        attend_backward(cross_proj, d_mix, d_cross_proj, rows, None)

        def memory_part(offset):
            piece = half_of(m, offset)
            return jnp.concatenate([d_cross_proj[1, piece], d_cross_proj[2, piece]], 1)

        def memory_weight(n):
            cols = slice(n * CHUNK, (n + 1) * CHUNK)
            return jnp.concatenate([w_cross[1, cols], w_cross[2, cols]], 1)

        for n in range(sent.shape[1] // CHUNK):
            cols = slice(n * CHUNK, (n + 1) * CHUNK)
            half_send[0, m, :, cols] = dot_nt(memory_part(other), memory_weight(n)).astype(BF)
        half_exchange(0, m).start()
        for n in range(sent.shape[1] // CHUNK):
            cols = slice(n * CHUNK, (n + 1) * CHUNK)
            spare[2 * m + n] = dot_nt(memory_part(own), memory_weight(n))
        project_out(d_cross_proj[0, rows], w_cross[0], m)
        exchange(4, 0, m).start()
        @pl.when(m == 1)
        def _():
            memory_leaves(1)

    def memory_leaves(m):
        half_exchange(0, m).wait()
        for n in range(sent.shape[1] // CHUNK):
            cols = slice(n * CHUNK, (n + 1) * CHUNK)
            half_send[0, m, :, cols] = (
                spare[2 * m + n] + half_got[0, m, :, cols].astype(F32)
            ).astype(BF)
        across_copy(half_send.at[0, m], d_out, 2, m).start()

    def attention_back(m):
        rows = rows_of(m)

        def norm_rows(buffer):
            def norm(k):
                strip = strip_of(m, k)
                grad = norm_backward(
                    resid[strip] + summed(buffer, strip),
                    unit1[strip].astype(F32),
                    scale1[strip],
                    gain1[...],
                    sums,
                    0,
                )
                resid[strip] = grad
                d_attn[strip] = grad.astype(BF)

            strips(norm)

        @pl.when(decoder)
        def _():
            exchange(4, 0, m).wait()

        @pl.when(encoder)
        def _():
            exchange(3, three, m).wait()

        norm_rows(0)
        d_mix[rows] = dot_nn(d_attn[rows], w_out[...]).astype(BF)
        attend_backward(proj, d_mix, d_proj, rows, limit)

        if ring:
            total.middle(m)

        def input_part(offset):
            piece = half_of(m, offset)
            return jnp.concatenate([d_proj[t, piece] for t in range(3)], 1)

        def input_weight(n):
            cols = slice(n * CHUNK, (n + 1) * CHUNK)
            return jnp.concatenate([w_qkv[t, cols] for t in range(3)], 1)

        for n in range(sent.shape[1] // CHUNK):
            cols = slice(n * CHUNK, (n + 1) * CHUNK)
            half_send[1, m, :, cols] = dot_nt(input_part(other), input_weight(n)).astype(BF)
        half_exchange(1, m).start()
        for n in range(sent.shape[1] // CHUNK):
            cols = slice(n * CHUNK, (n + 1) * CHUNK)
            resid[half_of(m, own), cols] += dot_nt(input_part(own), input_weight(n))

    @pl.when(decoder)
    def _():
        if ring:
            total.between()

        def both(m):
            exchange(3, three, m).wait()
            cross_backward(m)

        loop(2, both)

    def last_part(m):
        if ring:
            total.before(m)
        attention_back(m)

    loop(2, last_part)

    def finish_backward(m):
        half_exchange(1, m).wait()
        in_grad[0, m] = (
            resid[half_of(m, own)] + half_got[1, m].astype(F32)
        ).astype(BF)

    loop(2, finish_backward)
    grad_leaves = pltpu.make_async_copy(in_grad, grad_hbm, out_sem.at[3])
    grad_leaves.start()

    @pl.when(encoder)
    def _():
        for m in range(2):
            across_copy(seg_out.at[0, m], memory, 0, m).wait_send()

    @pl.when(decoder)
    def _():
        for m in range(2):
            across_copy(half_send.at[0, m], d_out, 2, m).wait_send()

    if ring:
        total.run(sums, norm_out, second_out)
        total.drain()
        total.norms_left(norm_out, second_out)
        seg_leaves.wait()
        grad_leaves.wait()
        return

    for i in range(6):
        norm_out[i : i + 1] = jnp.sum(sums[i], 0, keepdims=True)
    norm_out[6:8] = jnp.zeros_like(norm_out[6:8])
    seg_leaves.wait()
    grad_leaves.wait()
    copies = [
        pltpu.make_async_copy(a_fac, first_out, out_sem.at[0]),
        pltpu.make_async_copy(b_fac, second_out, out_sem.at[1]),
    ]
    for copy in copies:
        copy.start()
    for copy in copies:
        copy.wait()


def unpack_kernel(parts, seg, grads, norms, tiles, norm3, *outs):
    (seg_out, in_grad, qkv, proj_out, gain1, bias1, up, down, gain2, bias2, cross, cross_out, gain3, bias3,
     rows16, rows32, small_in, *rest) = outs
    small_out, (come, go) = rest[:6], rest[6:]
    rows = tiles.shape[1]
    small = rows // 2
    moves = [(seg.at[0], rows16.at[0], seg_out.at[0]), (grads.at[0], rows16.at[1], in_grad.at[0])]
    whole = [down.at[0, :, n * CHUNK : (n + 1) * CHUNK] for n in range(parts)]
    whole += [up.at[0, :, n * CHUNK : (n + 1) * CHUNK] for n in range(parts)]
    whole += [proj_out.at[0]] + [qkv.at[0, t] for t in range(3)]
    for n, target in enumerate(whole):
        moves.append((tiles.at[n], rows32.at[n], target))
    for q in range(4):
        n, half = 2 * parts + 4 + q // 2, pl.ds(q % 2 * small, small)
        moves.append((tiles.at[n, half], rows32.at[n, half], cross.at[q] if q < 3 else cross_out))
    tiny = [pltpu.make_async_copy(src, small_in.at[i], come.at[len(moves) + i]) for i, src in enumerate((norms, norm3))]
    first = [pltpu.make_async_copy(src, mid, come.at[i]) for i, (src, mid, dst) in enumerate(moves)]
    second = [pltpu.make_async_copy(mid, dst, go.at[i]) for i, (src, mid, dst) in enumerate(moves)]
    for copy in tiny + first:
        copy.start()
    for copy in tiny:
        copy.wait()
    values = [small_in[0, i : i + 1] for i in range(4)] + [small_in[1, i : i + 1, :small] for i in (4, 5)]
    for i, (value, ref, dst) in enumerate(zip(values, small_out, (gain1, bias1, gain2, bias2, gain3, bias3))):
        ref[...] = value
        second.append(pltpu.make_async_copy(ref, dst, go.at[len(moves) + i]))
        second[-1].start()
    for a, b in zip(first, second):
        a.wait()
        b.start()
    for copy in second:
        copy.wait()


def body(
    sections,
    ring,
    inputs,
    target_inputs,
    cotangent,
    slot_counts,
    w_qkv,
    w_out,
    norm1_gain,
    norm1_bias,
    w_up,
    w_down,
    norm2_gain,
    norm2_bias,
    cross_qkv,
    cross_out,
    norm3_gain,
    norm3_bias,
):
    micro, half, depth = inputs.shape
    rows = micro * 2 * half
    heads = w_out.shape[2]
    width = w_up.shape[2]
    parts = width // CHUNK
    chunks = 2 * parts + 8
    hbm = pl.BlockSpec(memory_space=pl.ANY)
    vmem = pl.BlockSpec(memory_space=VM)
    shape = jax.ShapeDtypeStruct
    if ring:
        results = (
            shape((8, depth // ring), F32),
            shape((chunks - 2, depth // ring, CHUNK), F32),
            shape((8, depth // ring), F32),
        )
        places = (hbm, hbm, hbm)
    else:
        results = (
            shape((8, depth), F32),
            shape((7, rows, depth), BF),
            shape((chunks, rows, CHUNK), BF),
        )
        places = (vmem, hbm, hbm)
    dma = pltpu.SemaphoreType.DMA
    regular = pltpu.SemaphoreType.REGULAR
    tile = (depth // ring, CHUNK) if ring else None
    share = (
        [
            VM((2, 8, depth // ring), F32),
            dma((2,)),
            VM((GradientShare.AHEAD * 4,) + tile, BF),
            VM((9, 8, depth), F32),
            VM((2,) + tile, BF),
            VM((2,) + tile, BF),
            VM((2,) + tile, F32),
            dma((GradientShare.AHEAD * 4,)),
            dma((GradientShare.AHEAD * 4,)),
            dma((GradientShare.DEPTH * 4, GradientShare.PIECES)),
            dma((GradientShare.WINDOW * 5, GradientShare.PIECES)),
            dma((4,)),
            dma((4,)),
            dma((9,)),
            dma((9,)),
            dma((2,)),
            dma((2,)),
            dma((13,)),
            dma((13,)),
            dma((GradientShare.FINAL,)),
            regular,
            regular,
            regular,
            regular,
        ]
        if ring
        else []
    )
    seg_out, in_grad, norms, first, second = pl.pallas_call(
        functools.partial(layer_kernel, sections, ring),
        out_shape=(
            shape((1, micro, half, depth), BF),
            shape((1, micro, half, depth), BF),
        )
        + results,
        in_specs=[hbm] * 16,
        out_specs=(hbm, hbm) + places,
        scratch_shapes=[VM((1, depth), F32)] * 6
        + [
            pltpu.SMEM(slot_counts.shape, jnp.int32),
            VM((1, micro, half, depth), BF),
            VM((1, micro, half, depth), BF),
            VM((3, depth, heads), BF),
            VM((depth, heads), BF),
            VM((depth, width), BF),
            VM((depth, width), BF),
            VM((3, depth, heads), BF),
            VM((depth, heads), BF),
            VM((7, rows, depth), BF),
            VM((chunks, rows, CHUNK), BF),
            VM((3, rows, heads), BF),
            VM((3, rows, heads), BF),
            VM((rows, depth), BF),
            VM((2, rows, depth), BF),
            VM((rows, depth), BF),
            VM((rows, 1), F32),
            VM((rows, 1), F32),
            VM((rows, 1), F32),
            VM((rows, depth), F32),
            VM((parts, rows, CHUNK), BF),
            VM((rows, heads), BF),
            VM((rows, depth), BF),
            VM((2, rows, depth), BF),
            VM((2, micro, half, depth), BF),
            VM((2, micro, half, depth), BF),
            VM((4, half, CHUNK), F32),
            VM((2 * half, depth), BF),
            VM((6, 8, depth), F32),
            pltpu.SemaphoreType.DMA((13,)),
            pltpu.SemaphoreType.DMA((12,)),
            pltpu.SemaphoreType.DMA((5, micro)),
            pltpu.SemaphoreType.DMA((5, micro)),
            pltpu.SemaphoreType.DMA((6, micro)),
            pltpu.SemaphoreType.DMA((6, micro)),
            pltpu.SemaphoreType.DMA((4,)),
        ]
        + share,
        compiler_params=pltpu.CompilerParams(
            collective_id=0, has_side_effects=True, vmem_limit_bytes=60 * 2**20
        ),
        name="layers",
    )(
        inputs,
        target_inputs,
        cotangent,
        slot_counts,
        w_qkv,
        w_out,
        norm1_gain,
        norm1_bias,
        w_up,
        w_down,
        norm2_gain,
        norm2_bias,
        cross_qkv,
        cross_out,
        norm3_gain[None],
        norm3_bias[None],
    )
    if ring:
        lanes = depth // ring
        row = shape((1, lanes), F32)
        small = shape((1, lanes // 2), F32)
        outs = pl.pallas_call(
            functools.partial(unpack_kernel, parts),
            out_shape=(
                shape(seg_out.shape, BF),
                shape(in_grad.shape, BF),
                shape((1, 3, lanes, heads), F32),
                shape((1, lanes, heads), F32),
                row,
                row,
                shape((1, lanes, width), F32),
                shape((1, lanes, width), F32),
                row,
                row,
                shape((3, lanes // 2, heads), F32),
                shape((lanes // 2, heads), F32),
                small,
                small,
            ),
            in_specs=[hbm] * 5,
            out_specs=(hbm,) * 14,
            scratch_shapes=[
                VM((2, micro, half, depth), BF),
                VM((chunks - 2, lanes, CHUNK), F32),
                VM((2, 8, lanes), F32),
                VM((1, lanes), F32),
                VM((1, lanes), F32),
                VM((1, lanes), F32),
                VM((1, lanes), F32),
                VM((1, lanes // 2), F32),
                VM((1, lanes // 2), F32),
                dma((2 * parts + 12,)),
                dma((2 * parts + 16,)),
            ],
            name="unpack",
        )(seg_out, in_grad, norms, first, second)
        return outs[:12] + (outs[12][0], outs[13][0])
    a_fac, b_fac = first, second
    decoder = lax.axis_index("section") == sections - 1

    def weight_grad(left, first, count):
        return jnp.einsum(
            "nd,tnc->tdc", a_fac[left], b_fac[first : first + count], preferred_element_type=F32
        ).astype(BF)

    def shared(grad, axes, dim):
        return lax.psum_scatter(grad, axes, scatter_dimension=dim, tiled=True)

    def wide(grad):
        return jnp.swapaxes(grad, 0, 1).reshape(depth, -1)

    grad_down = shared(wide(weight_grad(0, 0, parts)), "dp", 0)
    grad_up = shared(wide(weight_grad(1, parts, parts)), "dp", 0)
    grad_out = shared(weight_grad(2, 2 * parts, 1)[0], "dp", 0)
    grad_qkv = shared(weight_grad(3, 2 * parts + 1, 3), "dp", 1)
    cross = jnp.concatenate(
        [
            weight_grad(4, 2 * parts + 4, 1),
            weight_grad(5, 2 * parts + 5, 2),
            weight_grad(6, 2 * parts + 7, 1),
        ],
        0,
    )
    cross = shared(jnp.where(decoder, cross, jnp.zeros_like(cross)), ("section", "dp"), 1)
    small = shared(norms[:4], "dp", 1)
    norm3 = jnp.where(decoder, norms[4:6], jnp.zeros_like(norms[4:6]))
    norm3 = shared(norm3, ("section", "dp"), 1)
    return (
        seg_out,
        in_grad,
        grad_qkv[None].astype(F32),
        grad_out[None].astype(F32),
        small[0:1],
        small[1:2],
        grad_up[None].astype(F32),
        grad_down[None].astype(F32),
        small[2:3],
        small[3:4],
        cross[:3].astype(F32),
        cross[3].astype(F32),
        norm3[0],
        norm3[1],
    )


def solution(mesh):
    ring = 8 if mesh.shape["dp"] == 8 else 0
    return jax.shard_map(
        functools.partial(body, mesh.shape["section"], ring),
        mesh=mesh,
        in_specs=(
            P(None, ("dp", "mp"), None),
            P(None, ("dp", "mp"), None),
            P(None, ("dp", "mp"), None),
            P(),
            P("section", None, None, "mp"),
            P("section", None, "mp"),
            P("section", None),
            P("section", None),
            P("section", None, "mp"),
            P("section", None, "mp"),
            P("section", None),
            P("section", None),
            P(None, None, "mp"),
            P(None, "mp"),
            P(),
            P(),
        ),
        out_specs=(
            P("section", None, ("dp", "mp"), None),
            P("section", None, ("dp", "mp"), None),
            P("section", None, "dp", "mp"),
            P("section", "dp", "mp"),
            P("section", "dp"),
            P("section", "dp"),
            P("section", "dp", "mp"),
            P("section", "dp", "mp"),
            P("section", "dp"),
            P("section", "dp"),
            P(None, ("section", "dp"), "mp"),
            P(("section", "dp"), "mp"),
            P(("section", "dp")),
            P(("section", "dp")),
        ),
        check_vma=False,
    )
```
